32 devices in a mesh: dp: 8 (over z, core), fsdp: 4 (over y, x).
Axes of the slice: x: 2, y: 2, z: 4, core: 2. Of those that a mesh axis runs over, the one named last changes fastest.
Arguments:
- tokens: bfloat16 [8192, 1024], P(('dp', 'fsdp')), may hold values from -6 to 6
- memory: bfloat16 [4096, 1024], P(('dp', 'fsdp')), may hold values from -6 to 6
- target_segments: int32 [32, 256], P(('dp', 'fsdp')), may hold values from 0 to 3, never falling along the last dimension, each value on 1 to 192 neighbouring positions
- source_segments: int32 [32, 128], P(('dp', 'fsdp')), may hold values from 0 to 3, never falling along the last dimension, each value on 1 to 96 neighbouring positions
- self_query: bfloat16 [1024, 1024], P(('dp', 'fsdp')), may hold values from -0.1875 to 0.1875
- self_key: bfloat16 [1024, 1024], P(('dp', 'fsdp')), may hold values from -0.1875 to 0.1875
- self_value: bfloat16 [1024, 1024], P(('dp', 'fsdp')), may hold values from -0.1875 to 0.1875
- self_output: bfloat16 [1024, 1024], P(('dp', 'fsdp')), may hold values from -2 to 2
- cross_query: bfloat16 [1024, 1024], P(('dp', 'fsdp')), may hold values from -0.1875 to 0.1875
- cross_key: bfloat16 [1024, 1024], P(('dp', 'fsdp')), may hold values from -0.1875 to 0.1875
- cross_value: bfloat16 [1024, 1024], P(('dp', 'fsdp')), may hold values from -0.1875 to 0.1875
- cross_output: bfloat16 [1024, 1024], P(('dp', 'fsdp')), may hold values from -2 to 2
- expand_weight: bfloat16 [1024, 4096], P(('dp', 'fsdp')), may hold values from -0.1875 to 0.1875
- reduce_weight: bfloat16 [4096, 1024], P(('dp', 'fsdp')), may hold values from -0.75 to 0.75
- self_gain: bfloat16 [1024], P(('dp', 'fsdp')), may hold values from 0.099609375 to 1.8984375
- self_shift: bfloat16 [1024], P(('dp', 'fsdp')), may hold values from -3 to 3
- cross_gain: bfloat16 [1024], P(('dp', 'fsdp')), may hold values from 0.099609375 to 1.8984375
- cross_shift: bfloat16 [1024], P(('dp', 'fsdp')), may hold values from -3 to 3
- final_gain: bfloat16 [1024], P(('dp', 'fsdp')), may hold values from 0.099609375 to 1.8984375
- final_shift: bfloat16 [1024], P(('dp', 'fsdp')), may hold values from -3 to 3
- output_grad: bfloat16 [8192, 1024], P(('dp', 'fsdp')), may hold values from -6 to 6
Outputs:
- output: bfloat16 [8192, 1024], P(('dp', 'fsdp'))
- tokens_grad: float32 [8192, 1024], P(('dp', 'fsdp'))
- memory_grad: float32 [4096, 1024], P(('dp', 'fsdp'))
- self_query_grad: float32 [1024, 1024], P(('dp', 'fsdp'))
- self_key_grad: float32 [1024, 1024], P(('dp', 'fsdp'))
- self_value_grad: float32 [1024, 1024], P(('dp', 'fsdp'))
- self_output_grad: float32 [1024, 1024], P(('dp', 'fsdp'))
- cross_query_grad: float32 [1024, 1024], P(('dp', 'fsdp'))
- cross_key_grad: float32 [1024, 1024], P(('dp', 'fsdp'))
- cross_value_grad: float32 [1024, 1024], P(('dp', 'fsdp'))
- cross_output_grad: float32 [1024, 1024], P(('dp', 'fsdp'))
- expand_weight_grad: float32 [1024, 4096], P(('dp', 'fsdp'))
- reduce_weight_grad: float32 [4096, 1024], P(('dp', 'fsdp'))
- self_gain_grad: float32 [1024], P(('dp', 'fsdp'))
- self_shift_grad: float32 [1024], P(('dp', 'fsdp'))
- cross_gain_grad: float32 [1024], P(('dp', 'fsdp'))
- cross_shift_grad: float32 [1024], P(('dp', 'fsdp'))
- final_gain_grad: float32 [1024], P(('dp', 'fsdp'))
- final_shift_grad: float32 [1024], P(('dp', 'fsdp'))
The draws below stay inside these ranges and needn't reach their ends.
Inputs may be any that keep to these rules, and one draw needn't show every extreme that they name: `target_segments`: each row numbers its positions by sentence, 0 to 3 in order and never falling, every sentence with 1 to 192 positions. `source_segments`: each row numbers its positions by sentence, 0 to 3 in order and never falling, every sentence with 1 to 96 positions; source sentence j of a pack belongs to target sentence j of the same pack.
All inputs are finite; a program needn't handle non-finite values.
Results may differ from the reference program's by a relative error of at most 0.02.
The reference program's roundings to bfloat16 on the way count: a program that leaves them out, or rounds other values in their place, can miss the bound.
Values may be sent and summed in bfloat16 or wider, within the bound.
No kernel may reach another device: no remote copies, remote signals or barrier semaphores. Data moves between devices by JAX's collectives and lax.ppermute only.
A program may use at most 320 MiB of HBM per device.

```python
import math
import jax
import jax.numpy as jnp
import numpy as np
from jax import lax

D = 1024
HEADS = 16
HEAD_DIM = 64
FF = 4096
TOK_DEV = 256
MEM_DEV = 128
SENTS = 4
SENT_MOST = 192
SRC_MOST = 96
TOKENS = 8192
SOURCES = 4096
DEVICES = 32


def raised(values, own_key, source, target, blocks, factor):
    def block_of(axis_at):
        return (jnp.arange(values.shape[axis_at]) // (values.shape[axis_at] // blocks)).reshape((-1,) + (1,) * (values.ndim - 1 - axis_at))

    one_side = jax.random.permutation(own_key, blocks)[block_of(target)]
    other_side = (block_of(target) + blocks // 2) % blocks
    return jnp.where((block_of(source) == one_side) | (block_of(source) == other_side), factor * values, values)


def block_levels(rng, shape, cuts, low, top_value):
    factor_of = 1.0
    for position, shards_of in cuts:
        steps = jax.random.uniform(jax.random.fold_in(jax.random.fold_in(rng, 6), position), (shards_of,), jnp.float32, low / len(cuts), top_value / len(cuts))
        factor_of = factor_of * jnp.repeat(jnp.exp(steps), shape[position] // shards_of).reshape((-1,) + (1,) * (len(shape) - 1 - position))
    return factor_of


def split_up(amount, total, limit, lean):
    portions = [(1 << 20) // math.isqrt(standing ** lean) + 1 for standing in range(2, amount + 1)]
    spare, holding = total - limit - (amount - 1), [1] * (amount - 1)
    while spare > 0:
        candidates = [i for i in range(amount - 1) if holding[i] < limit]
        whole, remaining = sum([portions[i] for i in candidates]), spare
        for i in candidates:
            addition = min(limit - holding[i], max(1, remaining * portions[i] // whole), spare)
            holding[i] = holding[i] + addition
            spare = spare - addition
    return np.array([limit] + holding)


def ragged(stream_key, amount, total, limit, lean):
    if amount == 2:
        one = jax.random.randint(stream_key, (), max(1, total - limit), min(limit, total - 1) + 1)
        return jnp.stack([one, total - one])
    sizes = jnp.asarray(split_up(amount, total, limit, lean), jnp.int32)
    twos = (amount - 1) // 2
    donor, sink = sizes[1:1 + 2 * twos:2], sizes[2:2 + 2 * twos:2]
    room = jnp.minimum(donor - 1, limit - sink)
    passed = jax.random.randint(jax.random.fold_in(stream_key, 1), (twos,), 0, 1 << 20) % (room + 1)
    sizes = sizes.at[1:1 + 2 * twos:2].set(donor - passed).at[2:2 + 2 * twos:2].set(sink + passed)
    return sizes[jax.random.permutation(jax.random.fold_in(stream_key, 2), amount)]


def gaussian(own_key, shape, spread, most, shards=(), kind=jnp.bfloat16):
    entries = jax.random.normal(own_key, shape, jnp.float32) * spread
    if len(shards) > 0:
        entries = block_levels(own_key, shape, shards, -0.22, 0.18) * entries
    return jnp.clip(entries, min=-most, max=most).astype(kind)


def gaussian_with(stream_key, dims, deviation, reach, cuts, heavy, kind=jnp.bfloat16):
    values = deviation * jax.random.normal(stream_key, dims, jnp.float32)
    if cuts:
        values = values * block_levels(stream_key, dims, cuts, -0.22, 0.18)
    return jnp.clip(raised(values, jax.random.fold_in(stream_key, 3), *heavy), -reach, reach).astype(kind)


def setup_inputs(seed: int = 0) -> dict:
    key_of = jax.random.split(jax.random.key(seed), 22)
    tokens = gaussian_with(key_of[0], (TOKENS, D), 1.0, 6.0, ((0, 32),), (0, 1, 32, 2.75))
    memory = gaussian_with(key_of[1], (SOURCES, D), 1.0, 6.0, ((0, 32),), (0, 1, 32, 2.75))
    target_segments = jax.vmap(lambda own: jnp.searchsorted(jnp.cumsum(ragged(own, SENTS, TOK_DEV, SENT_MOST, 2)), jnp.arange(TOK_DEV), side="right"))(jax.random.split(key_of[2], DEVICES)).reshape((DEVICES, TOK_DEV)).astype(jnp.int32)
    source_segments = jax.vmap(lambda own: jnp.searchsorted(jnp.cumsum(ragged(own, SENTS, MEM_DEV, SRC_MOST, 2)), jnp.arange(MEM_DEV), side="right"))(jax.random.split(key_of[3], DEVICES)).reshape((DEVICES, MEM_DEV)).astype(jnp.int32)
    self_query = gaussian(key_of[4], (D, D), D ** -0.5, 0.1875, ((0, 32),))
    self_key = gaussian(key_of[5], (D, D), D ** -0.5, 0.1875, ((0, 32),))
    self_value = gaussian(key_of[6], (D, D), D ** -0.5, 0.1875, ((0, 32),))
    self_output = gaussian(key_of[7], (D, D), (D // 128) ** -0.5, 2.0, ((0, 32),))
    cross_query = gaussian(key_of[8], (D, D), D ** -0.5, 0.1875, ((0, 32),))
    cross_key = gaussian(key_of[9], (D, D), D ** -0.5, 0.1875, ((0, 32),))
    cross_value = gaussian(key_of[10], (D, D), D ** -0.5, 0.1875, ((0, 32),))
    cross_output = gaussian(key_of[11], (D, D), (D // 128) ** -0.5, 2.0, ((0, 32),))
    expand_weight = gaussian(key_of[12], (D, FF), D ** -0.5, 0.1875, ((0, 32),))
    reduce_weight = gaussian(key_of[13], (FF, D), (FF // 64) ** -0.5, 0.75, ((0, 32),))
    self_gain = jnp.clip(1.0 + 0.18 * jax.random.normal(key_of[14], (D,), jnp.float32), 0.099609375, 1.8984375).astype(jnp.bfloat16)
    self_shift = gaussian(key_of[15], (D,), 0.5, 3.0, ((0, 32),))
    cross_gain = jnp.clip(1.0 + 0.18 * jax.random.normal(key_of[16], (D,), jnp.float32), 0.099609375, 1.8984375).astype(jnp.bfloat16)
    cross_shift = gaussian(key_of[17], (D,), 0.5, 3.0, ((0, 32),))
    final_gain = jnp.clip(1.0 + 0.18 * jax.random.normal(key_of[18], (D,), jnp.float32), 0.099609375, 1.8984375).astype(jnp.bfloat16)
    final_shift = gaussian(key_of[19], (D,), 0.5, 3.0, ((0, 32),))
    output_grad = gaussian(key_of[20], (TOKENS, D), 1.0, 6.0, ((0, 32),))
    return dict(tokens=tokens, memory=memory, target_segments=target_segments, source_segments=source_segments, self_query=self_query, self_key=self_key, self_value=self_value, self_output=self_output, cross_query=cross_query, cross_key=cross_key, cross_value=cross_value, cross_output=cross_output, expand_weight=expand_weight, reduce_weight=reduce_weight, self_gain=self_gain, self_shift=self_shift, cross_gain=cross_gain, cross_shift=cross_shift, final_gain=final_gain, final_shift=final_shift, output_grad=output_grad)


@jax.custom_vjp
def low(v):
    return lax.optimization_barrier(v.astype(jnp.bfloat16)).astype(jnp.float32)

@jax.custom_vjp
def low_back(v):
    return v

def low_keep(v):
    return (low(v), None)

def low_pass(kept, grad):
    return (grad,)

def back_keep(v):
    return (v, None)

def back_low(kept, grad):
    return (low(grad),)
low.defvjp(low_keep, low_pass)
low_back.defvjp(back_keep, back_low)
RESIDUAL_SCALE = 300.0 ** 0.25
EPSILON = 1e-05
NEGATIVE = -1e+30
HIGHEST = lax.Precision.HIGHEST

def round_both(values):
    return low(low_back(values))

def product(left, right):
    return jnp.dot(left, right, precision=HIGHEST)

def normalize(summed, gain, shift):
    center = lax.optimization_barrier(jnp.mean(summed, axis=-1, keepdims=True))
    centred = summed - center
    inverse = lax.rsqrt(lax.optimization_barrier(jnp.mean(centred * centred, axis=-1, keepdims=True)) + EPSILON)
    return centred * inverse * gain + shift

def split_heads(matrix):
    return matrix.reshape(matrix.shape[0], HEADS, HEAD_DIM)

def attend(query_rows, key_rows, value_rows, allowed):
    scores = jnp.einsum('qhd,khd->hqk', split_heads(query_rows), split_heads(key_rows), precision=HIGHEST) * HEAD_DIM ** (-0.5)
    scores = low_back(scores)
    scores = jnp.where(allowed[None], scores, NEGATIVE)
    highest = lax.optimization_barrier(jnp.max(scores, axis=-1, keepdims=True))
    weights = jnp.exp(scores - highest)
    chances = low(weights / lax.optimization_barrier(jnp.sum(weights, axis=-1, keepdims=True)))
    context = jnp.einsum('hqk,khd->qhd', chances, split_heads(value_rows), precision=HIGHEST)
    return round_both(context.reshape(query_rows.shape[0], HEADS * HEAD_DIM))

def decoder_layer(token_pack, memory_pack, params, target_ids, source_ids):
    query_one, key_one, value_one, out_one, query_two, key_two, value_two, out_two, expand_full, reduce_full, gain_one, shift_one, gain_two, shift_two, gain_three, shift_three = params
    positions = jnp.arange(token_pack.shape[0], dtype=jnp.int32)
    causal = (target_ids[:, None] == target_ids[None, :]) & (positions[None, :] <= positions[:, None])
    crossing = target_ids[:, None] == source_ids[None, :]
    queries = round_both(product(token_pack, query_one))
    keys_self = round_both(product(token_pack, key_one))
    values_self = round_both(product(token_pack, value_one))
    branch_one = low_back(product(attend(queries, keys_self, values_self, causal), out_one))
    first = normalize(RESIDUAL_SCALE * token_pack + branch_one, gain_one, shift_one)
    first_low = low(first)
    queries_two = round_both(product(first_low, query_two))
    keys_two = round_both(product(memory_pack, key_two))
    values_two = round_both(product(memory_pack, value_two))
    branch_two = low_back(product(attend(queries_two, keys_two, values_two, crossing), out_two))
    second = normalize(RESIDUAL_SCALE * first + branch_two, gain_two, shift_two)
    second_low = low(second)
    inner = low_back(product(second_low, expand_full))
    active = low(jax.nn.gelu(inner, approximate=True))
    branch_three = low_back(product(active, reduce_full))
    return normalize(RESIDUAL_SCALE * second + branch_three, gain_three, shift_three)

def reference(tokens, memory, target_segments, source_segments, self_query, self_key, self_value, self_output, cross_query, cross_key, cross_value, cross_output, expand_weight, reduce_weight, self_gain, self_shift, cross_gain, cross_shift, final_gain, final_shift, output_grad):
    packs = tokens.shape[0] // TOK_DEV
    params = tuple((item.astype(jnp.float32) for item in (self_query, self_key, self_value, self_output, cross_query, cross_key, cross_value, cross_output, expand_weight, reduce_weight, self_gain, self_shift, cross_gain, cross_shift, final_gain, final_shift)))
    token_rows = tokens.astype(jnp.float32).reshape(packs, TOK_DEV, D)
    memory_rows = memory.astype(jnp.float32).reshape(packs, MEM_DEV, D)

    def whole(token_rows, memory_rows, params):

        def single(item):
            return jax.checkpoint(decoder_layer)(item[0], item[1], params, item[2], item[3])
        return lax.map(single, (token_rows, memory_rows, target_segments, source_segments))
    result, pullback = jax.vjp(whole, token_rows, memory_rows, params)
    d_tokens, d_memory, d_params = pullback(output_grad.astype(jnp.float32).reshape(packs, TOK_DEV, D))
    return (result.reshape(packs * TOK_DEV, D).astype(jnp.bfloat16), d_tokens.reshape(packs * TOK_DEV, D), d_memory.reshape(packs * MEM_DEV, D), d_params[0], d_params[1], d_params[2], d_params[3], d_params[4], d_params[5], d_params[6], d_params[7], d_params[8], d_params[9], d_params[10], d_params[11], d_params[12], d_params[13], d_params[14], d_params[15])
```

```python
import functools

import jax
import jax.numpy as jnp
from jax import lax
from jax.experimental import pallas as pl
from jax.experimental.pallas import tpu as pltpu
from jax.sharding import PartitionSpec as P

HEADS = 16
HEAD_DIM = 64


RESIDUAL_SCALE = 300.0**0.25
EPSILON = 1e-05
NEGATIVE = -1e30
ALL = ("dp", "fsdp")


class Grid:
    def __init__(self, mesh):
        self.depth = mesh.shape["dp"] // 2
        self.plane = mesh.shape["fsdp"]
        self.count = mesh.size
        self.fast = self.plane == 4 and mesh.shape["dp"] % 2 == 0

    def place(self):
        index = lax.axis_index(ALL)
        return jnp.stack([index // 8, index // 4 % 2, index // 2 % 2, index % 2]).astype(jnp.int32)

    def move(self, value, dz=0, dc=0, dy=0, dx=0):
        pairs = []
        for index in range(self.count):
            z, c, y, x = index // 8, index // 4 % 2, index // 2 % 2, index % 2
            source = (((z + dz) % self.depth * 2 + (c ^ dc)) * 2 + (y ^ dy)) * 2 + (x ^ dx)
            pairs.append((source, index))
        return lax.ppermute(value, ALL, pairs)


def collect(grid, shard):
    half = grid.depth // 2
    own = jnp.stack([shard] + [grid.move(shard, dz=k) for k in range(1, grid.depth)])
    over_x = grid.move(own, dx=1)
    over_y = grid.move(own, dy=1)
    low = grid.move(over_x[:half], dy=1)
    high = grid.move(over_y[half:], dx=1)
    near = [((0, 0, 0), 0, own), ((0, 0, 1), 0, over_x), ((0, 1, 0), 0, over_y)]
    near += [((0, 1, 1), 0, low), ((0, 1, 1), half, high)]
    far = [((1, dy, dx), first, grid.move(piece, dc=1)) for (_, dy, dx), first, piece in near]
    return near + far


def assemble_kernel(spots, depth, rows, place, *refs):
    pieces, whole, sems = refs[:-2], refs[-2], refs[-1]
    z, c, y, x = place[0], place[1], place[2], place[3]
    copies = []
    for (offsets, first, count), piece in zip(spots, pieces):
        dc, dy, dx = offsets
        for k in range(count):
            there = lax.rem(z + (first + k), depth)
            owner = ((there * 2 + (c ^ dc)) * 2 + (y ^ dy)) * 2 + (x ^ dx)
            spot = pl.ds(pl.multiple_of(owner * rows, rows), rows)
            target = whole.at[:, spot, :] if len(whole.shape) == 3 else whole.at[spot, :]
            copies.append(pltpu.make_async_copy(piece.at[k], target, sems.at[len(copies)]))
    for copy in copies:
        copy.start()
    for copy in copies:
        copy.wait()


def assemble(grid, place, pieces):
    shape = pieces[0][2].shape[1:]
    rows = shape[-2]
    spots = tuple((offsets, first, piece.shape[0]) for offsets, first, piece in pieces)
    whole = shape[:-2] + (rows * grid.count, shape[-1])
    return pl.pallas_call(
        functools.partial(assemble_kernel, spots, grid.depth, rows),
        out_shape=jax.ShapeDtypeStruct(whole, jnp.bfloat16),
        in_specs=[pl.BlockSpec(memory_space=pltpu.SMEM)]
        + [pl.BlockSpec(memory_space=pl.ANY)] * len(pieces),
        out_specs=pl.BlockSpec(memory_space=pl.ANY),
        scratch_shapes=[pltpu.SemaphoreType.DMA((grid.count,))],
        cost_estimate=pl.CostEstimate(
            flops=0, bytes_accessed=4 * grid.count * pieces[0][2][0].size, transcendentals=0
        ),
        name="assemble",
    )(place, *[piece for _, _, piece in pieces])


def terms_kernel(depth, rows, place, left, left_far, right, right_far, own, over_x, over_y, low, high, turned):
    z, c, y, x = place[0], place[1], place[2], place[3]
    tokens = left.shape[0]

    @pl.when(pl.program_id(0) == 0)
    def _():
        for k in range(depth):
            there = lax.rem(z + k, depth)
            columns = pl.ds(pl.multiple_of((there * 2 + c) * (4 * rows), 4 * rows), 4 * rows)
            for side, source in enumerate((left, left_far)):
                block = source[:, columns].T
                for dy in range(2):
                    for dx in range(2):
                        near = (dy ^ y) * 2 + (dx ^ x)
                        spot = dy * 2 + dx
                        turned[near, k * rows : (k + 1) * rows, side * tokens : (side + 1) * tokens] = block[
                            spot * rows : (spot + 1) * rows
                        ]

    half = depth // 2
    for spot in range(4):
        part = turned[spot]
        total = jnp.dot(part[:, :tokens], right[...], preferred_element_type=jnp.float32)
        total += jnp.dot(part[:, tokens:], right_far[...], preferred_element_type=jnp.float32)
        total = total.astype(jnp.bfloat16).reshape(depth, rows, -1)
        if spot == 0:
            own[...] = total
        elif spot == 1:
            over_x[...] = total
        elif spot == 2:
            over_y[...] = total
        else:
            low[...] = total[:half]
            high[...] = total[half:]


def terms(grid, place, left, left_far, right, right_far, tile):
    tokens, features = left.shape
    width = right.shape[1]
    rows = features // grid.count
    depth = grid.depth
    counts = (depth, depth, depth, depth // 2, depth // 2)
    return pl.pallas_call(
        functools.partial(terms_kernel, depth, rows),
        grid=(width // tile,),
        out_shape=[jax.ShapeDtypeStruct((n, rows, width), jnp.bfloat16) for n in counts],
        in_specs=[pl.BlockSpec(memory_space=pltpu.SMEM)]
        + [pl.BlockSpec((tokens, features), lambda j: (0, 0))] * 2
        + [pl.BlockSpec((tokens, tile), lambda j: (0, j))] * 2,
        out_specs=[pl.BlockSpec((n, rows, tile), lambda j: (0, 0, j)) for n in counts],
        scratch_shapes=[pltpu.VMEM((4, depth * rows, 2 * tokens), jnp.bfloat16)],
        compiler_params=pltpu.CompilerParams(vmem_limit_bytes=40 * 2**20),
        cost_estimate=pl.CostEstimate(
            flops=2 * tokens * features * width,
            bytes_accessed=4 * tokens * (features + width) + features * width,
            transcendentals=0,
        ),
        name="terms",
    )(place, left, left_far, right, right_far)


def settle(grid, pieces):
    own, over_x, over_y, low, high = pieces
    half = grid.depth // 2
    got_low = grid.move(low, dy=1)
    got_high = grid.move(high, dx=1)
    wide = jnp.float32
    over_x = over_x.at[:half].add(got_low)
    over_y = over_y.at[half:].add(got_high)
    got_x = grid.move(over_x, dx=1)
    got_y = grid.move(over_y, dy=1)
    column = [
        (own[k].astype(wide) + got_x[k].astype(wide) + got_y[k].astype(wide)).astype(jnp.bfloat16)
        for k in range(grid.depth)
    ]
    total = column[0].astype(wide)
    for k in range(1, grid.depth):
        total = total + grid.move(column[k], dz=-k).astype(wide)
    return total


def matmul(left, right):
    return jnp.dot(left, right, preferred_element_type=jnp.float32)


def across(left, right):
    return jnp.einsum("ti,tj->ij", left, right, preferred_element_type=jnp.float32)


def against(left, right):
    return jnp.einsum("ti,ji->tj", left, right, preferred_element_type=jnp.float32)


def gelu_tanh(values):
    return jax.nn.gelu(values, approximate=True)


def normalize(summed, gain, shift):
    center = jnp.mean(summed, axis=-1, keepdims=True)
    centred = summed - center
    inverse = lax.rsqrt(jnp.mean(centred * centred, axis=-1, keepdims=True) + EPSILON)
    scaled = centred * inverse
    return (scaled * gain + shift, scaled, inverse)


def normalize_back(incoming, scaled, inverse, gain):
    spread = incoming * gain
    d_summed = inverse * (
        spread
        - jnp.mean(spread, axis=-1, keepdims=True)
        - scaled * jnp.mean(spread * scaled, axis=-1, keepdims=True)
    )
    return (d_summed, jnp.sum(incoming * scaled, axis=0), jnp.sum(incoming, axis=0))


def split_heads(matrix):
    return matrix.reshape(matrix.shape[0], HEADS, HEAD_DIM)


def scores_of(query_rows, key_rows, allowed):
    raw = jnp.einsum(
        "qhd,khd->hqk",
        split_heads(query_rows),
        split_heads(key_rows),
        preferred_element_type=jnp.float32,
    ) * HEAD_DIM ** (-0.5)
    return jnp.where(allowed[None], raw, NEGATIVE)


def attend_forward(query_rows, key_rows, value_rows, allowed):
    scores = scores_of(query_rows, key_rows, allowed)
    highest = jnp.max(scores, axis=-1, keepdims=True)
    weights = jnp.exp(scores - highest)
    totals = jnp.sum(weights, axis=-1, keepdims=True)
    chances = (weights / totals).astype(jnp.bfloat16)
    context = jnp.einsum(
        "hqk,khd->qhd", chances, split_heads(value_rows), preferred_element_type=jnp.float32
    )
    return (
        context.reshape(query_rows.shape[0], HEADS * HEAD_DIM).astype(jnp.bfloat16),
        highest + jnp.log(totals),
    )


def attend_back(query_rows, key_rows, value_rows, allowed, logsum, d_context):
    query_heads = split_heads(query_rows)
    key_heads = split_heads(key_rows)
    d_heads = split_heads(d_context)
    chances = jnp.exp(scores_of(query_rows, key_rows, allowed) - logsum)
    d_chances = jnp.einsum(
        "qhd,khd->hqk", d_heads, split_heads(value_rows), preferred_element_type=jnp.float32
    )
    d_value = jnp.einsum(
        "hqk,qhd->khd", chances.astype(jnp.bfloat16), d_heads, preferred_element_type=jnp.float32
    )
    centre = jnp.sum(d_chances * chances, axis=-1, keepdims=True)
    d_scores = (chances * (d_chances - centre)).astype(jnp.bfloat16)
    d_query = jnp.einsum(
        "hqk,khd->qhd", d_scores, key_heads, preferred_element_type=jnp.float32
    ) * HEAD_DIM ** (-0.5)
    d_key = jnp.einsum(
        "hqk,qhd->khd", d_scores, query_heads, preferred_element_type=jnp.float32
    ) * HEAD_DIM ** (-0.5)
    query_count = query_rows.shape[0]
    key_count = key_rows.shape[0]
    return (
        d_query.reshape(query_count, HEADS * HEAD_DIM).astype(jnp.bfloat16),
        d_key.reshape(key_count, HEADS * HEAD_DIM).astype(jnp.bfloat16),
        d_value.reshape(key_count, HEADS * HEAD_DIM).astype(jnp.bfloat16),
    )


def gather_norms(rows):
    held = rows.shape[1]
    count = lax.axis_size(ALL)
    spread = jnp.zeros((8, held * count), jnp.float32)
    spread = lax.dynamic_update_slice(spread, rows, (0, lax.axis_index(ALL) * held))
    return lax.psum(spread, ALL)


def sum_norms(terms_of):
    held = terms_of.shape[1] // lax.axis_size(ALL)
    total = lax.psum(jnp.pad(terms_of, ((0, 2), (0, 0))), ALL)
    return lax.dynamic_slice(total, (0, lax.axis_index(ALL) * held), (8, held))


def whole_of(grid, place, rows):
    if not grid.fast:
        return lax.all_gather(rows, ALL, axis=rows.ndim - 2, tiled=True)
    return assemble(grid, place, collect(grid, rows))


def summed(grid, place, left, right):
    if not grid.fast:
        return lax.psum_scatter(across(left, right), ALL, scatter_dimension=0, tiled=True)
    left_far = grid.move(left, dc=1)
    right_far = grid.move(right, dc=1)
    return settle(grid, terms(grid, place, left, left_far, right, right_far, 512))


def per_device(
    grid,
    tokens,
    memory,
    target_segments,
    source_segments,
    self_query,
    self_key,
    self_value,
    self_output,
    cross_query,
    cross_key,
    cross_value,
    cross_output,
    expand_weight,
    reduce_weight,
    self_gain,
    self_shift,
    cross_gain,
    cross_shift,
    final_gain,
    final_shift,
    output_grad,
):
    norm_rows = jnp.stack([self_gain, self_shift, cross_gain, cross_shift, final_gain, final_shift])
    place = grid.place()
    gains = gather_norms(norm_rows.astype(jnp.float32))
    first_rows = jnp.stack([self_query, self_key, self_value, self_output])
    second_rows = jnp.stack([cross_query, cross_key, cross_value, cross_output])
    matrices_one = whole_of(grid, place, first_rows)
    matrices_two = whole_of(grid, place, second_rows)
    expand_full = whole_of(grid, place, expand_weight)
    reduce_full = whole_of(grid, place, reduce_weight)
    matrices = [matrices_one[i] for i in range(4)] + [matrices_two[i] for i in range(4)]
    target_ids = target_segments[0]
    source_ids = source_segments[0]
    positions = lax.iota(jnp.int32, tokens.shape[0])
    causal = (target_ids[:, None] == target_ids[None, :]) & (
        positions[None, :] <= positions[:, None]
    )
    crossing = target_ids[:, None] == source_ids[None, :]
    query_one = matmul(tokens, matrices[0]).astype(jnp.bfloat16)
    key_one = matmul(tokens, matrices[1]).astype(jnp.bfloat16)
    value_one = matmul(tokens, matrices[2]).astype(jnp.bfloat16)
    context_one, logsum_one = attend_forward(query_one, key_one, value_one, causal)
    branch_one = matmul(context_one, matrices[3])
    first, first_scaled, first_inverse = normalize(
        RESIDUAL_SCALE * tokens.astype(jnp.float32) + branch_one, gains[0], gains[1]
    )
    first_low = first.astype(jnp.bfloat16)
    query_two = matmul(first_low, matrices[4]).astype(jnp.bfloat16)
    key_two = matmul(memory, matrices[5]).astype(jnp.bfloat16)
    value_two = matmul(memory, matrices[6]).astype(jnp.bfloat16)
    context_two, logsum_two = attend_forward(query_two, key_two, value_two, crossing)
    branch_two = matmul(context_two, matrices[7])
    second, second_scaled, second_inverse = normalize(
        RESIDUAL_SCALE * first + branch_two, gains[2], gains[3]
    )
    second_low = second.astype(jnp.bfloat16)
    inner = matmul(second_low, expand_full)
    active = gelu_tanh(inner).astype(jnp.bfloat16)
    branch_three = matmul(active, reduce_full)
    final, final_scaled, final_inverse = normalize(
        RESIDUAL_SCALE * second + branch_three, gains[4], gains[5]
    )
    output = final.astype(jnp.bfloat16)
    d_sum_three, final_gain_term, final_shift_term = normalize_back(
        output_grad.astype(jnp.float32), final_scaled, final_inverse, gains[4]
    )
    d_branch_three = d_sum_three.astype(jnp.bfloat16)
    reduce_term = summed(grid, place, active, d_branch_three)
    d_active = against(d_branch_three, reduce_full)
    d_inner = jax.vjp(gelu_tanh, inner)[1](d_active)[0].astype(jnp.bfloat16)
    expand_term = summed(grid, place, second_low, d_inner)
    d_second = RESIDUAL_SCALE * d_sum_three + against(d_inner, expand_full)
    d_sum_two, cross_gain_term, cross_shift_term = normalize_back(
        d_second, second_scaled, second_inverse, gains[2]
    )
    d_branch_two = d_sum_two.astype(jnp.bfloat16)
    cross_output_term = summed(grid, place, context_two, d_branch_two)
    d_context_two = against(d_branch_two, matrices[7]).astype(jnp.bfloat16)
    d_query_two, d_key_two, d_value_two = attend_back(
        query_two, key_two, value_two, crossing, logsum_two, d_context_two
    )
    cross_query_term = summed(grid, place, first_low, d_query_two)
    cross_key_term = summed(grid, place, memory, d_key_two)
    cross_value_term = summed(grid, place, memory, d_value_two)
    memory_grad = against(d_key_two, matrices[5]) + against(d_value_two, matrices[6])
    d_first = RESIDUAL_SCALE * d_sum_two + against(d_query_two, matrices[4])
    d_sum_one, self_gain_term, self_shift_term = normalize_back(
        d_first, first_scaled, first_inverse, gains[0]
    )
    d_branch_one = d_sum_one.astype(jnp.bfloat16)
    self_output_term = summed(grid, place, context_one, d_branch_one)
    d_context_one = against(d_branch_one, matrices[3]).astype(jnp.bfloat16)
    d_query_one, d_key_one, d_value_one = attend_back(
        query_one, key_one, value_one, causal, logsum_one, d_context_one
    )
    self_query_term = summed(grid, place, tokens, d_query_one)
    self_key_term = summed(grid, place, tokens, d_key_one)
    self_value_term = summed(grid, place, tokens, d_value_one)
    tokens_grad = (
        RESIDUAL_SCALE * d_sum_one
        + against(d_query_one, matrices[0])
        + against(d_key_one, matrices[1])
        + against(d_value_one, matrices[2])
    )
    norm_terms = jnp.stack(
        [
            self_gain_term,
            self_shift_term,
            cross_gain_term,
            cross_shift_term,
            final_gain_term,
            final_shift_term,
        ]
    )
    norm_owned = sum_norms(norm_terms)
    return (
        output,
        tokens_grad,
        memory_grad,
        self_query_term,
        self_key_term,
        self_value_term,
        self_output_term,
        cross_query_term,
        cross_key_term,
        cross_value_term,
        cross_output_term,
        expand_term,
        reduce_term,
        norm_owned[0],
        norm_owned[1],
        norm_owned[2],
        norm_owned[3],
        norm_owned[4],
        norm_owned[5],
    )


def solution(mesh):
    return jax.shard_map(
        functools.partial(per_device, Grid(mesh)),
        mesh=mesh,
        in_specs=(
            P(("dp", "fsdp"), None),
            P(("dp", "fsdp"), None),
            P(("dp", "fsdp"), None),
            P(("dp", "fsdp"), None),
            P(("dp", "fsdp"), None),
            P(("dp", "fsdp"), None),
            P(("dp", "fsdp"), None),
            P(("dp", "fsdp"), None),
            P(("dp", "fsdp"), None),
            P(("dp", "fsdp"), None),
            P(("dp", "fsdp"), None),
            P(("dp", "fsdp"), None),
            P(("dp", "fsdp"), None),
            P(("dp", "fsdp"), None),
            P(("dp", "fsdp")),
            P(("dp", "fsdp")),
            P(("dp", "fsdp")),
            P(("dp", "fsdp")),
            P(("dp", "fsdp")),
            P(("dp", "fsdp")),
            P(("dp", "fsdp"), None),
        ),
        out_specs=(
            P(("dp", "fsdp"), None),
            P(("dp", "fsdp"), None),
            P(("dp", "fsdp"), None),
            P(("dp", "fsdp"), None),
            P(("dp", "fsdp"), None),
            P(("dp", "fsdp"), None),
            P(("dp", "fsdp"), None),
            P(("dp", "fsdp"), None),
            P(("dp", "fsdp"), None),
            P(("dp", "fsdp"), None),
            P(("dp", "fsdp"), None),
            P(("dp", "fsdp"), None),
            P(("dp", "fsdp"), None),
            P(("dp", "fsdp")),
            P(("dp", "fsdp")),
            P(("dp", "fsdp")),
            P(("dp", "fsdp")),
            P(("dp", "fsdp")),
            P(("dp", "fsdp")),
        ),
        check_vma=False,
    )
```

```python
import functools

import jax
import jax.numpy as jnp
from jax import lax
from jax.experimental import pallas as pl
from jax.experimental.pallas import tpu as pltpu
from jax.sharding import PartitionSpec as P

HEADS = 16
HEAD_DIM = 64


RESIDUAL_SCALE = 300.0**0.25
EPSILON = 1e-05
NEGATIVE = -1e30
ALL = ("dp", "fsdp")


class Grid:
    def __init__(self, mesh):
        self.depth = mesh.shape["dp"] // 2
        self.count = mesh.size
        self.fast = mesh.shape["fsdp"] == 4 and mesh.shape["dp"] == 8

    def place(self):
        index = lax.axis_index(ALL)
        return jnp.stack([index // 8, index // 4 % 2, index // 2 % 2, index % 2]).astype(jnp.int32)

    def move(self, value, dz=0, dc=0, dy=0, dx=0):
        offset = ((dz * 2 + dc) * 2 + dy) * 2 + dx
        return lax.ppermute(value, ALL, [(index ^ offset, index) for index in range(self.count)])


def after(value, *others):
    return lax.optimization_barrier((value,) + others)[0]


def gather_direct(grid, shard):
    return jnp.stack([shard] + [grid.move(shard, dz=k) for k in range(1, grid.depth)])


def gather_pair(grid, shard):
    return jnp.stack([shard, grid.move(shard, dz=1)])


def gather_pairs(grid, pair):
    return jnp.concatenate([pair, grid.move(pair, dz=2)])


def gather_sides(grid, own):
    return grid.move(own, dx=1), grid.move(own, dy=1)


def gather_corner(grid, own, sides):
    half = grid.depth // 2
    low = grid.move(sides[0][:half], dy=1)
    high = grid.move(sides[1][half:], dx=1)
    far = grid.move(jnp.concatenate([own, *sides]), dc=1)
    return low, high, far


def gather_last(grid, low, high):
    corner = jnp.concatenate([low, high])
    return corner, grid.move(corner, dc=1)


def wide_dot(left, right):
    return jnp.dot(left, right, preferred_element_type=jnp.float32)


def dot_rows(left, right):
    return lax.dot_general(left, right, (((1,), (1,)), ((), ())), preferred_element_type=jnp.float32)


def dot_columns(left, right):
    return lax.dot_general(left, right, (((0,), (0,)), ((), ())), preferred_element_type=jnp.float32)


def whole_call(body, name, inputs, shapes, scratch=(), limit=56):
    arrays, specs = [], []
    for item in inputs:
        if not isinstance(item, tuple):
            item = (item, item.shape, (0,) * item.ndim)
        arrays.append(item[0])
        if len(item) == 2:
            specs.append(pl.BlockSpec(memory_space=item[1]))
        else:
            specs.append(pl.BlockSpec(item[1], lambda i, index=item[2]: index))
    outs, out_specs = [], []
    for item in shapes:
        outs.append(jax.ShapeDtypeStruct(item[0], item[1]))
        if len(item) == 3:
            out_specs.append(pl.BlockSpec(memory_space=item[2]))
        else:
            out_specs.append(pl.BlockSpec(item[0], lambda i, rank=len(item[0]): (0,) * rank))
    return pl.pallas_call(
        body,
        grid=(1,),
        out_shape=outs,
        in_specs=specs,
        out_specs=out_specs,
        scratch_shapes=list(scratch),
        compiler_params=pltpu.CompilerParams(vmem_limit_bytes=limit * 2**20),
        cost_estimate=pl.CostEstimate(flops=1, bytes_accessed=1, transcendentals=0),
        name=name,
    )(*arrays)


def arrivals_of(depth, rows, place, pieces, held, sems, held_norms=None):
    own, over_x, over_y, far, corner, corner_far = pieces
    z, c, y, x = place[0], place[1], place[2], place[3]
    width = held.shape[-1]
    arrivals = []
    for k in range(depth):
        column = []
        for n in range(8):
            dc, dy, dx = n // 4, n // 2 % 2, n % 2
            if n % 4 == 3:
                piece, spot = (corner_far if dc else corner), k
            elif dc:
                piece, spot = far, (n % 4) * depth + k
            else:
                piece, spot = (own, over_x, over_y)[n], k
            owner = (((z ^ k) * 2 + (c ^ dc)) * 2 + (y ^ dy)) * 2 + (x ^ dx)
            target = held.at[..., pl.ds(pl.multiple_of(owner * rows, rows), rows), :]
            source = piece.at[spot]
            order = k * 8 + n
            if held_norms is None:
                column.append(pltpu.make_async_copy(source, target, sems.at[order]))
            else:
                column.append(pltpu.make_async_copy(source.at[..., :width], target, sems.at[order]))
                column.append(
                    pltpu.make_async_copy(
                        source.at[0:2, :, pl.ds(width, 128)],
                        held_norms.at[owner],
                        sems.at[8 * depth + order],
                    )
                )
        for copy in column:
            copy.start()
        arrivals.append(column)
    return arrivals


def pass_on(depth, rows, place, arrivals, held, whole, sems):
    leaving = []
    for k in range(depth):
        for copy in arrivals[k]:
            copy.wait()
        spot = pl.ds(pl.multiple_of((place[0] ^ k) * (8 * rows), 8 * rows), 8 * rows)
        leaving.append(pltpu.make_async_copy(held.at[..., spot, :], whole.at[..., spot, :], sems.at[k]))
        leaving[k].start()
    return leaving


def norm_rows_of(summed, gain, shift):
    center = jnp.mean(summed, axis=-1, keepdims=True)
    centred = summed - center
    inverse = lax.rsqrt(jnp.mean(centred * centred, axis=-1, keepdims=True) + EPSILON)
    scaled = centred * inverse
    return scaled * gain + shift, scaled, inverse


def norm_rows_back(incoming, scaled, inverse, gain):
    spread_out = incoming * gain
    d_summed = inverse * (
        spread_out
        - jnp.mean(spread_out, axis=-1, keepdims=True)
        - scaled * jnp.mean(spread_out * scaled, axis=-1, keepdims=True)
    )
    return d_summed, jnp.sum(incoming * scaled, axis=0, keepdims=True), jnp.sum(incoming, axis=0, keepdims=True)


def head_halves():
    lane = lax.broadcasted_iota(jnp.int32, (1, 2 * HEAD_DIM), 1)
    return [
        jnp.where(lane < HEAD_DIM, 1.0, 0.0).astype(jnp.bfloat16),
        jnp.where(lane < HEAD_DIM, 0.0, 1.0).astype(jnp.bfloat16),
    ]


def attend_heads(query, key, value, allowed, context, logsum):
    halves = head_halves()
    lane = lax.broadcasted_iota(jnp.int32, logsum.shape, 1)
    logsum[...] = jnp.zeros_like(logsum)

    def pair(p, carry):
        lanes = pl.ds(pl.multiple_of(p * 2 * HEAD_DIM, 2 * HEAD_DIM), 2 * HEAD_DIM)
        queries, keys, values = query[:, lanes], key[:, lanes], value[:, lanes]
        total = None
        for side, half in enumerate(halves):
            scores = dot_rows(queries * half, keys) * HEAD_DIM ** (-0.5)
            scores = jnp.where(allowed[...] > 0, scores, NEGATIVE)
            highest = jnp.max(scores, axis=-1, keepdims=True)
            weights = jnp.exp(scores - highest)
            totals = jnp.sum(weights, axis=-1, keepdims=True)
            chances = (weights * (1.0 / totals)).astype(jnp.bfloat16)
            part = wide_dot(chances, values * half)
            total = part if total is None else total + part
            logsum[...] = jnp.where(lane == 2 * p + side, highest + jnp.log(totals), logsum[...])
        context[:, lanes] = total.astype(jnp.bfloat16)
        return carry

    lax.fori_loop(0, HEADS // 2, pair, 0)


def attend_heads_back(query, key, value, allowed, logsum, d_context, d_query, d_key, d_value):
    halves = head_halves()
    lane = lax.broadcasted_iota(jnp.int32, logsum.shape, 1)
    scale = HEAD_DIM ** (-0.5)

    def pair(p, carry):
        lanes = pl.ds(pl.multiple_of(p * 2 * HEAD_DIM, 2 * HEAD_DIM), 2 * HEAD_DIM)
        queries, keys, values, d_outs = query[:, lanes], key[:, lanes], value[:, lanes], d_context[:, lanes]
        sums = [None, None, None]
        for side, half in enumerate(halves):
            own_sum = jnp.sum(jnp.where(lane == 2 * p + side, logsum[...], 0.0), axis=-1, keepdims=True)
            own_queries, own_outs = queries * half, d_outs * half
            scores = dot_rows(own_queries, keys) * scale
            scores = jnp.where(allowed[...] > 0, scores, NEGATIVE)
            chances = jnp.exp(scores - own_sum)
            d_chances = dot_rows(own_outs, values)
            centre = jnp.sum(d_chances * chances, axis=-1, keepdims=True)
            d_scores = (chances * (d_chances - centre)).astype(jnp.bfloat16)
            parts = (
                wide_dot(d_scores, keys * half),
                dot_columns(d_scores, own_queries),
                dot_columns(chances.astype(jnp.bfloat16), own_outs),
            )
            sums = [part if old is None else old + part for old, part in zip(sums, parts)]
        d_query[:, lanes] = (sums[0] * scale).astype(jnp.bfloat16)
        d_key[:, lanes] = (sums[1] * scale).astype(jnp.bfloat16)
        d_value[:, lanes] = sums[2].astype(jnp.bfloat16)
        return carry

    lax.fori_loop(0, HEADS // 2, pair, 0)


def self_allowed(ids_column, ids_row, allowed):
    rows, columns = allowed.shape
    later = lax.broadcasted_iota(jnp.int32, (rows, columns), 0) >= lax.broadcasted_iota(
        jnp.int32, (rows, columns), 1
    )
    same = ids_column[...] == ids_row[...]
    allowed[...] = jnp.where(later & same, 1.0, 0.0)


def cross_allowed(ids_column, ids_row, allowed):
    allowed[...] = jnp.where(ids_column[...] == ids_row[...], 1.0, 0.0)


def self_forward_kernel(depth, rows, place, tokens, ids_column, ids_row, *refs):
    pieces, refs = refs[:6], refs[6:]
    whole, gains, query, key, value, context, logsum, first, first_low, scaled, inverse = refs[:11]
    held, held_norms, allowed, in_sems, out_sems = refs[11:]
    arrivals = arrivals_of(depth, rows, place, pieces, held, in_sems, held_norms)
    self_allowed(ids_column, ids_row, allowed)
    leaving = pass_on(depth, rows, place, arrivals, held, whole, out_sems)
    packed = held_norms[0].astype(jnp.float32)
    for owner in range(1, 8 * depth):
        packed += held_norms[owner].astype(jnp.float32)
    gains[...] = jnp.zeros_like(gains)
    for n in range(6):
        for j in range(8):
            r = n * 8 + j
            gains[n : n + 1, j * 128 : (j + 1) * 128] = packed[r // rows, r % rows : r % rows + 1, :]
    for n, out in enumerate((query, key, value)):
        out[...] = wide_dot(tokens[...], held[n]).astype(jnp.bfloat16)
    attend_heads(query, key, value, allowed, context, logsum)
    branch = wide_dot(context[...], held[3])
    summed = RESIDUAL_SCALE * tokens[...].astype(jnp.float32) + branch
    first[...], scaled[...], inverse[...] = norm_rows_of(summed, gains[0:1, :], gains[1:2, :])
    first_low[...] = first[...].astype(jnp.bfloat16)
    for copy in leaving:
        copy.wait()


def self_forward(grid, place, tokens, ids_column, ids_row, pieces):
    count, width = tokens.shape
    rows = pieces[0].shape[2]
    low, full = jnp.bfloat16, jnp.float32
    shape = (count, width)
    return whole_call(
        functools.partial(self_forward_kernel, grid.depth, rows),
        "self_forward",
        [(place, pltpu.SMEM), tokens, ids_column, ids_row] + [(piece, pl.ANY) for piece in pieces],
        [((4, width, width), low, pl.ANY), ((8, width), full)]
        + [(shape, low)] * 4
        + [((count, 128), full), (shape, full), (shape, low), (shape, full), ((count, 1), full)],
        [
            pltpu.VMEM((4, width, width), low),
            pltpu.VMEM((grid.count, 2, rows, 128), low),
            pltpu.VMEM((count, count), full),
            pltpu.SemaphoreType.DMA((2 * grid.count,)),
            pltpu.SemaphoreType.DMA((grid.depth,)),
        ],
    )


def cross_forward_kernel(depth, rows, place, first, first_low, memory, gains, ids_column, ids_row, *refs):
    pieces, refs = refs[:6], refs[6:]
    whole, query, key, value, context, logsum, second, second_low, scaled, inverse = refs[:10]
    held, allowed, in_sems, out_sems = refs[10:]
    arrivals = arrivals_of(depth, rows, place, pieces, held, in_sems)
    cross_allowed(ids_column, ids_row, allowed)
    leaving = pass_on(depth, rows, place, arrivals, held, whole, out_sems)
    query[...] = wide_dot(first_low[...], held[0]).astype(jnp.bfloat16)
    key[...] = wide_dot(memory[...], held[1]).astype(jnp.bfloat16)
    value[...] = wide_dot(memory[...], held[2]).astype(jnp.bfloat16)
    attend_heads(query, key, value, allowed, context, logsum)
    summed = RESIDUAL_SCALE * first[...] + wide_dot(context[...], held[3])
    second[...], scaled[...], inverse[...] = norm_rows_of(summed, gains[2:3, :], gains[3:4, :])
    second_low[...] = second[...].astype(jnp.bfloat16)
    for copy in leaving:
        copy.wait()


def cross_forward(grid, place, first, first_low, memory, gains, ids_column, ids_row, pieces):
    count, width = first.shape
    others = memory.shape[0]
    rows = pieces[0].shape[2]
    low, full = jnp.bfloat16, jnp.float32
    shape, other_shape = (count, width), (others, width)
    return whole_call(
        functools.partial(cross_forward_kernel, grid.depth, rows),
        "cross_forward",
        [(place, pltpu.SMEM), first, first_low, memory, gains, ids_column, ids_row]
        + [(piece, pl.ANY) for piece in pieces],
        [((4, width, width), low, pl.ANY), (shape, low), (other_shape, low), (other_shape, low), (shape, low)]
        + [((count, 128), full), (shape, full), (shape, low), (shape, full), ((count, 1), full)],
        [
            pltpu.VMEM((4, width, width), low),
            pltpu.VMEM((count, others), full),
            pltpu.SemaphoreType.DMA((grid.count,)),
            pltpu.SemaphoreType.DMA((grid.depth,)),
        ],
    )


TANH_SCALE = 0.7978845608028654
TANH_CUBE = 0.044715


def expand_forward_kernel(depth, rows, place, second_low, *refs):
    pieces, refs = refs[:6], refs[6:]
    whole, active, slope, held, in_sems, out_sems = refs
    arrivals = arrivals_of(depth, rows, place, pieces, held, in_sems)
    leaving = pass_on(depth, rows, place, arrivals, held, whole, out_sems)
    left = second_low[...]

    def tile(j, carry):
        lanes = pl.ds(pl.multiple_of(j * 512, 512), 512)
        inner = wide_dot(left, held[:, lanes])
        square = inner * inner
        bend = jnp.tanh(TANH_SCALE * (inner * (1.0 + TANH_CUBE * square)))
        half = 0.5 + 0.5 * bend
        active[:, lanes] = (inner * half).astype(jnp.bfloat16)
        slope[:, lanes] = half + (0.5 * TANH_SCALE) * inner * (1.0 - bend * bend) * (
            1.0 + (3.0 * TANH_CUBE) * square
        )
        return carry

    lax.fori_loop(0, held.shape[1] // 512, tile, 0)
    for copy in leaving:
        copy.wait()


def expand_forward(grid, place, second_low, pieces):
    count, width = second_low.shape
    rows, hidden = pieces[0].shape[1:]
    low = jnp.bfloat16
    return whole_call(
        functools.partial(expand_forward_kernel, grid.depth, rows),
        "expand_forward",
        [(place, pltpu.SMEM), second_low] + [(piece, pl.ANY) for piece in pieces],
        [((width, hidden), low, pl.ANY), ((count, hidden), low), ((count, hidden), jnp.float32)],
        [
            pltpu.VMEM((width, hidden), low),
            pltpu.SemaphoreType.DMA((grid.count,)),
            pltpu.SemaphoreType.DMA((grid.depth,)),
        ],
    )


def reduce_both_kernel(depth, rows, place, active, slope, second, gains, output_grad, *refs):
    pieces, refs = refs[:6], refs[6:]
    output, d_summed, d_branch, d_inner, norm_terms, held, in_sems = refs
    arrivals = arrivals_of(depth, rows, place, pieces, held, in_sems)
    for column in arrivals:
        for copy in column:
            copy.wait()
    summed = RESIDUAL_SCALE * second[...] + wide_dot(active[...], held[...])
    final, scaled, inverse = norm_rows_of(summed, gains[4:5, :], gains[5:6, :])
    output[...] = final.astype(jnp.bfloat16)
    d_sum, gain_term, shift_term = norm_rows_back(
        output_grad[...].astype(jnp.float32), scaled, inverse, gains[4:5, :]
    )
    norm_terms[0:1, :] = gain_term
    norm_terms[1:2, :] = shift_term
    d_summed[...] = d_sum
    d_branch[...] = d_sum.astype(jnp.bfloat16)
    left = d_branch[...]

    def tile(j, carry):
        lanes = pl.ds(pl.multiple_of(j * 512, 512), 512)
        d_active = dot_rows(left, held[lanes, :])
        d_inner[:, lanes] = (d_active * slope[:, lanes]).astype(jnp.bfloat16)
        return carry

    lax.fori_loop(0, held.shape[0] // 512, tile, 0)


def reduce_both(grid, place, active, slope, second, gains, output_grad, pieces):
    count, width = second.shape
    hidden = active.shape[1]
    rows = pieces[0].shape[1]
    low, full = jnp.bfloat16, jnp.float32
    shape = (count, width)
    return whole_call(
        functools.partial(reduce_both_kernel, grid.depth, rows),
        "reduce_both",
        [(place, pltpu.SMEM), active, slope, second, gains, output_grad]
        + [(piece, pl.ANY) for piece in pieces],
        [(shape, low), (shape, full), (shape, low), ((count, hidden), low), ((2, width), full)],
        [pltpu.VMEM((hidden, width), low), pltpu.SemaphoreType.DMA((grid.count,))],
    )


def expand_back_kernel(d_inner, expand, d_sum_three, scaled, inverse, gains, out_weight, d_summed, d_branch, d_context, norm_terms):
    d_second = RESIDUAL_SCALE * d_sum_three[...] + dot_rows(d_inner[...], expand[...])
    d_sum, norm_terms[0:1, :], norm_terms[1:2, :] = norm_rows_back(
        d_second, scaled[...], inverse[...], gains[2:3, :]
    )
    d_summed[...] = d_sum
    d_branch[...] = d_sum.astype(jnp.bfloat16)
    d_context[...] = dot_rows(d_branch[...], out_weight[0]).astype(jnp.bfloat16)


def expand_back(d_inner, expand, d_sum_three, scaled, inverse, gains, second_full):
    shape = d_sum_three.shape
    width = shape[1]
    low, full = jnp.bfloat16, jnp.float32
    return whole_call(
        expand_back_kernel,
        "expand_back",
        [d_inner, expand, d_sum_three, scaled, inverse, gains, (second_full, (1, width, width), (3, 0, 0))],
        [(shape, full), (shape, low), (shape, low), ((2, width), full)],
    )


def cross_back_kernel(
    query, key, value, logsum, d_context, ids_column, ids_row, d_sum_two, scaled, inverse, gains,
    query_weight, out_weight, d_query, d_key, d_value, d_summed, d_branch, d_context_one, norm_terms, allowed,
):
    cross_allowed(ids_column, ids_row, allowed)
    attend_heads_back(query, key, value, allowed, logsum, d_context, d_query, d_key, d_value)
    d_first = RESIDUAL_SCALE * d_sum_two[...] + dot_rows(d_query[...], query_weight[0])
    d_sum, norm_terms[0:1, :], norm_terms[1:2, :] = norm_rows_back(
        d_first, scaled[...], inverse[...], gains[0:1, :]
    )
    d_summed[...] = d_sum
    d_branch[...] = d_sum.astype(jnp.bfloat16)
    d_context_one[...] = dot_rows(d_branch[...], out_weight[0]).astype(jnp.bfloat16)


def cross_back(query, key, value, logsum, d_context, ids_column, ids_row, d_sum_two, scaled, inverse, gains, second_full, first_full):
    shape, other_shape = query.shape, key.shape
    width = shape[1]
    low, full = jnp.bfloat16, jnp.float32
    block = (1, width, width)
    return whole_call(
        cross_back_kernel,
        "cross_back",
        [query, key, value, logsum, d_context, ids_column, ids_row, d_sum_two, scaled, inverse, gains]
        + [(second_full, block, (0, 0, 0)), (first_full, block, (3, 0, 0))],
        [(shape, low), (other_shape, low), (other_shape, low), (shape, full), (shape, low), (shape, low)]
        + [((2, width), full)],
        [pltpu.VMEM((shape[0], other_shape[0]), full)],
    )


def self_back_kernel(query, key, value, logsum, d_context, ids_column, ids_row, d_rows, allowed):
    self_allowed(ids_column, ids_row, allowed)
    count = query.shape[0]
    outs = [d_rows.at[n * count : (n + 1) * count] for n in range(3)]
    attend_heads_back(query, key, value, allowed, logsum, d_context, *outs)


def self_back(query, key, value, logsum, d_context, ids_column, ids_row):
    count, width = query.shape
    return whole_call(
        self_back_kernel,
        "self_back",
        [query, key, value, logsum, d_context, ids_column, ids_row],
        [((3 * count, width), jnp.bfloat16)],
        [pltpu.VMEM((count, count), jnp.float32)],
    )[0]


def inputs_back_kernel(d_rows, d_key, d_value, d_sum_one, w_query, w_key, w_value, w_key_two, w_value_two, tokens_grad, memory_grad):
    count = d_sum_one.shape[0]
    total = RESIDUAL_SCALE * d_sum_one[...]
    for n, weight in enumerate((w_query, w_key, w_value)):
        total += dot_rows(d_rows[n * count : (n + 1) * count, :], weight[0])
    tokens_grad[...] = total
    memory_grad[...] = dot_rows(d_key[...], w_key_two[0]) + dot_rows(d_value[...], w_value_two[0])


def inputs_back(d_rows, d_key, d_value, d_sum_one, first_full, second_full):
    width = d_key.shape[1]
    block = (1, width, width)
    return whole_call(
        inputs_back_kernel,
        "inputs_back",
        [d_rows, d_key, d_value, d_sum_one]
        + [(first_full, block, (n, 0, 0)) for n in range(3)]
        + [(second_full, block, (n, 0, 0)) for n in (1, 2)],
        [(d_sum_one.shape, jnp.float32), (d_key.shape, jnp.float32)],
    )


def turn(depth, rows, place, sources, turned):
    z, c, y, x = place[0], place[1], place[2], place[3]
    tokens = sources[0].shape[0]
    for k in range(depth):
        there = z ^ k
        columns = pl.ds(pl.multiple_of((there * 2 + c) * (4 * rows), 4 * rows), 4 * rows)
        for side, source in enumerate(sources):
            block = source[:, columns].T
            named = [block[n * rows : (n + 1) * rows] for n in range(4)]
            named = [jnp.where(x == 0, named[n], named[n ^ 1]) for n in range(4)]
            named = [jnp.where(y == 0, named[n], named[n ^ 2]) for n in range(4)]
            for spot in range(4):
                turned[spot, k * rows : (k + 1) * rows, side * tokens : (side + 1) * tokens] = named[spot]


def spread(depth, rows, turned, rights, outs):
    tokens = rights[0].shape[0]
    own, over_x, over_y, low, high = outs
    half = depth // 2
    for spot in range(4):
        part = turned[spot]
        total = jnp.dot(part[:, :tokens], rights[0][...], preferred_element_type=jnp.float32)
        total += jnp.dot(
            part[:, tokens : 2 * tokens], rights[1][...], preferred_element_type=jnp.float32
        )
        total = total.astype(jnp.bfloat16).reshape(depth, rows, -1)
        if spot < 3:
            outs[spot][...] = total
        else:
            low[...] = total[:half]
            high[...] = total[half:]


def tiled_kernel(depth, rows, place, left, left_far, right, right_far, *refs):
    outs, turned = refs[:5], refs[5]

    @pl.when(pl.program_id(0) == 0)
    def _():
        turn(depth, rows, place, (left, left_far), turned)

    spread(depth, rows, turned, (right, right_far), outs)


def group_kernel(depth, rows, count, place, *refs):
    inputs, outs, turned = refs[: 4 * count], refs[4 * count : 4 * count + 5], refs[-1]
    for m in range(count):
        left, left_far, right, right_far = inputs[4 * m : 4 * m + 4]
        turn(depth, rows, place, (left, left_far), turned)
        spread(depth, rows, turned, (right, right_far), [out.at[:, m] for out in outs])


def piece_counts(grid):
    return (grid.depth, grid.depth, grid.depth, grid.depth // 2, grid.depth // 2)


def tiled_terms(grid, place, left, left_far, right, right_far, tile):
    tokens, features = left.shape
    width = right.shape[1]
    rows = features // grid.count
    left_row = 0
    if left_far.shape[0] != tokens:
        left_row = 4
    return pl.pallas_call(
        functools.partial(tiled_kernel, grid.depth, rows),
        grid=(width // tile,),
        out_shape=[jax.ShapeDtypeStruct((n, rows, width), jnp.bfloat16) for n in piece_counts(grid)],
        in_specs=[
            pl.BlockSpec(memory_space=pltpu.SMEM),
            pl.BlockSpec((tokens, features), lambda j: (0, 0)),
            pl.BlockSpec((tokens, features), lambda j: (left_row, 0)),
        ]
        + [pl.BlockSpec((tokens, tile), lambda j: (0, j))] * 2,
        out_specs=[pl.BlockSpec((n, rows, tile), lambda j: (0, 0, j)) for n in piece_counts(grid)],
        scratch_shapes=[pltpu.VMEM((4, grid.depth * rows, 2 * tokens), jnp.bfloat16)],
        compiler_params=pltpu.CompilerParams(vmem_limit_bytes=40 * 2**20),
        cost_estimate=pl.CostEstimate(flops=1, bytes_accessed=1, transcendentals=0),
        name="terms",
    )(place, left, left_far, right, right_far)


def group_terms(grid, place, pairs):
    width = 1024
    rows = width // grid.count
    arrays, specs = [], []
    for tokens, left, right in pairs:
        for near, far, row in (left, right):
            arrays += [near, far]
            specs += [pl.BlockSpec((tokens, width), lambda i, row=row: (row, 0))] * 2
    most = max(tokens for tokens, _, _ in pairs)
    shapes = [(n, len(pairs), rows, width) for n in piece_counts(grid)]
    return pl.pallas_call(
        functools.partial(group_kernel, grid.depth, rows, len(pairs)),
        grid=(1,),
        out_shape=[jax.ShapeDtypeStruct(shape, jnp.bfloat16) for shape in shapes],
        in_specs=[pl.BlockSpec(memory_space=pltpu.SMEM)] + specs,
        out_specs=[pl.BlockSpec(shape, lambda i: (0, 0, 0, 0)) for shape in shapes],
        scratch_shapes=[pltpu.VMEM((4, grid.depth * rows, 2 * most), jnp.bfloat16)],
        compiler_params=pltpu.CompilerParams(vmem_limit_bytes=48 * 2**20),
        cost_estimate=pl.CostEstimate(flops=1, bytes_accessed=1, transcendentals=0),
        name="terms",
    )(place, *arrays)


def settle_corner(grid, pieces):
    low, high = pieces[3:]
    return grid.move(low, dy=1), grid.move(high, dx=1)


def settle_sides(grid, pieces, corner):
    half = grid.depth // 2
    over_x = pieces[1].at[:half].add(corner[0])
    over_y = pieces[2].at[half:].add(corner[1])
    return (over_x, over_y), (grid.move(over_x, dx=1), grid.move(over_y, dy=1))


def settle_pairs(grid, pieces, sides):
    half = grid.depth // 2
    near, distant = [
        (
            pieces[0][part].astype(jnp.float32)
            + sides[0][part].astype(jnp.float32)
            + sides[1][part].astype(jnp.float32)
        ).astype(jnp.bfloat16)
        for part in (slice(0, half), slice(half, None))
    ]
    return near, grid.move(distant, dz=2)


def settle_pair(grid, near, got):
    leaving = (near[1].astype(jnp.float32) + got[1].astype(jnp.float32)).astype(jnp.bfloat16)
    return leaving, grid.move(leaving, dz=1)


def settle_total(near, got, last):
    return near[0].astype(jnp.float32) + got[0].astype(jnp.float32) + last.astype(jnp.float32)


def sum_norms(grid, terms_of):
    held = terms_of.shape[1] // grid.count
    total = jnp.pad(terms_of, ((0, 8 - terms_of.shape[0]), (0, 0)))
    if not grid.fast:
        total = lax.psum(total, ALL)
    else:
        for step in (dict(dc=1), dict(dy=1), dict(dx=1), dict(dz=1), dict(dz=2)):
            total = total + grid.move(total, **step)
    return lax.dynamic_slice(total, (0, lax.axis_index(ALL) * held), (8, held))


def fetch(attention_rows, expand_rows, reduce_rows, norm_rows):
    gathered = (
        lax.all_gather(attention_rows, ("dp", "fsdp"), axis=1, tiled=True),
        lax.all_gather(expand_rows, ("dp", "fsdp"), axis=0, tiled=True),
        lax.all_gather(reduce_rows, ("dp", "fsdp"), axis=0, tiled=True),
        lax.all_gather(norm_rows, ("dp", "fsdp"), axis=1, tiled=True),
    )
    return gathered


def settle(attention_terms, expand_terms, reduce_terms, norm_terms):
    owned = (
        lax.psum_scatter(attention_terms, ("dp", "fsdp"), scatter_dimension=1, tiled=True),
        lax.psum_scatter(expand_terms, ("dp", "fsdp"), scatter_dimension=0, tiled=True),
        lax.psum_scatter(reduce_terms, ("dp", "fsdp"), scatter_dimension=0, tiled=True),
        lax.psum_scatter(norm_terms, ("dp", "fsdp"), scatter_dimension=1, tiled=True),
    )
    return owned


def matmul(left, right):
    return jnp.dot(left, right, preferred_element_type=jnp.float32)


def across(left, right):
    return jnp.einsum("ti,tj->ij", left, right, preferred_element_type=jnp.float32)


def against(left, right):
    return jnp.einsum("ti,ji->tj", left, right, preferred_element_type=jnp.float32)


def gelu_tanh(values):
    return jax.nn.gelu(values, approximate=True)


def normalize(summed, gain, shift):
    center = jnp.mean(summed, axis=-1, keepdims=True)
    centred = summed - center
    inverse = lax.rsqrt(jnp.mean(centred * centred, axis=-1, keepdims=True) + EPSILON)
    scaled = centred * inverse
    return (scaled * gain + shift, scaled, inverse)


def normalize_back(incoming, scaled, inverse, gain):
    spread = incoming * gain
    d_summed = inverse * (
        spread
        - jnp.mean(spread, axis=-1, keepdims=True)
        - scaled * jnp.mean(spread * scaled, axis=-1, keepdims=True)
    )
    return (d_summed, jnp.sum(incoming * scaled, axis=0), jnp.sum(incoming, axis=0))


def split_heads(matrix):
    return matrix.reshape(matrix.shape[0], HEADS, HEAD_DIM)


def scores_of(query_rows, key_rows, allowed):
    raw = jnp.einsum(
        "qhd,khd->hqk",
        split_heads(query_rows),
        split_heads(key_rows),
        preferred_element_type=jnp.float32,
    ) * HEAD_DIM ** (-0.5)
    return jnp.where(allowed[None], raw, NEGATIVE)


def attend_forward(query_rows, key_rows, value_rows, allowed):
    scores = scores_of(query_rows, key_rows, allowed)
    highest = jnp.max(scores, axis=-1, keepdims=True)
    weights = jnp.exp(scores - highest)
    totals = jnp.sum(weights, axis=-1, keepdims=True)
    chances = (weights / totals).astype(jnp.bfloat16)
    context = jnp.einsum(
        "hqk,khd->qhd", chances, split_heads(value_rows), preferred_element_type=jnp.float32
    )
    return (
        context.reshape(query_rows.shape[0], HEADS * HEAD_DIM).astype(jnp.bfloat16),
        highest + jnp.log(totals),
    )


def attend_back(query_rows, key_rows, value_rows, allowed, logsum, d_context):
    query_heads = split_heads(query_rows)
    key_heads = split_heads(key_rows)
    d_heads = split_heads(d_context)
    chances = jnp.exp(scores_of(query_rows, key_rows, allowed) - logsum)
    d_chances = jnp.einsum(
        "qhd,khd->hqk", d_heads, split_heads(value_rows), preferred_element_type=jnp.float32
    )
    d_value = jnp.einsum(
        "hqk,qhd->khd", chances.astype(jnp.bfloat16), d_heads, preferred_element_type=jnp.float32
    )
    centre = jnp.sum(d_chances * chances, axis=-1, keepdims=True)
    d_scores = (chances * (d_chances - centre)).astype(jnp.bfloat16)
    d_query = jnp.einsum(
        "hqk,khd->qhd", d_scores, key_heads, preferred_element_type=jnp.float32
    ) * HEAD_DIM ** (-0.5)
    d_key = jnp.einsum(
        "hqk,qhd->khd", d_scores, query_heads, preferred_element_type=jnp.float32
    ) * HEAD_DIM ** (-0.5)
    query_count = query_rows.shape[0]
    key_count = key_rows.shape[0]
    return (
        d_query.reshape(query_count, HEADS * HEAD_DIM).astype(jnp.bfloat16),
        d_key.reshape(key_count, HEADS * HEAD_DIM).astype(jnp.bfloat16),
        d_value.reshape(key_count, HEADS * HEAD_DIM).astype(jnp.bfloat16),
    )


def plain_device(
    tokens,
    memory,
    target_segments,
    source_segments,
    self_query,
    self_key,
    self_value,
    self_output,
    cross_query,
    cross_key,
    cross_value,
    cross_output,
    expand_weight,
    reduce_weight,
    self_gain,
    self_shift,
    cross_gain,
    cross_shift,
    final_gain,
    final_shift,
    output_grad,
):
    attention_rows = jnp.stack(
        [
            self_query,
            self_key,
            self_value,
            self_output,
            cross_query,
            cross_key,
            cross_value,
            cross_output,
        ]
    )
    norm_rows = jnp.stack([self_gain, self_shift, cross_gain, cross_shift, final_gain, final_shift])
    matrices, expand_full, reduce_full, norm_full = fetch(
        attention_rows, expand_weight, reduce_weight, norm_rows
    )
    gains = norm_full.astype(jnp.float32)
    target_ids = target_segments[0]
    source_ids = source_segments[0]
    positions = lax.iota(jnp.int32, tokens.shape[0])
    causal = (target_ids[:, None] == target_ids[None, :]) & (
        positions[None, :] <= positions[:, None]
    )
    crossing = target_ids[:, None] == source_ids[None, :]
    query_one = matmul(tokens, matrices[0]).astype(jnp.bfloat16)
    key_one = matmul(tokens, matrices[1]).astype(jnp.bfloat16)
    value_one = matmul(tokens, matrices[2]).astype(jnp.bfloat16)
    context_one, logsum_one = attend_forward(query_one, key_one, value_one, causal)
    branch_one = matmul(context_one, matrices[3])
    first, first_scaled, first_inverse = normalize(
        RESIDUAL_SCALE * tokens.astype(jnp.float32) + branch_one, gains[0], gains[1]
    )
    first_low = first.astype(jnp.bfloat16)
    query_two = matmul(first_low, matrices[4]).astype(jnp.bfloat16)
    key_two = matmul(memory, matrices[5]).astype(jnp.bfloat16)
    value_two = matmul(memory, matrices[6]).astype(jnp.bfloat16)
    context_two, logsum_two = attend_forward(query_two, key_two, value_two, crossing)
    branch_two = matmul(context_two, matrices[7])
    second, second_scaled, second_inverse = normalize(
        RESIDUAL_SCALE * first + branch_two, gains[2], gains[3]
    )
    second_low = second.astype(jnp.bfloat16)
    inner = matmul(second_low, expand_full)
    active = gelu_tanh(inner).astype(jnp.bfloat16)
    branch_three = matmul(active, reduce_full)
    final, final_scaled, final_inverse = normalize(
        RESIDUAL_SCALE * second + branch_three, gains[4], gains[5]
    )
    output = final.astype(jnp.bfloat16)
    matrices, expand_full, reduce_full, norm_full = fetch(
        attention_rows, expand_weight, reduce_weight, norm_rows
    )
    gains = norm_full.astype(jnp.float32)
    d_sum_three, final_gain_term, final_shift_term = normalize_back(
        output_grad.astype(jnp.float32), final_scaled, final_inverse, gains[4]
    )
    d_branch_three = d_sum_three.astype(jnp.bfloat16)
    reduce_term = across(active, d_branch_three)
    d_active = against(d_branch_three, reduce_full)
    d_inner = jax.vjp(gelu_tanh, inner)[1](d_active)[0].astype(jnp.bfloat16)
    expand_term = across(second_low, d_inner)
    d_second = RESIDUAL_SCALE * d_sum_three + against(d_inner, expand_full)
    d_sum_two, cross_gain_term, cross_shift_term = normalize_back(
        d_second, second_scaled, second_inverse, gains[2]
    )
    d_branch_two = d_sum_two.astype(jnp.bfloat16)
    cross_output_term = across(context_two, d_branch_two)
    d_context_two = against(d_branch_two, matrices[7]).astype(jnp.bfloat16)
    d_query_two, d_key_two, d_value_two = attend_back(
        query_two, key_two, value_two, crossing, logsum_two, d_context_two
    )
    cross_query_term = across(first_low, d_query_two)
    cross_key_term = across(memory, d_key_two)
    cross_value_term = across(memory, d_value_two)
    memory_grad = against(d_key_two, matrices[5]) + against(d_value_two, matrices[6])
    d_first = RESIDUAL_SCALE * d_sum_two + against(d_query_two, matrices[4])
    d_sum_one, self_gain_term, self_shift_term = normalize_back(
        d_first, first_scaled, first_inverse, gains[0]
    )
    d_branch_one = d_sum_one.astype(jnp.bfloat16)
    self_output_term = across(context_one, d_branch_one)
    d_context_one = against(d_branch_one, matrices[3]).astype(jnp.bfloat16)
    d_query_one, d_key_one, d_value_one = attend_back(
        query_one, key_one, value_one, causal, logsum_one, d_context_one
    )
    self_query_term = across(tokens, d_query_one)
    self_key_term = across(tokens, d_key_one)
    self_value_term = across(tokens, d_value_one)
    tokens_grad = (
        RESIDUAL_SCALE * d_sum_one
        + against(d_query_one, matrices[0])
        + against(d_key_one, matrices[1])
        + against(d_value_one, matrices[2])
    )
    attention_terms = jnp.stack(
        [
            self_query_term,
            self_key_term,
            self_value_term,
            self_output_term,
            cross_query_term,
            cross_key_term,
            cross_value_term,
            cross_output_term,
        ]
    )
    norm_terms = jnp.stack(
        [
            self_gain_term,
            self_shift_term,
            cross_gain_term,
            cross_shift_term,
            final_gain_term,
            final_shift_term,
        ]
    )
    attention_owned, expand_owned, reduce_owned, norm_owned = settle(
        attention_terms, expand_term, reduce_term, norm_terms
    )
    return (
        output,
        tokens_grad,
        memory_grad,
        attention_owned[0],
        attention_owned[1],
        attention_owned[2],
        attention_owned[3],
        attention_owned[4],
        attention_owned[5],
        attention_owned[6],
        attention_owned[7],
        expand_owned,
        reduce_owned,
        norm_owned[0],
        norm_owned[1],
        norm_owned[2],
        norm_owned[3],
        norm_owned[4],
        norm_owned[5],
    )


def per_device(
    grid,
    tokens,
    memory,
    target_segments,
    source_segments,
    self_query,
    self_key,
    self_value,
    self_output,
    cross_query,
    cross_key,
    cross_value,
    cross_output,
    expand_weight,
    reduce_weight,
    self_gain,
    self_shift,
    cross_gain,
    cross_shift,
    final_gain,
    final_shift,
    output_grad,
):
    if not grid.fast:
        return plain_device(
            tokens,
            memory,
            target_segments,
            source_segments,
            self_query,
            self_key,
            self_value,
            self_output,
            cross_query,
            cross_key,
            cross_value,
            cross_output,
            expand_weight,
            reduce_weight,
            self_gain,
            self_shift,
            cross_gain,
            cross_shift,
            final_gain,
            final_shift,
            output_grad,
        )
    place = grid.place()
    held_rows = self_gain.shape[0]
    norm_rows = jnp.stack([self_gain, self_shift, cross_gain, cross_shift, final_gain, final_shift])
    extra = jnp.zeros((16, held_rows * grid.count), jnp.bfloat16)
    extra = lax.dynamic_update_slice(extra, norm_rows, (0, lax.axis_index(ALL) * held_rows))
    extra = extra.reshape(4, 32, 128)
    first_rows = jnp.concatenate([jnp.stack([self_query, self_key, self_value, self_output]), extra], axis=-1)
    second_rows = jnp.stack([cross_query, cross_key, cross_value, cross_output])
    target_column, target_row = target_segments.reshape(-1, 1), target_segments
    source_row = source_segments

    first_own = gather_direct(grid, first_rows)
    second_pair = gather_pair(grid, second_rows)
    first_own, second_pair, expand_rows = after((first_own, second_pair, expand_weight))
    first_sides = gather_sides(grid, first_own)
    second_own = gather_pairs(grid, second_pair)
    expand_pair = gather_pair(grid, expand_rows)
    first_sides, second_own, expand_pair, reduce_rows = after(
        (first_sides, second_own, expand_pair, reduce_weight)
    )
    first_ends = gather_corner(grid, first_own, first_sides)
    second_sides = gather_sides(grid, second_own)
    expand_own = gather_pairs(grid, expand_pair)
    first_corner = gather_last(grid, *first_ends[:2])
    first_pieces = (first_own, *first_sides, first_ends[2], *first_corner)
    second_sides, expand_own, reduce_rows, first_pieces = after(
        (second_sides, expand_own, reduce_rows, first_pieces)
    )
    second_ends = gather_corner(grid, second_own, second_sides)
    expand_sides = gather_sides(grid, expand_own)
    reduce_pair = gather_pair(grid, reduce_rows)
    first_out = self_forward(grid, place, tokens, target_column, target_row, first_pieces)
    first_out, second_ends, reduce_pair = after((first_out, second_ends, reduce_pair))
    first_full, gains, query_one, key_one, value_one, context_one, logsum_one = first_out[:7]
    first, first_low, first_scaled, first_inverse = first_out[7:]
    reduce_own = gather_pairs(grid, reduce_pair)
    second_corner = gather_last(grid, *second_ends[:2])
    second_pieces = (second_own, *second_sides, second_ends[2], *second_corner)
    expand_sides, reduce_own, second_pieces = after((expand_sides, reduce_own, second_pieces))
    expand_ends = gather_corner(grid, expand_own, expand_sides)
    reduce_sides = gather_sides(grid, reduce_own)
    second_out = cross_forward(
        grid, place, first, first_low, memory, gains, target_column, source_row, second_pieces
    )
    second_out, expand_ends = after((second_out, expand_ends))
    second_full, query_two, key_two, value_two, context_two, logsum_two = second_out[:6]
    second, second_low, second_scaled, second_inverse = second_out[6:]
    held = jnp.concatenate([tokens, context_one, first_low, context_two, second_low, memory])
    held_far = grid.move(held, dc=1)
    expand_corner = gather_last(grid, *expand_ends[:2])
    expand_pieces = (expand_own, *expand_sides, expand_ends[2], *expand_corner)
    reduce_sides, expand_pieces = after((reduce_sides, expand_pieces))
    reduce_ends = gather_corner(grid, reduce_own, reduce_sides)
    expand_full, active, slope = expand_forward(grid, place, second_low, expand_pieces)
    active, reduce_ends, held_far = after((active, reduce_ends, held_far))
    active_far = grid.move(active, dc=1)
    reduce_corner = gather_last(grid, *reduce_ends[:2])
    reduce_pieces = (reduce_own, *reduce_sides, reduce_ends[2], *reduce_corner)
    output, d_sum_three, d_branch_three, d_inner, final_terms = reduce_both(
        grid, place, active, slope, second, gains, output_grad, reduce_pieces
    )
    d_branch_three_far = grid.move(d_branch_three, dc=1)
    d_inner_far = grid.move(d_inner, dc=1)
    d_sum_two, d_branch_two, d_context_two, cross_terms_of_norm = expand_back(
        d_inner, expand_full, d_sum_three, second_scaled, second_inverse, gains, second_full
    )
    reduce_terms = tiled_terms(
        grid, place, active, active_far, after(d_branch_three, d_branch_two), d_branch_three_far, 512
    )
    reduce_corner = settle_corner(grid, reduce_terms)
    expand_terms = tiled_terms(
        grid, place, second_low, held_far, after(d_inner, *reduce_terms), d_inner_far, 1024
    )
    expand_corner = settle_corner(grid, expand_terms)
    reduce_mine, reduce_sides = settle_sides(grid, after(reduce_terms, *expand_terms), reduce_corner)
    cross_out = cross_back(
        query_two, key_two, value_two, logsum_two, after(d_context_two, *reduce_mine), target_column,
        source_row, d_sum_two, first_scaled, first_inverse, gains, second_full, first_full,
    )
    d_query_two, d_key_two, d_value_two, d_sum_one, d_branch_one, d_context_one, self_terms_of_norm = cross_out
    back = jnp.concatenate([d_branch_two, d_query_two, d_branch_one, d_key_two, d_value_two])
    back_far = grid.move(back, dc=1)
    expand_mine, expand_sides = settle_sides(grid, after(expand_terms, back), expand_corner)
    norm_owned = sum_norms(grid, jnp.concatenate([self_terms_of_norm, cross_terms_of_norm, final_terms]))
    back = after(back, *expand_mine)
    pairs = [
        (256, (held, held_far, 1), (back, back_far, 2)),
        (256, (held, held_far, 2), (back, back_far, 1)),
        (128, (held, held_far, 10), (back, back_far, 6)),
        (128, (held, held_far, 10), (back, back_far, 7)),
        (256, (held, held_far, 3), (back, back_far, 0)),
    ]
    cross_terms = group_terms(grid, place, pairs)
    cross_corner = settle_corner(grid, cross_terms)
    back_one = self_back(
        query_one, key_one, value_one, logsum_one, after(d_context_one, *cross_terms), target_column, target_row
    )
    back_one_far = grid.move(back_one, dc=1)
    reduce_near, reduce_got = settle_pairs(grid, after(reduce_terms, back_one), reduce_sides)
    cross_mine, cross_sides = settle_sides(grid, after(cross_terms, reduce_near), cross_corner)
    tokens_grad, memory_grad = inputs_back(
        after(back_one, *cross_mine), d_key_two, d_value_two, d_sum_one, first_full, second_full
    )
    expand_near, expand_got = settle_pairs(grid, after(expand_terms, tokens_grad), expand_sides)
    reduce_leaving, reduce_last = settle_pair(grid, after(reduce_near, expand_near), reduce_got)
    back_one = after(back_one, reduce_leaving)
    pairs = [(256, (held, held_far, 0), (back_one, back_one_far, i)) for i in range(3)]
    self_terms = group_terms(grid, place, pairs)
    self_corner = settle_corner(grid, self_terms)
    expand_leaving, expand_last = settle_pair(grid, after(expand_near, *self_terms), expand_got)
    cross_near, cross_got = settle_pairs(grid, after(cross_terms, expand_leaving), cross_sides)
    self_mine, self_sides = settle_sides(grid, after(self_terms, cross_near), self_corner)
    cross_leaving, cross_last = settle_pair(grid, after(cross_near, *self_mine), cross_got)
    self_near, self_got = settle_pairs(grid, after(self_terms, cross_leaving), self_sides)
    self_leaving, self_last = settle_pair(grid, self_near, self_got)
    reduce_term = settle_total(reduce_near, reduce_got, reduce_last)
    expand_term = settle_total(expand_near, expand_got, expand_last)
    cross_owned = settle_total(cross_near, cross_got, cross_last)
    self_owned = settle_total(self_near, self_got, self_last)
    return (
        output,
        tokens_grad,
        memory_grad,
        *[self_owned[i] for i in range(3)],
        *[cross_owned[i] for i in range(5)],
        expand_term,
        reduce_term,
        *[norm_owned[i] for i in range(6)],
    )


def solution(mesh):
    return jax.shard_map(
        functools.partial(per_device, Grid(mesh)),
        mesh=mesh,
        in_specs=(
            P(("dp", "fsdp"), None),
            P(("dp", "fsdp"), None),
            P(("dp", "fsdp"), None),
            P(("dp", "fsdp"), None),
            P(("dp", "fsdp"), None),
            P(("dp", "fsdp"), None),
            P(("dp", "fsdp"), None),
            P(("dp", "fsdp"), None),
            P(("dp", "fsdp"), None),
            P(("dp", "fsdp"), None),
            P(("dp", "fsdp"), None),
            P(("dp", "fsdp"), None),
            P(("dp", "fsdp"), None),
            P(("dp", "fsdp"), None),
            P(("dp", "fsdp")),
            P(("dp", "fsdp")),
            P(("dp", "fsdp")),
            P(("dp", "fsdp")),
            P(("dp", "fsdp")),
            P(("dp", "fsdp")),
            P(("dp", "fsdp"), None),
        ),
        out_specs=(
            P(("dp", "fsdp"), None),
            P(("dp", "fsdp"), None),
            P(("dp", "fsdp"), None),
            P(("dp", "fsdp"), None),
            P(("dp", "fsdp"), None),
            P(("dp", "fsdp"), None),
            P(("dp", "fsdp"), None),
            P(("dp", "fsdp"), None),
            P(("dp", "fsdp"), None),
            P(("dp", "fsdp"), None),
            P(("dp", "fsdp"), None),
            P(("dp", "fsdp"), None),
            P(("dp", "fsdp"), None),
            P(("dp", "fsdp")),
            P(("dp", "fsdp")),
            P(("dp", "fsdp")),
            P(("dp", "fsdp")),
            P(("dp", "fsdp")),
            P(("dp", "fsdp")),
        ),
        check_vma=False,
    )
```

```python
import functools

import jax
import jax.numpy as jnp
from jax import lax
from jax.experimental import pallas as pl
from jax.experimental.pallas import tpu as pltpu
from jax.sharding import PartitionSpec as P

HEADS = 16
HEAD_DIM = 64


RESIDUAL_SCALE = 300.0**0.25
EPSILON = 1e-05
NEGATIVE = -1e30
ALL = ("dp", "fsdp")


class Grid:
    def __init__(self, mesh):
        self.depth = mesh.shape["dp"] // 2
        self.count = mesh.size
        self.fast = mesh.shape["fsdp"] == 4 and mesh.shape["dp"] == 8
        self.axes = ("z", "core", "y", "x") if self.fast else ALL
        self.mesh = mesh
        if self.fast:
            self.mesh = jax.sharding.Mesh(mesh.devices.reshape(4, 2, 2, 2), self.axes)

    def place(self):
        return jnp.stack([lax.axis_index(axis) for axis in self.axes]).astype(jnp.int32)

    def index(self):
        return lax.axis_index(self.axes)

    def move(self, value, dz=0, dc=0, dy=0, dx=0):
        offset = ((dz * 2 + dc) * 2 + dy) * 2 + dx
        return lax.ppermute(value, self.axes, [(index ^ offset, index) for index in range(self.count)])

    def cores(self, twice):
        return lax.all_to_all(twice, "core", 0, 0, tiled=True)


def after(value, *others):
    return lax.optimization_barrier((value,) + others)[0]


def gather_direct(grid, shard):
    return jnp.stack([shard] + [grid.move(shard, dz=k) for k in range(1, grid.depth)])


def gather_pair(grid, shard):
    return jnp.stack([shard, grid.move(shard, dz=1)])


def gather_pairs(grid, pair):
    return jnp.concatenate([pair, grid.move(pair, dz=2)])


def gather_sides(grid, own):
    return grid.move(own, dx=1), grid.move(own, dy=1)


def gather_corner(grid, own, sides):
    half = grid.depth // 2
    low = grid.move(sides[0][:half], dy=1)
    high = grid.move(sides[1][half:], dx=1)
    far = grid.move(jnp.concatenate([own, *sides]), dc=1)
    return low, high, far


def gather_last(grid, low, high):
    corner = jnp.concatenate([low, high])
    return corner, grid.move(corner, dc=1)


def wide_dot(left, right):
    return jnp.dot(left, right, preferred_element_type=jnp.float32)


def dot_rows(left, right):
    return lax.dot_general(left, right, (((1,), (1,)), ((), ())), preferred_element_type=jnp.float32)


def dot_columns(left, right):
    return lax.dot_general(left, right, (((0,), (0,)), ((), ())), preferred_element_type=jnp.float32)


def whole_call(body, name, inputs, shapes, scratch=(), limit=56):
    arrays, specs = [], []
    for item in inputs:
        if not isinstance(item, tuple):
            item = (item, item.shape, (0,) * item.ndim)
        arrays.append(item[0])
        if len(item) == 2:
            specs.append(pl.BlockSpec(memory_space=item[1]))
        else:
            specs.append(pl.BlockSpec(item[1], lambda i, index=item[2]: index))
    outs, out_specs = [], []
    for item in shapes:
        outs.append(jax.ShapeDtypeStruct(item[0], item[1]))
        if len(item) == 3:
            out_specs.append(pl.BlockSpec(memory_space=item[2]))
        else:
            out_specs.append(pl.BlockSpec(item[0], lambda i, rank=len(item[0]): (0,) * rank))
    return pl.pallas_call(
        body,
        grid=(1,),
        out_shape=outs,
        in_specs=specs,
        out_specs=out_specs,
        scratch_shapes=list(scratch),
        compiler_params=pltpu.CompilerParams(vmem_limit_bytes=limit * 2**20),
        cost_estimate=pl.CostEstimate(flops=1, bytes_accessed=1, transcendentals=0),
        name=name,
    )(*arrays)


def arrivals_of(depth, rows, place, pieces, held, sems, held_norms=None, these=range(8)):
    own, over_x, over_y, far = pieces[:4]
    corner, corner_far = pieces[4:] if len(pieces) == 6 else (None, None)
    z, c, y, x = place[0], place[1], place[2], place[3]
    width = held.shape[-1]
    arrivals = []
    for k in range(depth):
        column = []
        for n in these:
            dc, dy, dx = n // 4, n // 2 % 2, n % 2
            if n % 4 == 3:
                piece, spot = (corner_far if dc else corner), k
            elif dc:
                piece, spot = far, (n % 4) * depth + k
            else:
                piece, spot = (own, over_x, over_y)[n], k
            owner = (((z ^ k) * 2 + (c ^ dc)) * 2 + (y ^ dy)) * 2 + (x ^ dx)
            target = held.at[..., pl.ds(pl.multiple_of(owner * rows, rows), rows), :]
            source = piece.at[spot]
            order = k * 8 + n
            if held_norms is None:
                column.append(pltpu.make_async_copy(source, target, sems.at[order]))
            else:
                column.append(pltpu.make_async_copy(source.at[..., :width], target, sems.at[order]))
                column.append(
                    pltpu.make_async_copy(
                        source.at[0:2, :, pl.ds(width, 128)],
                        held_norms.at[owner],
                        sems.at[8 * depth + order],
                    )
                )
        for copy in column:
            copy.start()
        arrivals.append(column)
    return arrivals


def pass_on(depth, rows, place, arrivals, held, whole, sems):
    leaving = []
    for k in range(depth):
        for copy in arrivals[k]:
            copy.wait()
        spot = pl.ds(pl.multiple_of((place[0] ^ k) * (8 * rows), 8 * rows), 8 * rows)
        leaving.append(pltpu.make_async_copy(held.at[..., spot, :], whole.at[..., spot, :], sems.at[k]))
        leaving[k].start()
    return leaving


def norm_rows_of(summed, gain, shift):
    center = jnp.mean(summed, axis=-1, keepdims=True)
    centred = summed - center
    inverse = lax.rsqrt(jnp.mean(centred * centred, axis=-1, keepdims=True) + EPSILON)
    scaled = centred * inverse
    return scaled * gain + shift, scaled, inverse


def norm_rows_back(incoming, scaled, inverse, gain):
    spread_out = incoming * gain
    d_summed = inverse * (
        spread_out
        - jnp.mean(spread_out, axis=-1, keepdims=True)
        - scaled * jnp.mean(spread_out * scaled, axis=-1, keepdims=True)
    )
    return d_summed, jnp.sum(incoming * scaled, axis=0, keepdims=True), jnp.sum(incoming, axis=0, keepdims=True)


def head_halves():
    lane = lax.broadcasted_iota(jnp.int32, (1, 2 * HEAD_DIM), 1)
    return [
        jnp.where(lane < HEAD_DIM, 1.0, 0.0).astype(jnp.bfloat16),
        jnp.where(lane < HEAD_DIM, 0.0, 1.0).astype(jnp.bfloat16),
    ]


def attend_heads(query, key, value, allowed, context, logsum):
    halves = head_halves()
    lane = lax.broadcasted_iota(jnp.int32, logsum.shape, 1)
    logsum[...] = jnp.zeros_like(logsum)

    def pair(p, carry):
        lanes = pl.ds(pl.multiple_of(p * 2 * HEAD_DIM, 2 * HEAD_DIM), 2 * HEAD_DIM)
        queries, keys, values = query[:, lanes], key[:, lanes], value[:, lanes]
        total = None
        for side, half in enumerate(halves):
            scores = dot_rows(queries * half, keys) * HEAD_DIM ** (-0.5)
            scores = jnp.where(allowed[...] > 0, scores, NEGATIVE)
            highest = jnp.max(scores, axis=-1, keepdims=True)
            weights = jnp.exp(scores - highest)
            totals = jnp.sum(weights, axis=-1, keepdims=True)
            chances = (weights * (1.0 / totals)).astype(jnp.bfloat16)
            part = wide_dot(chances, values * half)
            total = part if total is None else total + part
            logsum[...] = jnp.where(lane == 2 * p + side, highest + jnp.log(totals), logsum[...])
        context[:, lanes] = total.astype(jnp.bfloat16)
        return carry

    lax.fori_loop(0, HEADS // 2, pair, 0)


def attend_heads_back(query, key, value, allowed, logsum, d_context, d_query, d_key, d_value):
    halves = head_halves()
    lane = lax.broadcasted_iota(jnp.int32, logsum.shape, 1)
    scale = HEAD_DIM ** (-0.5)

    def pair(p, carry):
        lanes = pl.ds(pl.multiple_of(p * 2 * HEAD_DIM, 2 * HEAD_DIM), 2 * HEAD_DIM)
        queries, keys, values, d_outs = query[:, lanes], key[:, lanes], value[:, lanes], d_context[:, lanes]
        sums = [None, None, None]
        for side, half in enumerate(halves):
            own_sum = jnp.sum(jnp.where(lane == 2 * p + side, logsum[...], 0.0), axis=-1, keepdims=True)
            own_queries, own_outs = queries * half, d_outs * half
            scores = dot_rows(own_queries, keys) * scale
            scores = jnp.where(allowed[...] > 0, scores, NEGATIVE)
            chances = jnp.exp(scores - own_sum)
            d_chances = dot_rows(own_outs, values)
            centre = jnp.sum(d_chances * chances, axis=-1, keepdims=True)
            d_scores = (chances * (d_chances - centre)).astype(jnp.bfloat16)
            parts = (
                wide_dot(d_scores, keys * half),
                dot_columns(d_scores, own_queries),
                dot_columns(chances.astype(jnp.bfloat16), own_outs),
            )
            sums = [part if old is None else old + part for old, part in zip(sums, parts)]
        d_query[:, lanes] = (sums[0] * scale).astype(jnp.bfloat16)
        d_key[:, lanes] = (sums[1] * scale).astype(jnp.bfloat16)
        d_value[:, lanes] = sums[2].astype(jnp.bfloat16)
        return carry

    lax.fori_loop(0, HEADS // 2, pair, 0)


def self_allowed(ids_column, ids_row, allowed):
    rows, columns = allowed.shape
    later = lax.broadcasted_iota(jnp.int32, (rows, columns), 0) >= lax.broadcasted_iota(
        jnp.int32, (rows, columns), 1
    )
    same = ids_column[...] == ids_row[...]
    allowed[...] = jnp.where(later & same, 1.0, 0.0)


def cross_allowed(ids_column, ids_row, allowed):
    allowed[...] = jnp.where(ids_column[...] == ids_row[...], 1.0, 0.0)


def self_forward_kernel(depth, rows, place, tokens, ids_column, ids_row, *refs):
    pieces, refs = refs[:6], refs[6:]
    whole, gains, query, key, value, context, logsum, first, first_low, scaled, inverse = refs[:11]
    held, held_norms, allowed, in_sems, out_sems = refs[11:]
    arrivals = arrivals_of(depth, rows, place, pieces, held, in_sems, held_norms)
    self_allowed(ids_column, ids_row, allowed)
    leaving = pass_on(depth, rows, place, arrivals, held, whole, out_sems)
    packed = held_norms[0].astype(jnp.float32)
    for owner in range(1, 8 * depth):
        packed += held_norms[owner].astype(jnp.float32)
    gains[...] = jnp.zeros_like(gains)
    for n in range(6):
        for j in range(8):
            r = n * 8 + j
            gains[n : n + 1, j * 128 : (j + 1) * 128] = packed[r // rows, r % rows : r % rows + 1, :]
    for n, out in enumerate((query, key, value)):
        out[...] = wide_dot(tokens[...], held[n]).astype(jnp.bfloat16)
    attend_heads(query, key, value, allowed, context, logsum)
    branch = wide_dot(context[...], held[3])
    summed = RESIDUAL_SCALE * tokens[...].astype(jnp.float32) + branch
    first[...], scaled[...], inverse[...] = norm_rows_of(summed, gains[0:1, :], gains[1:2, :])
    first_low[...] = first[...].astype(jnp.bfloat16)
    for copy in leaving:
        copy.wait()


def self_forward(grid, place, tokens, ids_column, ids_row, pieces):
    count, width = tokens.shape
    rows = pieces[0].shape[2]
    low, full = jnp.bfloat16, jnp.float32
    shape = (count, width)
    return whole_call(
        functools.partial(self_forward_kernel, grid.depth, rows),
        "self_forward",
        [(place, pltpu.SMEM), tokens, ids_column, ids_row] + [(piece, pl.ANY) for piece in pieces],
        [((4, width, width), low, pl.ANY), ((8, width), full)]
        + [(shape, low)] * 4
        + [((count, 128), full), (shape, full), (shape, low), (shape, full), ((count, 1), full)],
        [
            pltpu.VMEM((4, width, width), low),
            pltpu.VMEM((grid.count, 2, rows, 128), low),
            pltpu.VMEM((count, count), full),
            pltpu.SemaphoreType.DMA((2 * grid.count,)),
            pltpu.SemaphoreType.DMA((grid.depth,)),
        ],
    )


def cross_forward_kernel(depth, rows, place, first, first_low, memory, gains, ids_column, ids_row, *refs):
    pieces, refs = refs[:6], refs[6:]
    whole, query, key, value, context, logsum, second, second_low, scaled, inverse = refs[:10]
    held, allowed, in_sems, out_sems = refs[10:]
    arrivals = arrivals_of(depth, rows, place, pieces, held, in_sems)
    cross_allowed(ids_column, ids_row, allowed)
    leaving = pass_on(depth, rows, place, arrivals, held, whole, out_sems)
    query[...] = wide_dot(first_low[...], held[0]).astype(jnp.bfloat16)
    key[...] = wide_dot(memory[...], held[1]).astype(jnp.bfloat16)
    value[...] = wide_dot(memory[...], held[2]).astype(jnp.bfloat16)
    attend_heads(query, key, value, allowed, context, logsum)
    summed = RESIDUAL_SCALE * first[...] + wide_dot(context[...], held[3])
    second[...], scaled[...], inverse[...] = norm_rows_of(summed, gains[2:3, :], gains[3:4, :])
    second_low[...] = second[...].astype(jnp.bfloat16)
    for copy in leaving:
        copy.wait()


def cross_forward(grid, place, first, first_low, memory, gains, ids_column, ids_row, pieces):
    count, width = first.shape
    others = memory.shape[0]
    rows = pieces[0].shape[2]
    low, full = jnp.bfloat16, jnp.float32
    shape, other_shape = (count, width), (others, width)
    return whole_call(
        functools.partial(cross_forward_kernel, grid.depth, rows),
        "cross_forward",
        [(place, pltpu.SMEM), first, first_low, memory, gains, ids_column, ids_row]
        + [(piece, pl.ANY) for piece in pieces],
        [((4, width, width), low, pl.ANY), (shape, low), (other_shape, low), (other_shape, low), (shape, low)]
        + [((count, 128), full), (shape, full), (shape, low), (shape, full), ((count, 1), full)],
        [
            pltpu.VMEM((4, width, width), low),
            pltpu.VMEM((count, others), full),
            pltpu.SemaphoreType.DMA((grid.count,)),
            pltpu.SemaphoreType.DMA((grid.depth,)),
        ],
    )


TANH_SCALE = 0.7978845608028654
TANH_CUBE = 0.044715


def expand_forward_kernel(depth, rows, place, second_low, *refs):
    pieces, refs = refs[:6], refs[6:]
    whole, active, slope, held, in_sems, out_sems = refs
    arrivals = arrivals_of(depth, rows, place, pieces, held, in_sems)
    leaving = pass_on(depth, rows, place, arrivals, held, whole, out_sems)
    left = second_low[...]

    def tile(j, carry):
        lanes = pl.ds(pl.multiple_of(j * 512, 512), 512)
        inner = wide_dot(left, held[:, lanes])
        square = inner * inner
        bend = jnp.tanh(TANH_SCALE * (inner * (1.0 + TANH_CUBE * square)))
        half = 0.5 + 0.5 * bend
        active[:, lanes] = (inner * half).astype(jnp.bfloat16)
        slope[:, lanes] = half + (0.5 * TANH_SCALE) * inner * (1.0 - bend * bend) * (
            1.0 + (3.0 * TANH_CUBE) * square
        )
        return carry

    lax.fori_loop(0, held.shape[1] // 512, tile, 0)
    for copy in leaving:
        copy.wait()


def expand_forward(grid, place, second_low, pieces):
    count, width = second_low.shape
    rows, hidden = pieces[0].shape[1:]
    low = jnp.bfloat16
    return whole_call(
        functools.partial(expand_forward_kernel, grid.depth, rows),
        "expand_forward",
        [(place, pltpu.SMEM), second_low] + [(piece, pl.ANY) for piece in pieces],
        [((width, hidden), low, pl.ANY), ((count, hidden), low), ((count, hidden), jnp.float32)],
        [
            pltpu.VMEM((width, hidden), low),
            pltpu.SemaphoreType.DMA((grid.count,)),
            pltpu.SemaphoreType.DMA((grid.depth,)),
        ],
    )


def reduce_first_kernel(depth, rows, place, active, own, over_x, over_y, far, partial, held, sems):
    z, c, y, x = place[0], place[1], place[2], place[3]
    pieces = (own, over_x, over_y, far)
    arrivals = arrivals_of(depth, rows, place, pieces, held, sems, these=(0, 1, 2, 4, 5, 6))
    for there in range(depth):
        for core in range(2):
            owner = ((there * 2 + core) * 2 + (1 - y)) * 2 + (1 - x)
            held[pl.ds(pl.multiple_of(owner * rows, rows), rows), :] = jnp.zeros((rows, held.shape[1]), held.dtype)
    for column in arrivals:
        for copy in column:
            copy.wait()
    partial[...] = wide_dot(active[...], held[...])


def reduce_first(grid, place, active, pieces):
    count, hidden = active.shape
    rows, width = pieces[0].shape[1:]
    return whole_call(
        functools.partial(reduce_first_kernel, grid.depth, rows),
        "reduce_first",
        [(place, pltpu.SMEM), active] + [(piece, pl.ANY) for piece in pieces],
        [((count, width), jnp.float32)],
        [pltpu.VMEM((hidden, width), jnp.bfloat16), pltpu.SemaphoreType.DMA((grid.count,))],
    )[0]


def reduce_last_kernel(depth, rows, place, active, partial, second, gains, output_grad, corner, corner_far, output, d_summed, d_branch, norm_terms):
    z, c, y, x = place[0], place[1], place[2], place[3]
    summed = RESIDUAL_SCALE * second[...] + partial[...]
    for k in range(depth):
        for dc, piece in enumerate((corner, corner_far)):
            owner = (((z ^ k) * 2 + (c ^ dc)) * 2 + (1 - y)) * 2 + (1 - x)
            summed += wide_dot(active[:, pl.ds(pl.multiple_of(owner * rows, rows), rows)], piece[k])
    final, scaled, inverse = norm_rows_of(summed, gains[4:5, :], gains[5:6, :])
    output[...] = final.astype(jnp.bfloat16)
    d_sum, norm_terms[0:1, :], norm_terms[1:2, :] = norm_rows_back(
        output_grad[...].astype(jnp.float32), scaled, inverse, gains[4:5, :]
    )
    d_summed[...] = d_sum
    d_branch[...] = d_sum.astype(jnp.bfloat16)


def reduce_finish(grid, place, active, partial, second, gains, output_grad, corner, corner_far):
    shape = second.shape
    low, full = jnp.bfloat16, jnp.float32
    return whole_call(
        functools.partial(reduce_last_kernel, grid.depth, corner.shape[1]),
        "reduce_last",
        [(place, pltpu.SMEM), active, partial, second, gains, output_grad, corner, corner_far],
        [(shape, low), (shape, full), (shape, low), ((2, shape[1]), full)],
    )


def reduce_back_kernel(depth, rows, place, d_branch, slope, *refs):
    pieces, refs = refs[:6], refs[6:]
    d_inner, held, sems = refs
    for column in arrivals_of(depth, rows, place, pieces, held, sems):
        for copy in column:
            copy.wait()
    left = d_branch[...]

    def tile(j, carry):
        lanes = pl.ds(pl.multiple_of(j * 512, 512), 512)
        d_active = dot_rows(left, held[lanes, :])
        d_inner[:, lanes] = (d_active * slope[:, lanes]).astype(jnp.bfloat16)
        return carry

    lax.fori_loop(0, held.shape[0] // 512, tile, 0)


def reduce_back(grid, place, d_branch, slope, pieces):
    count, width = d_branch.shape
    hidden = slope.shape[1]
    return whole_call(
        functools.partial(reduce_back_kernel, grid.depth, pieces[0].shape[1]),
        "reduce_back",
        [(place, pltpu.SMEM), d_branch, slope] + [(piece, pl.ANY) for piece in pieces],
        [((count, hidden), jnp.bfloat16)],
        [pltpu.VMEM((hidden, width), jnp.bfloat16), pltpu.SemaphoreType.DMA((grid.count,))],
    )[0]


def expand_back_kernel(d_inner, expand, d_sum_three, scaled, inverse, gains, out_weight, d_summed, d_branch, d_context, norm_terms):
    d_second = RESIDUAL_SCALE * d_sum_three[...] + dot_rows(d_inner[...], expand[...])
    d_sum, norm_terms[0:1, :], norm_terms[1:2, :] = norm_rows_back(
        d_second, scaled[...], inverse[...], gains[2:3, :]
    )
    d_summed[...] = d_sum
    d_branch[...] = d_sum.astype(jnp.bfloat16)
    d_context[...] = dot_rows(d_branch[...], out_weight[0]).astype(jnp.bfloat16)


def expand_back(d_inner, expand, d_sum_three, scaled, inverse, gains, second_full):
    shape = d_sum_three.shape
    width = shape[1]
    low, full = jnp.bfloat16, jnp.float32
    return whole_call(
        expand_back_kernel,
        "expand_back",
        [d_inner, expand, d_sum_three, scaled, inverse, gains]
        + [(second_full, (1, width, width), (3, 0, 0))],
        [(shape, full), (shape, low), (shape, low), ((2, width), full)],
    )


def cross_back_kernel(
    query, key, value, logsum, d_context, ids_column, ids_row, d_branch_two, d_sum_two, scaled, inverse, gains,
    query_weight, out_weight, back, d_summed, d_context_one, norm_terms, allowed,
):
    count, others = query.shape[0], key.shape[0]
    cross_allowed(ids_column, ids_row, allowed)
    rows = back.at[0]
    d_query = rows.at[count : 2 * count]
    d_key = rows.at[3 * count : 3 * count + others]
    d_value = rows.at[3 * count + others : 3 * count + 2 * others]
    attend_heads_back(query, key, value, allowed, logsum, d_context, d_query, d_key, d_value)
    d_first = RESIDUAL_SCALE * d_sum_two[...] + dot_rows(d_query[...], query_weight[0])
    d_sum, norm_terms[0:1, :], norm_terms[1:2, :] = norm_rows_back(
        d_first, scaled[...], inverse[...], gains[0:1, :]
    )
    d_summed[...] = d_sum
    d_branch = d_sum.astype(jnp.bfloat16)
    rows[0:count, :] = d_branch_two[...]
    rows[2 * count : 3 * count, :] = d_branch
    back[1] = rows[...]
    d_context_one[...] = dot_rows(d_branch, out_weight[0]).astype(jnp.bfloat16)


def cross_back(query, key, value, logsum, d_context, ids_column, ids_row, d_branch_two, d_sum_two, scaled, inverse, gains, second_full, first_full):
    shape, other_shape = query.shape, key.shape
    width = shape[1]
    low, full = jnp.bfloat16, jnp.float32
    block = (1, width, width)
    return whole_call(
        cross_back_kernel,
        "cross_back",
        [query, key, value, logsum, d_context, ids_column, ids_row, d_branch_two, d_sum_two, scaled, inverse, gains]
        + [(second_full, block, (0, 0, 0)), (first_full, block, (3, 0, 0))],
        [((2, 3 * shape[0] + 2 * other_shape[0], width), low), (shape, full), (shape, low), ((2, width), full)],
        [pltpu.VMEM((shape[0], other_shape[0]), full)],
    )


def self_back_kernel(query, key, value, logsum, d_context, ids_column, ids_row, d_rows, allowed):
    self_allowed(ids_column, ids_row, allowed)
    count = query.shape[0]
    outs = [d_rows.at[n * count : (n + 1) * count] for n in range(3)]
    attend_heads_back(query, key, value, allowed, logsum, d_context, *outs)


def self_back(query, key, value, logsum, d_context, ids_column, ids_row):
    count, width = query.shape
    return whole_call(
        self_back_kernel,
        "self_back",
        [query, key, value, logsum, d_context, ids_column, ids_row],
        [((3 * count, width), jnp.bfloat16)],
        [pltpu.VMEM((count, count), jnp.float32)],
    )[0]


def inputs_back_kernel(d_rows, d_key, d_value, d_sum_one, w_query, w_key, w_value, w_key_two, w_value_two, tokens_grad, memory_grad):
    count = d_sum_one.shape[0]
    total = RESIDUAL_SCALE * d_sum_one[...]
    for n, weight in enumerate((w_query, w_key, w_value)):
        total += dot_rows(d_rows[n * count : (n + 1) * count, :], weight[0])
    tokens_grad[...] = total
    memory_grad[...] = dot_rows(d_key[0], w_key_two[0]) + dot_rows(d_value[0], w_value_two[0])


def inputs_back(d_rows, back, d_sum_one, first_full, second_full):
    count, width = d_sum_one.shape
    others = (back.shape[1] - 3 * count) // 2
    first_row = 3 * count // others
    block = (1, width, width)
    return whole_call(
        inputs_back_kernel,
        "inputs_back",
        [d_rows]
        + [(back, (1, others, width), (0, first_row + n, 0)) for n in (0, 1)]
        + [d_sum_one]
        + [(first_full, block, (n, 0, 0)) for n in range(3)]
        + [(second_full, block, (n, 0, 0)) for n in (1, 2)],
        [((count, width), jnp.float32), ((others, width), jnp.float32)],
    )


def turn(depth, rows, place, sources, turned, spots=range(4)):
    z, c, y, x = place[0], place[1], place[2], place[3]
    tokens = sources[0].shape[0]
    for k in range(depth):
        there = z ^ k
        columns = pl.ds(pl.multiple_of((there * 2 + c) * (4 * rows), 4 * rows), 4 * rows)
        for side, source in enumerate(sources):
            block = source[:, columns].T
            named = [block[n * rows : (n + 1) * rows] for n in range(4)]
            named = [jnp.where(x == 0, named[n], named[n ^ 1]) for n in range(4)]
            named = [jnp.where(y == 0, named[n], named[n ^ 2]) for n in range(4)]
            for at, spot in enumerate(spots):
                turned[at, k * rows : (k + 1) * rows, side * tokens : (side + 1) * tokens] = named[spot]


def spread(depth, rows, turned, rights, outs, spots=range(4)):
    tokens = rights[0].shape[0]
    half = depth // 2
    for at, spot in enumerate(spots):
        part = turned[at]
        total = jnp.dot(part[:, :tokens], rights[0][...], preferred_element_type=jnp.float32)
        total += jnp.dot(
            part[:, tokens : 2 * tokens], rights[1][...], preferred_element_type=jnp.float32
        )
        total = total.astype(jnp.bfloat16).reshape(depth, rows, -1)
        if spot < 3:
            outs[at][...] = total
        else:
            outs[at][...] = total[:half]
            outs[at + 1][...] = total[half:]


def tiled_kernel(depth, rows, spots, place, left, left_far, right, right_far, *refs):
    outs, turned = refs[:-1], refs[-1]

    @pl.when(pl.program_id(0) == 0)
    def _():
        turn(depth, rows, place, (left, left_far), turned, spots)

    spread(depth, rows, turned, (right, right_far), outs, spots)


def group_kernel(depth, rows, count, by_core, place, *refs):
    each = 3 if by_core else 4
    core = place[1]
    inputs, outs, turned = refs[: each * count], refs[each * count : each * count + 5], refs[-1]
    for m in range(count):
        left, left_far, *rights = inputs[each * m : each * m + each]
        if by_core:
            rights = (rights[0].at[core], rights[0].at[1 - core])
        turn(depth, rows, place, (left, left_far), turned)
        spread(depth, rows, turned, rights, [out.at[:, m] for out in outs])


def piece_counts(depth, spots=range(4)):
    counts = []
    for spot in spots:
        counts += [depth] if spot < 3 else [depth // 2, depth // 2]
    return counts


def tiled_terms(grid, place, left, left_far, right, right_far, tile, spots=range(4)):
    tokens, features = left.shape
    width = right.shape[1]
    rows = features // grid.count
    left_row = 4 if left_far.shape[0] != tokens else 0
    counts = piece_counts(grid.depth, spots)
    return pl.pallas_call(
        functools.partial(tiled_kernel, grid.depth, rows, spots),
        grid=(width // tile,),
        out_shape=[jax.ShapeDtypeStruct((n, rows, width), jnp.bfloat16) for n in counts],
        in_specs=[
            pl.BlockSpec(memory_space=pltpu.SMEM),
            pl.BlockSpec((tokens, features), lambda j: (0, 0)),
            pl.BlockSpec((tokens, features), lambda j: (left_row, 0)),
        ]
        + [pl.BlockSpec((tokens, tile), lambda j: (0, j))] * 2,
        out_specs=[pl.BlockSpec((n, rows, tile), lambda j: (0, 0, j)) for n in counts],
        scratch_shapes=[pltpu.VMEM((len(spots), grid.depth * rows, 2 * tokens), jnp.bfloat16)],
        compiler_params=pltpu.CompilerParams(vmem_limit_bytes=40 * 2**20),
        cost_estimate=pl.CostEstimate(flops=1, bytes_accessed=1, transcendentals=0),
        name="terms",
    )(place, left, left_far, right, right_far)


def group_terms(grid, place, held, held_far, right, right_far, pairs):
    by_core = right_far is None
    width = held.shape[1]
    rows = width // grid.count
    arrays, specs = [], []
    for tokens, left_row, right_row in pairs:
        arrays += [held, held_far, right]
        specs += [pl.BlockSpec((tokens, width), lambda i, row=left_row: (row, 0))] * 2
        if by_core:
            specs += [pl.BlockSpec((2, tokens, width), lambda i, row=right_row: (0, row, 0))]
        else:
            arrays += [right_far]
            specs += [pl.BlockSpec((tokens, width), lambda i, row=right_row: (row, 0))] * 2
    most = max(tokens for tokens, _, _ in pairs)
    shapes = [(n, len(pairs), rows, width) for n in piece_counts(grid.depth)]
    return pl.pallas_call(
        functools.partial(group_kernel, grid.depth, rows, len(pairs), by_core),
        grid=(1,),
        out_shape=[jax.ShapeDtypeStruct(shape, jnp.bfloat16) for shape in shapes],
        in_specs=[pl.BlockSpec(memory_space=pltpu.SMEM)] + specs,
        out_specs=[pl.BlockSpec(shape, lambda i: (0, 0, 0, 0)) for shape in shapes],
        scratch_shapes=[pltpu.VMEM((4, grid.depth * rows, 2 * most), jnp.bfloat16)],
        compiler_params=pltpu.CompilerParams(vmem_limit_bytes=48 * 2**20),
        cost_estimate=pl.CostEstimate(flops=1, bytes_accessed=1, transcendentals=0),
        name="terms",
    )(place, *arrays)


def corner_added(grid, pieces, low, high):
    half = grid.depth // 2
    return pieces[1].at[:half].add(low), pieces[2].at[half:].add(high)


def plane_sum(own, over_x, over_y):
    wide = jnp.float32
    return (own.astype(wide) + over_x.astype(wide) + over_y.astype(wide)).astype(jnp.bfloat16)


def plane_sums(grid, pieces, over_x, over_y):
    half = grid.depth // 2
    return [
        plane_sum(pieces[0][part], over_x[part], over_y[part]) for part in (slice(0, half), slice(half, None))
    ]


def pair_sum(near, got):
    return (near[1].astype(jnp.float32) + got[1].astype(jnp.float32)).astype(jnp.bfloat16)


def total_of(*terms_of):
    return sum([term.astype(jnp.float32) for term in terms_of[1:]], terms_of[0].astype(jnp.float32))


def fetch(attention_rows, expand_rows, reduce_rows, norm_rows):
    gathered = (
        lax.all_gather(attention_rows, ("dp", "fsdp"), axis=1, tiled=True),
        lax.all_gather(expand_rows, ("dp", "fsdp"), axis=0, tiled=True),
        lax.all_gather(reduce_rows, ("dp", "fsdp"), axis=0, tiled=True),
        lax.all_gather(norm_rows, ("dp", "fsdp"), axis=1, tiled=True),
    )
    return gathered


def settle(attention_terms, expand_terms, reduce_terms, norm_terms):
    owned = (
        lax.psum_scatter(attention_terms, ("dp", "fsdp"), scatter_dimension=1, tiled=True),
        lax.psum_scatter(expand_terms, ("dp", "fsdp"), scatter_dimension=0, tiled=True),
        lax.psum_scatter(reduce_terms, ("dp", "fsdp"), scatter_dimension=0, tiled=True),
        lax.psum_scatter(norm_terms, ("dp", "fsdp"), scatter_dimension=1, tiled=True),
    )
    return owned


def matmul(left, right):
    return jnp.dot(left, right, preferred_element_type=jnp.float32)


def across(left, right):
    return jnp.einsum("ti,tj->ij", left, right, preferred_element_type=jnp.float32)


def against(left, right):
    return jnp.einsum("ti,ji->tj", left, right, preferred_element_type=jnp.float32)


def gelu_tanh(values):
    return jax.nn.gelu(values, approximate=True)


def normalize(summed, gain, shift):
    center = jnp.mean(summed, axis=-1, keepdims=True)
    centred = summed - center
    inverse = lax.rsqrt(jnp.mean(centred * centred, axis=-1, keepdims=True) + EPSILON)
    scaled = centred * inverse
    return (scaled * gain + shift, scaled, inverse)


def normalize_back(incoming, scaled, inverse, gain):
    spread = incoming * gain
    d_summed = inverse * (
        spread
        - jnp.mean(spread, axis=-1, keepdims=True)
        - scaled * jnp.mean(spread * scaled, axis=-1, keepdims=True)
    )
    return (d_summed, jnp.sum(incoming * scaled, axis=0), jnp.sum(incoming, axis=0))


def split_heads(matrix):
    return matrix.reshape(matrix.shape[0], HEADS, HEAD_DIM)


def scores_of(query_rows, key_rows, allowed):
    raw = jnp.einsum(
        "qhd,khd->hqk",
        split_heads(query_rows),
        split_heads(key_rows),
        preferred_element_type=jnp.float32,
    ) * HEAD_DIM ** (-0.5)
    return jnp.where(allowed[None], raw, NEGATIVE)


def attend_forward(query_rows, key_rows, value_rows, allowed):
    scores = scores_of(query_rows, key_rows, allowed)
    highest = jnp.max(scores, axis=-1, keepdims=True)
    weights = jnp.exp(scores - highest)
    totals = jnp.sum(weights, axis=-1, keepdims=True)
    chances = (weights / totals).astype(jnp.bfloat16)
    context = jnp.einsum(
        "hqk,khd->qhd", chances, split_heads(value_rows), preferred_element_type=jnp.float32
    )
    return (
        context.reshape(query_rows.shape[0], HEADS * HEAD_DIM).astype(jnp.bfloat16),
        highest + jnp.log(totals),
    )


def attend_back(query_rows, key_rows, value_rows, allowed, logsum, d_context):
    query_heads = split_heads(query_rows)
    key_heads = split_heads(key_rows)
    d_heads = split_heads(d_context)
    chances = jnp.exp(scores_of(query_rows, key_rows, allowed) - logsum)
    d_chances = jnp.einsum(
        "qhd,khd->hqk", d_heads, split_heads(value_rows), preferred_element_type=jnp.float32
    )
    d_value = jnp.einsum(
        "hqk,qhd->khd", chances.astype(jnp.bfloat16), d_heads, preferred_element_type=jnp.float32
    )
    centre = jnp.sum(d_chances * chances, axis=-1, keepdims=True)
    d_scores = (chances * (d_chances - centre)).astype(jnp.bfloat16)
    d_query = jnp.einsum(
        "hqk,khd->qhd", d_scores, key_heads, preferred_element_type=jnp.float32
    ) * HEAD_DIM ** (-0.5)
    d_key = jnp.einsum(
        "hqk,qhd->khd", d_scores, query_heads, preferred_element_type=jnp.float32
    ) * HEAD_DIM ** (-0.5)
    query_count = query_rows.shape[0]
    key_count = key_rows.shape[0]
    return (
        d_query.reshape(query_count, HEADS * HEAD_DIM).astype(jnp.bfloat16),
        d_key.reshape(key_count, HEADS * HEAD_DIM).astype(jnp.bfloat16),
        d_value.reshape(key_count, HEADS * HEAD_DIM).astype(jnp.bfloat16),
    )


def plain_device(
    tokens,
    memory,
    target_segments,
    source_segments,
    self_query,
    self_key,
    self_value,
    self_output,
    cross_query,
    cross_key,
    cross_value,
    cross_output,
    expand_weight,
    reduce_weight,
    self_gain,
    self_shift,
    cross_gain,
    cross_shift,
    final_gain,
    final_shift,
    output_grad,
):
    attention_rows = jnp.stack(
        [
            self_query,
            self_key,
            self_value,
            self_output,
            cross_query,
            cross_key,
            cross_value,
            cross_output,
        ]
    )
    norm_rows = jnp.stack([self_gain, self_shift, cross_gain, cross_shift, final_gain, final_shift])
    matrices, expand_full, reduce_full, norm_full = fetch(
        attention_rows, expand_weight, reduce_weight, norm_rows
    )
    gains = norm_full.astype(jnp.float32)
    target_ids = target_segments[0]
    source_ids = source_segments[0]
    positions = lax.iota(jnp.int32, tokens.shape[0])
    causal = (target_ids[:, None] == target_ids[None, :]) & (
        positions[None, :] <= positions[:, None]
    )
    crossing = target_ids[:, None] == source_ids[None, :]
    query_one = matmul(tokens, matrices[0]).astype(jnp.bfloat16)
    key_one = matmul(tokens, matrices[1]).astype(jnp.bfloat16)
    value_one = matmul(tokens, matrices[2]).astype(jnp.bfloat16)
    context_one, logsum_one = attend_forward(query_one, key_one, value_one, causal)
    branch_one = matmul(context_one, matrices[3])
    first, first_scaled, first_inverse = normalize(
        RESIDUAL_SCALE * tokens.astype(jnp.float32) + branch_one, gains[0], gains[1]
    )
    first_low = first.astype(jnp.bfloat16)
    query_two = matmul(first_low, matrices[4]).astype(jnp.bfloat16)
    key_two = matmul(memory, matrices[5]).astype(jnp.bfloat16)
    value_two = matmul(memory, matrices[6]).astype(jnp.bfloat16)
    context_two, logsum_two = attend_forward(query_two, key_two, value_two, crossing)
    branch_two = matmul(context_two, matrices[7])
    second, second_scaled, second_inverse = normalize(
        RESIDUAL_SCALE * first + branch_two, gains[2], gains[3]
    )
    second_low = second.astype(jnp.bfloat16)
    inner = matmul(second_low, expand_full)
    active = gelu_tanh(inner).astype(jnp.bfloat16)
    branch_three = matmul(active, reduce_full)
    final, final_scaled, final_inverse = normalize(
        RESIDUAL_SCALE * second + branch_three, gains[4], gains[5]
    )
    output = final.astype(jnp.bfloat16)
    matrices, expand_full, reduce_full, norm_full = fetch(
        attention_rows, expand_weight, reduce_weight, norm_rows
    )
    gains = norm_full.astype(jnp.float32)
    d_sum_three, final_gain_term, final_shift_term = normalize_back(
        output_grad.astype(jnp.float32), final_scaled, final_inverse, gains[4]
    )
    d_branch_three = d_sum_three.astype(jnp.bfloat16)
    reduce_term = across(active, d_branch_three)
    d_active = against(d_branch_three, reduce_full)
    d_inner = jax.vjp(gelu_tanh, inner)[1](d_active)[0].astype(jnp.bfloat16)
    expand_term = across(second_low, d_inner)
    d_second = RESIDUAL_SCALE * d_sum_three + against(d_inner, expand_full)
    d_sum_two, cross_gain_term, cross_shift_term = normalize_back(
        d_second, second_scaled, second_inverse, gains[2]
    )
    d_branch_two = d_sum_two.astype(jnp.bfloat16)
    cross_output_term = across(context_two, d_branch_two)
    d_context_two = against(d_branch_two, matrices[7]).astype(jnp.bfloat16)
    d_query_two, d_key_two, d_value_two = attend_back(
        query_two, key_two, value_two, crossing, logsum_two, d_context_two
    )
    cross_query_term = across(first_low, d_query_two)
    cross_key_term = across(memory, d_key_two)
    cross_value_term = across(memory, d_value_two)
    memory_grad = against(d_key_two, matrices[5]) + against(d_value_two, matrices[6])
    d_first = RESIDUAL_SCALE * d_sum_two + against(d_query_two, matrices[4])
    d_sum_one, self_gain_term, self_shift_term = normalize_back(
        d_first, first_scaled, first_inverse, gains[0]
    )
    d_branch_one = d_sum_one.astype(jnp.bfloat16)
    self_output_term = across(context_one, d_branch_one)
    d_context_one = against(d_branch_one, matrices[3]).astype(jnp.bfloat16)
    d_query_one, d_key_one, d_value_one = attend_back(
        query_one, key_one, value_one, causal, logsum_one, d_context_one
    )
    self_query_term = across(tokens, d_query_one)
    self_key_term = across(tokens, d_key_one)
    self_value_term = across(tokens, d_value_one)
    tokens_grad = (
        RESIDUAL_SCALE * d_sum_one
        + against(d_query_one, matrices[0])
        + against(d_key_one, matrices[1])
        + against(d_value_one, matrices[2])
    )
    attention_terms = jnp.stack(
        [
            self_query_term,
            self_key_term,
            self_value_term,
            self_output_term,
            cross_query_term,
            cross_key_term,
            cross_value_term,
            cross_output_term,
        ]
    )
    norm_terms = jnp.stack(
        [
            self_gain_term,
            self_shift_term,
            cross_gain_term,
            cross_shift_term,
            final_gain_term,
            final_shift_term,
        ]
    )
    attention_owned, expand_owned, reduce_owned, norm_owned = settle(
        attention_terms, expand_term, reduce_term, norm_terms
    )
    return (
        output,
        tokens_grad,
        memory_grad,
        attention_owned[0],
        attention_owned[1],
        attention_owned[2],
        attention_owned[3],
        attention_owned[4],
        attention_owned[5],
        attention_owned[6],
        attention_owned[7],
        expand_owned,
        reduce_owned,
        norm_owned[0],
        norm_owned[1],
        norm_owned[2],
        norm_owned[3],
        norm_owned[4],
        norm_owned[5],
    )


def per_device(
    grid,
    tokens,
    memory,
    target_segments,
    source_segments,
    self_query,
    self_key,
    self_value,
    self_output,
    cross_query,
    cross_key,
    cross_value,
    cross_output,
    expand_weight,
    reduce_weight,
    self_gain,
    self_shift,
    cross_gain,
    cross_shift,
    final_gain,
    final_shift,
    output_grad,
):
    if not grid.fast:
        return plain_device(
            tokens,
            memory,
            target_segments,
            source_segments,
            self_query,
            self_key,
            self_value,
            self_output,
            cross_query,
            cross_key,
            cross_value,
            cross_output,
            expand_weight,
            reduce_weight,
            self_gain,
            self_shift,
            cross_gain,
            cross_shift,
            final_gain,
            final_shift,
            output_grad,
        )
    place = grid.place()
    held_rows = self_gain.shape[0]
    norm_rows = jnp.stack([self_gain, self_shift, cross_gain, cross_shift, final_gain, final_shift])
    extra = jnp.zeros((16, held_rows * grid.count), jnp.bfloat16)
    extra = lax.dynamic_update_slice(extra, norm_rows, (0, grid.index() * held_rows))
    extra = extra.reshape(4, 32, 128)
    first_rows = jnp.concatenate([jnp.stack([self_query, self_key, self_value, self_output]), extra], axis=-1)
    second_rows = jnp.stack([cross_query, cross_key, cross_value, cross_output])
    target_column, target_row = target_segments.reshape(-1, 1), target_segments
    source_row = source_segments

    first_own = gather_direct(grid, first_rows)
    second_pair = gather_pair(grid, second_rows)
    first_own, second_pair, expand_rows = after((first_own, second_pair, expand_weight))
    first_sides = gather_sides(grid, first_own)
    second_own = gather_pairs(grid, second_pair)
    expand_pair = gather_pair(grid, expand_rows)
    first_sides, second_own, expand_pair, reduce_rows = after(
        (first_sides, second_own, expand_pair, reduce_weight)
    )
    first_ends = gather_corner(grid, first_own, first_sides)
    second_sides = gather_sides(grid, second_own)
    expand_own = gather_pairs(grid, expand_pair)
    first_corner = gather_last(grid, *first_ends[:2])
    first_pieces = (first_own, *first_sides, first_ends[2], *first_corner)
    second_sides, expand_own, reduce_rows, first_pieces = after(
        (second_sides, expand_own, reduce_rows, first_pieces)
    )
    second_ends = gather_corner(grid, second_own, second_sides)
    expand_sides = gather_sides(grid, expand_own)
    reduce_pair = gather_pair(grid, reduce_rows)
    first_out = self_forward(grid, place, tokens, target_column, target_row, first_pieces)
    first_out, second_ends, reduce_pair = after((first_out, second_ends, reduce_pair))
    first_full, gains, query_one, key_one, value_one, context_one, logsum_one = first_out[:7]
    first, first_low, first_scaled, first_inverse = first_out[7:]
    reduce_own = gather_pairs(grid, reduce_pair)
    second_corner = gather_last(grid, *second_ends[:2])
    second_pieces = (second_own, *second_sides, second_ends[2], *second_corner)
    expand_sides, reduce_own, second_pieces = after((expand_sides, reduce_own, second_pieces))
    expand_ends = gather_corner(grid, expand_own, expand_sides)
    reduce_sides = gather_sides(grid, reduce_own)
    second_out = cross_forward(
        grid, place, first, first_low, memory, gains, target_column, source_row, second_pieces
    )
    second_out, expand_ends = after((second_out, expand_ends))
    second_full, query_two, key_two, value_two, context_two, logsum_two = second_out[:6]
    second, second_low, second_scaled, second_inverse = second_out[6:]
    held = jnp.concatenate([tokens, context_one, first_low, context_two, second_low, memory])
    held_far = grid.move(held, dc=1)
    expand_corner = gather_last(grid, *expand_ends[:2])
    expand_pieces = (expand_own, *expand_sides, expand_ends[2], *expand_corner)
    reduce_sides, expand_pieces = after((reduce_sides, expand_pieces))
    reduce_ends = gather_corner(grid, reduce_own, reduce_sides)
    expand_full, active, slope = expand_forward(grid, place, second_low, expand_pieces)
    active_far = grid.move(active, dc=1)
    partial = reduce_first(grid, place, active, (reduce_own, *reduce_sides, reduce_ends[2]))
    reduce_low, reduce_high, partial = after((*reduce_ends[:2], partial))
    reduce_corner = gather_last(grid, reduce_low, reduce_high)
    reduce_pieces = (reduce_own, *reduce_sides, reduce_ends[2], *reduce_corner)
    output, d_sum_three, d_branch_three, final_norm_terms = reduce_finish(
        grid, place, active, partial, second, gains, output_grad, *reduce_corner
    )
    d_branches = (d_branch_three, grid.move(d_branch_three, dc=1))
    reduce_low, reduce_high = after(
        tuple(tiled_terms(grid, place, active, active_far, *d_branches, 1024, (3,)))
    )
    reduce_terms = tiled_terms(
        grid, place, after(active, reduce_low), active_far, *d_branches, 512, (0, 1, 2)
    )
    d_inner = reduce_back(grid, place, after(d_branch_three, *reduce_terms), slope, reduce_pieces)
    reduce_low, reduce_high = grid.move(reduce_low, dy=1), grid.move(reduce_high, dx=1)
    reduce_low, reduce_high, d_inner = after((reduce_low, reduce_high, d_inner))
    reduce_sends = corner_added(grid, reduce_terms, reduce_low, reduce_high)
    reduce_sends, d_inner = after((reduce_sends, d_inner))
    reduce_x, reduce_y = grid.move(reduce_sends[0], dx=1), grid.move(reduce_sends[1], dy=1)
    d_inner_far = grid.move(d_inner, dc=1)
    d_sum_two, d_branch_two, d_context_two, cross_norm_terms = expand_back(
        d_inner, expand_full, d_sum_three, second_scaled, second_inverse, gains, second_full
    )
    expand_terms = tiled_terms(grid, place, second_low, held_far, after(d_inner, d_context_two), d_inner_far, 1024)
    expand_terms, d_context_two = after((expand_terms, d_context_two))
    expand_low, expand_high = grid.move(expand_terms[3], dy=1), grid.move(expand_terms[4], dx=1)
    back, d_sum_one, d_context_one, self_norm_terms = cross_back(
        query_two, key_two, value_two, logsum_two, d_context_two, target_column,
        source_row, d_branch_two, d_sum_two, first_scaled, first_inverse, gains, second_full, first_full,
    )
    norm_terms = jnp.concatenate([self_norm_terms, cross_norm_terms, final_norm_terms])
    expand_low, expand_high, reduce_x, reduce_y, back, norm_terms = after(
        (expand_low, expand_high, reduce_x, reduce_y, back, norm_terms)
    )
    expand_sends = corner_added(grid, expand_terms, expand_low, expand_high)
    expand_sends, back = after((expand_sends, back))
    expand_x, expand_y = grid.move(expand_sends[0], dx=1), grid.move(expand_sends[1], dy=1)
    reduce_near, reduce_pass = plane_sums(grid, reduce_terms, *after((reduce_x, reduce_y), expand_sends))
    reduce_near, reduce_pass, back = after((reduce_near, reduce_pass, back))
    reduce_got = grid.move(reduce_pass, dz=2)
    backs = grid.cores(back)
    pairs = [(256, 1, 2), (256, 2, 1), (128, 10, 6), (128, 10, 7), (256, 3, 0)]
    cross_terms = group_terms(grid, place, held, held_far, backs, None, pairs)
    cross_terms, d_context_one = after((cross_terms, d_context_one))
    cross_low, cross_high = grid.move(cross_terms[3], dy=1), grid.move(cross_terms[4], dx=1)
    back_one = self_back(
        query_one, key_one, value_one, logsum_one, d_context_one, target_column, target_row
    )
    cross_low, cross_high, back_one, reduce_got, expand_x, expand_y = after(
        (cross_low, cross_high, back_one, reduce_got, expand_x, expand_y)
    )
    cross_sends = corner_added(grid, cross_terms, cross_low, cross_high)
    reduce_leaving = pair_sum(reduce_near, reduce_got)
    cross_sends, back_one, reduce_leaving = after((cross_sends, back_one, reduce_leaving))
    cross_x, cross_y = grid.move(cross_sends[0], dx=1), grid.move(cross_sends[1], dy=1)
    back_one_far = grid.move(back_one, dc=1)
    reduce_last = grid.move(reduce_leaving, dz=1)
    expand_near, expand_pass = plane_sums(grid, expand_terms, *after((expand_x, expand_y), cross_sends))
    expand_near, expand_pass, back_one = after((expand_near, expand_pass, back_one))
    expand_got = grid.move(expand_pass, dz=2)
    self_terms = group_terms(
        grid, place, held, held_far, back_one, back_one_far, [(256, 0, n) for n in range(3)]
    )
    tokens_grad, memory_grad = inputs_back(
        after(back_one, *self_terms), back, d_sum_one, first_full, second_full
    )
    cross_x, cross_y, expand_got, reduce_last, self_low, self_high = after(
        (cross_x, cross_y, expand_got, reduce_last, self_terms[3], self_terms[4]), tokens_grad
    )
    cross_near, cross_pass = plane_sums(grid, cross_terms, cross_x, cross_y)
    expand_leaving = pair_sum(expand_near, expand_got)
    cross_near, cross_pass, self_low, self_high, expand_leaving = after(
        (cross_near, cross_pass, self_low, self_high, expand_leaving)
    )
    self_low, self_high = grid.move(self_low, dy=1), grid.move(self_high, dx=1)
    cross_got = grid.move(cross_pass, dz=2)
    expand_last = grid.move(expand_leaving, dz=1)
    self_low, self_high, expand_last = after((self_low, self_high, expand_last))
    self_sends = corner_added(grid, self_terms, self_low, self_high)
    self_sends, norm_terms = after((self_sends, norm_terms))
    self_x, self_y = grid.move(self_sends[0], dx=1), grid.move(self_sends[1], dy=1)
    norm_got = lax.all_to_all(norm_terms.reshape(6, grid.count, held_rows), grid.axes, 1, 0, tiled=True)
    self_x, self_y, norm_got = after((self_x, self_y, norm_got))
    self_column = after([plane_sum(self_terms[0][k], self_x[k], self_y[k]) for k in range(grid.depth)])
    self_others = [grid.move(self_column[k], dz=k) for k in (2, 3, 1)]
    cross_leaving = pair_sum(cross_near, after(cross_got, self_column))
    cross_last = grid.move(cross_leaving, dz=1)
    reduce_term = total_of(reduce_near[0], reduce_got[0], reduce_last)
    expand_term = total_of(expand_near[0], expand_got[0], expand_last)
    cross_owned = total_of(cross_near[0], cross_got[0], cross_last)
    self_owned = total_of(self_column[0], *self_others)
    norm_owned = jnp.sum(norm_got.reshape(grid.count, 6, held_rows), axis=0)
    return (
        output,
        tokens_grad,
        memory_grad,
        *[self_owned[i] for i in range(3)],
        *[cross_owned[i] for i in range(5)],
        expand_term,
        reduce_term,
        *[norm_owned[i] for i in range(6)],
    )


def solution(mesh):
    grid = Grid(mesh)
    rows = P(grid.axes, None)
    parts = P(grid.axes)
    return jax.shard_map(
        functools.partial(per_device, grid),
        mesh=grid.mesh,
        in_specs=(
            rows,
            rows,
            rows,
            rows,
            rows,
            rows,
            rows,
            rows,
            rows,
            rows,
            rows,
            rows,
            rows,
            rows,
            parts,
            parts,
            parts,
            parts,
            parts,
            parts,
            rows,
        ),
        out_specs=(
            rows,
            rows,
            rows,
            rows,
            rows,
            rows,
            rows,
            rows,
            rows,
            rows,
            rows,
            rows,
            rows,
            parts,
            parts,
            parts,
            parts,
            parts,
            parts,
        ),
        check_vma=False,
    )
```

```python
import functools

import jax
import jax.numpy as jnp
from jax import lax
from jax.experimental import pallas as pl
from jax.experimental.pallas import tpu as pltpu
from jax.sharding import PartitionSpec as P

HEADS = 16
HEAD_DIM = 64


RESIDUAL_SCALE = 300.0**0.25
EPSILON = 1e-05
NEGATIVE = -1e30
ALL = ("dp", "fsdp")


class Grid:
    def __init__(self, mesh):
        self.depth = mesh.shape["dp"] // 2
        self.count = mesh.size
        self.fast = mesh.shape["fsdp"] == 4 and mesh.shape["dp"] == 8
        self.axes = ("z", "core", "y", "x") if self.fast else ALL
        self.mesh = mesh
        if self.fast:
            self.mesh = jax.sharding.Mesh(mesh.devices.reshape(4, 2, 2, 2), self.axes)

    def place(self):
        return jnp.stack([lax.axis_index(axis) for axis in self.axes]).astype(jnp.int32)

    def index(self):
        return lax.axis_index(self.axes)

    def move(self, value, dz=0, dc=0, dy=0, dx=0):
        offset = ((dz * 2 + dc) * 2 + dy) * 2 + dx
        return lax.ppermute(value, self.axes, [(index ^ offset, index) for index in range(self.count)])

    def cores(self, twice):
        return lax.all_to_all(twice, "core", 0, 0, tiled=True)


def after(value, *others):
    return lax.optimization_barrier((value,) + others)[0]


def wide_dot(left, right):
    return jnp.dot(left, right, preferred_element_type=jnp.float32)


def dot_rows(left, right):
    return lax.dot_general(left, right, (((1,), (1,)), ((), ())), preferred_element_type=jnp.float32)


def dot_columns(left, right):
    return lax.dot_general(left, right, (((0,), (0,)), ((), ())), preferred_element_type=jnp.float32)


def whole_call(body, name, inputs, shapes, scratch=(), limit=56):
    arrays, specs = [], []
    for item in inputs:
        if not isinstance(item, tuple):
            item = (item, item.shape, (0,) * item.ndim)
        arrays.append(item[0])
        if len(item) == 2:
            specs.append(pl.BlockSpec(memory_space=item[1]))
        else:
            specs.append(pl.BlockSpec(item[1], lambda i, index=item[2]: index))
    outs, out_specs = [], []
    for item in shapes:
        outs.append(jax.ShapeDtypeStruct(item[0], item[1]))
        if len(item) == 3:
            out_specs.append(pl.BlockSpec(memory_space=item[2]))
        else:
            out_specs.append(pl.BlockSpec(item[0], lambda i, rank=len(item[0]): (0,) * rank))
    return pl.pallas_call(
        body,
        grid=(1,),
        out_shape=outs,
        in_specs=specs,
        out_specs=out_specs,
        scratch_shapes=list(scratch),
        compiler_params=pltpu.CompilerParams(vmem_limit_bytes=limit * 2**20),
        cost_estimate=pl.CostEstimate(flops=1, bytes_accessed=1, transcendentals=0),
        name=name,
    )(*arrays)


def in_two(depth, pieces, dc, side, k):
    return pieces[dc], side * depth + k


def in_rest(base):
    def locate(depth, pieces, dc, side, k):
        half = depth // 2
        own, over_x, over_y, low, high = pieces[5 * dc : 5 * dc + 5]
        if side == 0:
            return own, base + k
        if side < 3:
            return (over_x, over_y)[side - 1], half + k
        return (low, k) if k < half else (high, k - half)

    return locate


def in_last(depth, pieces, dc, side, k):
    own, over_x, over_y, corner = pieces[4 * dc : 4 * dc + 4]
    return (own, over_x, over_y, corner)[side], depth // 2 + k if side in (1, 2) else k


def in_second(depth, pieces, dc, side, k):
    half = depth // 2
    sides, low, high = pieces[3 * dc : 3 * dc + 3]
    if side < 3:
        return sides, side * depth + k
    return (low, k) if k < half else (high, k - half)


def arrivals_of(depth, rows, place, locate, pieces, held, sems, held_norms=None, these=range(8), blocks=0):
    z, c, y, x = place[0], place[1], place[2], place[3]
    width = held.shape[-1]
    arrivals = []
    for k in range(depth):
        column = []
        for n in these:
            dc, dy, dx = n // 4, n // 2 % 2, n % 2
            piece, spot = locate(depth, pieces, dc, n % 4, k)
            owner = (((z ^ k) * 2 + (c ^ dc)) * 2 + (y ^ dy)) * 2 + (x ^ dx)
            if blocks:
                target = held.at[pl.ds(owner * blocks, blocks)]
            else:
                target = held.at[..., pl.ds(pl.multiple_of(owner * rows, rows), rows), :]
            source = piece.at[spot]
            order = k * 8 + n
            if held_norms is None:
                column.append(pltpu.make_async_copy(source, target, sems.at[order]))
            else:
                column.append(pltpu.make_async_copy(source.at[..., :width], target, sems.at[order]))
                column.append(
                    pltpu.make_async_copy(
                        source.at[0:2, :, pl.ds(width, 128)],
                        held_norms.at[owner],
                        sems.at[8 * depth + order],
                    )
                )
        for copy in column:
            copy.start()
        arrivals.append(column)
    return arrivals


def pass_on(depth, rows, place, arrivals, held, whole, sems):
    leaving = []
    for k in range(depth):
        for copy in arrivals[k]:
            copy.wait()
        spot = pl.ds(pl.multiple_of((place[0] ^ k) * (8 * rows), 8 * rows), 8 * rows)
        leaving.append(pltpu.make_async_copy(held.at[..., spot, :], whole.at[..., spot, :], sems.at[k]))
        leaving[k].start()
    return leaving


def norm_rows_of(summed, gain, shift):
    center = jnp.mean(summed, axis=-1, keepdims=True)
    centred = summed - center
    inverse = lax.rsqrt(jnp.mean(centred * centred, axis=-1, keepdims=True) + EPSILON)
    scaled = centred * inverse
    return scaled * gain + shift, scaled, inverse


def norm_rows_back(incoming, scaled, inverse, gain):
    spread_out = incoming * gain
    d_summed = inverse * (
        spread_out
        - jnp.mean(spread_out, axis=-1, keepdims=True)
        - scaled * jnp.mean(spread_out * scaled, axis=-1, keepdims=True)
    )
    return d_summed, jnp.sum(incoming * scaled, axis=0, keepdims=True), jnp.sum(incoming, axis=0, keepdims=True)


def head_halves():
    lane = lax.broadcasted_iota(jnp.int32, (1, 2 * HEAD_DIM), 1)
    return [
        jnp.where(lane < HEAD_DIM, 1.0, 0.0).astype(jnp.bfloat16),
        jnp.where(lane < HEAD_DIM, 0.0, 1.0).astype(jnp.bfloat16),
    ]


def attend_heads(query, key, value, allowed, context, logsum):
    halves = head_halves()
    lane = lax.broadcasted_iota(jnp.int32, logsum.shape, 1)
    logsum[...] = jnp.zeros_like(logsum)

    def pair(p, carry):
        lanes = pl.ds(pl.multiple_of(p * 2 * HEAD_DIM, 2 * HEAD_DIM), 2 * HEAD_DIM)
        queries, keys, values = query[:, lanes], key[:, lanes], value[:, lanes]
        total = None
        for side, half in enumerate(halves):
            scores = dot_rows(queries * half, keys) * HEAD_DIM ** (-0.5)
            scores = jnp.where(allowed[...] > 0, scores, NEGATIVE)
            highest = jnp.max(scores, axis=-1, keepdims=True)
            weights = jnp.exp(scores - highest)
            totals = jnp.sum(weights, axis=-1, keepdims=True)
            chances = (weights * (1.0 / totals)).astype(jnp.bfloat16)
            part = wide_dot(chances, values * half)
            total = part if total is None else total + part
            logsum[...] = jnp.where(lane == 2 * p + side, highest + jnp.log(totals), logsum[...])
        context[:, lanes] = total.astype(jnp.bfloat16)
        return carry

    lax.fori_loop(0, HEADS // 2, pair, 0)


def attend_heads_back(query, key, value, allowed, logsum, d_context, d_query, d_key, d_value):
    halves = head_halves()
    lane = lax.broadcasted_iota(jnp.int32, logsum.shape, 1)
    scale = HEAD_DIM ** (-0.5)

    def pair(p, carry):
        lanes = pl.ds(pl.multiple_of(p * 2 * HEAD_DIM, 2 * HEAD_DIM), 2 * HEAD_DIM)
        queries, keys, values, d_outs = query[:, lanes], key[:, lanes], value[:, lanes], d_context[:, lanes]
        sums = [None, None, None]
        for side, half in enumerate(halves):
            own_sum = jnp.sum(jnp.where(lane == 2 * p + side, logsum[...], 0.0), axis=-1, keepdims=True)
            own_queries, own_outs = queries * half, d_outs * half
            scores = dot_rows(own_queries, keys) * scale
            scores = jnp.where(allowed[...] > 0, scores, NEGATIVE)
            chances = jnp.exp(scores - own_sum)
            d_chances = dot_rows(own_outs, values)
            centre = jnp.sum(d_chances * chances, axis=-1, keepdims=True)
            d_scores = (chances * (d_chances - centre)).astype(jnp.bfloat16)
            parts = (
                wide_dot(d_scores, keys * half),
                dot_columns(d_scores, own_queries),
                dot_columns(chances.astype(jnp.bfloat16), own_outs),
            )
            sums = [part if old is None else old + part for old, part in zip(sums, parts)]
        d_query[:, lanes] = (sums[0] * scale).astype(jnp.bfloat16)
        d_key[:, lanes] = (sums[1] * scale).astype(jnp.bfloat16)
        d_value[:, lanes] = sums[2].astype(jnp.bfloat16)
        return carry

    lax.fori_loop(0, HEADS // 2, pair, 0)


def self_allowed(ids_column, ids_row, allowed):
    rows, columns = allowed.shape
    later = lax.broadcasted_iota(jnp.int32, (rows, columns), 0) >= lax.broadcasted_iota(
        jnp.int32, (rows, columns), 1
    )
    same = ids_column[...] == ids_row[...]
    allowed[...] = jnp.where(later & same, 1.0, 0.0)


def cross_allowed(ids_column, ids_row, allowed):
    allowed[...] = jnp.where(ids_column[...] == ids_row[...], 1.0, 0.0)


def self_forward_kernel(depth, rows, place, tokens, ids_column, ids_row, *refs):
    pieces, refs = refs[:2], refs[2:]
    whole, gains, query, key, value, context, logsum, first, first_low, scaled, inverse = refs[:11]
    held, held_norms, allowed, in_sems, out_sems = refs[11:]
    arrivals = arrivals_of(depth, rows, place, in_two, pieces, held, in_sems, held_norms)
    self_allowed(ids_column, ids_row, allowed)
    leaving = pass_on(depth, rows, place, arrivals, held, whole, out_sems)
    packed = held_norms[0].astype(jnp.float32)
    for owner in range(1, 8 * depth):
        packed += held_norms[owner].astype(jnp.float32)
    gains[...] = jnp.zeros_like(gains)
    for n in range(6):
        for j in range(8):
            r = n * 8 + j
            gains[n : n + 1, j * 128 : (j + 1) * 128] = packed[r // rows, r % rows : r % rows + 1, :]
    for n, out in enumerate((query, key, value)):
        out[...] = wide_dot(tokens[...], held[n]).astype(jnp.bfloat16)
    attend_heads(query, key, value, allowed, context, logsum)
    branch = wide_dot(context[...], held[3])
    summed = RESIDUAL_SCALE * tokens[...].astype(jnp.float32) + branch
    first[...], scaled[...], inverse[...] = norm_rows_of(summed, gains[0:1, :], gains[1:2, :])
    first_low[...] = first[...].astype(jnp.bfloat16)
    for copy in leaving:
        copy.wait()


def self_forward(grid, place, tokens, ids_column, ids_row, pieces):
    count, width = tokens.shape
    rows = pieces[0].shape[2]
    low, full = jnp.bfloat16, jnp.float32
    shape = (count, width)
    return whole_call(
        functools.partial(self_forward_kernel, grid.depth, rows),
        "self_forward",
        [(place, pltpu.SMEM), tokens, ids_column, ids_row] + [(piece, pl.ANY) for piece in pieces],
        [((4, width, width), low, pl.ANY), ((8, width), full)]
        + [(shape, low)] * 4
        + [((count, 128), full), (shape, full), (shape, low), (shape, full), ((count, 1), full)],
        [
            pltpu.VMEM((4, width, width), low),
            pltpu.VMEM((grid.count, 2, rows, 128), low),
            pltpu.VMEM((count, count), full),
            pltpu.SemaphoreType.DMA((2 * grid.count,)),
            pltpu.SemaphoreType.DMA((grid.depth,)),
        ],
    )


def cross_forward_kernel(depth, rows, place, first, first_low, memory, gains, ids_column, ids_row, *refs):
    pieces, refs = refs[:6], refs[6:]
    whole, query, key, value, context, logsum, second, second_low, scaled, inverse = refs[:10]
    held, allowed, in_sems, out_sems = refs[10:]
    arrivals = arrivals_of(depth, rows, place, in_second, pieces, held, in_sems)
    cross_allowed(ids_column, ids_row, allowed)
    leaving = pass_on(depth, rows, place, arrivals, held, whole, out_sems)
    query[...] = wide_dot(first_low[...], held[0]).astype(jnp.bfloat16)
    key[...] = wide_dot(memory[...], held[1]).astype(jnp.bfloat16)
    value[...] = wide_dot(memory[...], held[2]).astype(jnp.bfloat16)
    attend_heads(query, key, value, allowed, context, logsum)
    summed = RESIDUAL_SCALE * first[...] + wide_dot(context[...], held[3])
    second[...], scaled[...], inverse[...] = norm_rows_of(summed, gains[2:3, :], gains[3:4, :])
    second_low[...] = second[...].astype(jnp.bfloat16)
    for copy in leaving:
        copy.wait()


def cross_forward(grid, place, first, first_low, memory, gains, ids_column, ids_row, pieces):
    count, width = first.shape
    others = memory.shape[0]
    rows = pieces[0].shape[2]
    low, full = jnp.bfloat16, jnp.float32
    shape, other_shape = (count, width), (others, width)
    return whole_call(
        functools.partial(cross_forward_kernel, grid.depth, rows),
        "cross_forward",
        [(place, pltpu.SMEM), first, first_low, memory, gains, ids_column, ids_row]
        + [(piece, pl.ANY) for piece in pieces],
        [((4, width, width), low, pl.ANY), (shape, low), (other_shape, low), (other_shape, low), (shape, low)]
        + [((count, 128), full), (shape, full), (shape, low), (shape, full), ((count, 1), full)],
        [
            pltpu.VMEM((4, width, width), low),
            pltpu.VMEM((count, others), full),
            pltpu.SemaphoreType.DMA((grid.count,)),
            pltpu.SemaphoreType.DMA((grid.depth,)),
        ],
    )


TANH_SCALE = 0.7978845608028654
TANH_CUBE = 0.044715


def expand_forward_kernel(depth, rows, place, second_low, *refs):
    pieces, refs = refs[:10], refs[10:]
    whole, active, slope, held, in_sems, out_sems = refs
    arrivals = arrivals_of(depth, rows, place, in_rest(3 * depth), pieces, held, in_sems)
    leaving = pass_on(depth, rows, place, arrivals, held, whole, out_sems)
    left = second_low[...]
    block = held.shape[2]

    def tile(j, carry):
        for part in range(block // 512):
            lanes = pl.ds(pl.multiple_of(j * block + part * 512, 512), 512)
            inner = wide_dot(left, held[j, :, part * 512 : (part + 1) * 512])
            square = inner * inner
            bend = jnp.tanh(TANH_SCALE * (inner * (1.0 + TANH_CUBE * square)))
            half = 0.5 + 0.5 * bend
            active[:, lanes] = (inner * half).astype(jnp.bfloat16)
            slope[:, lanes] = half + (0.5 * TANH_SCALE) * inner * (1.0 - bend * bend) * (
                1.0 + (3.0 * TANH_CUBE) * square
            )
        return carry

    lax.fori_loop(0, held.shape[0], tile, 0)
    for copy in leaving:
        copy.wait()


def expand_forward(grid, place, second_low, pieces):
    count, width = second_low.shape
    blocks, rows, block = pieces[0].shape[1:]
    hidden = blocks * block
    low = jnp.bfloat16
    return whole_call(
        functools.partial(expand_forward_kernel, grid.depth, rows),
        "expand_forward",
        [(place, pltpu.SMEM), second_low] + [(piece, pl.ANY) for piece in pieces],
        [((blocks, width, block), low, pl.ANY), ((count, hidden), low), ((count, hidden), jnp.float32)],
        [
            pltpu.VMEM((blocks, width, block), low),
            pltpu.SemaphoreType.DMA((grid.count,)),
            pltpu.SemaphoreType.DMA((grid.depth,)),
        ],
    )


def rows_of(held):
    return held.reshape(held.shape[0] * held.shape[1], held.shape[2])


def reduce_first_kernel(depth, place, active, *refs):
    pieces, (partial, held, sems) = refs[:6], refs[6:]
    z, c, y, x = place[0], place[1], place[2], place[3]
    blocks, rows, width = pieces[0].shape[1:]

    def locate(depth, pieces, dc, side, k):
        return (pieces[3 * dc], k) if side == 0 else (pieces[3 * dc + side], depth // 2 + k)

    arrivals = arrivals_of(
        depth, rows, place, locate, pieces, held, sems, these=(0, 1, 2, 4, 5, 6), blocks=blocks
    )
    for there in range(depth):
        for core in range(2):
            owner = ((there * 2 + core) * 2 + (1 - y)) * 2 + (1 - x)
            held[pl.ds(owner * blocks, blocks)] = jnp.zeros((blocks, rows, width), held.dtype)
    span = 8 * blocks
    for k, column in enumerate(arrivals):
        for copy in column:
            copy.wait()
        there = z ^ k
        lanes = pl.ds(pl.multiple_of(there * (span * rows), span * rows), span * rows)
        part = wide_dot(active[:, lanes], rows_of(held[pl.ds(there * span, span)]))
        partial[...] = part if k == 0 else partial[...] + part


def reduce_first(grid, place, active, pieces):
    count, hidden = active.shape
    blocks, rows, width = pieces[0].shape[1:]
    return whole_call(
        functools.partial(reduce_first_kernel, grid.depth),
        "reduce_first",
        [(place, pltpu.SMEM), active] + [(piece, pl.ANY) for piece in pieces],
        [((count, width), jnp.float32)],
        [
            pltpu.VMEM((grid.count * blocks, rows, width), jnp.bfloat16),
            pltpu.SemaphoreType.DMA((grid.count,)),
        ],
    )[0]


def reduce_finish_kernel(depth, place, active, partial, second, gains, output_grad, *refs):
    corners, (output, d_summed, d_branch, norm_terms) = refs[:2], refs[2:]
    z, c, y, x = place[0], place[1], place[2], place[3]
    summed = RESIDUAL_SCALE * second[...] + partial[...]
    for k in range(depth):
        for dc in range(2):
            piece = rows_of(corners[dc][k])
            rows = piece.shape[0]
            owner = (((z ^ k) * 2 + (c ^ dc)) * 2 + (1 - y)) * 2 + (1 - x)
            summed += wide_dot(active[:, pl.ds(pl.multiple_of(owner * rows, rows), rows)], piece)
    final, scaled, inverse = norm_rows_of(summed, gains[4:5, :], gains[5:6, :])
    output[...] = final.astype(jnp.bfloat16)
    d_sum, norm_terms[0:1, :], norm_terms[1:2, :] = norm_rows_back(
        output_grad[...].astype(jnp.float32), scaled, inverse, gains[4:5, :]
    )
    d_summed[...] = d_sum
    d_branch[...] = d_sum.astype(jnp.bfloat16)


def reduce_finish(grid, place, active, partial, second, gains, output_grad, corners):
    shape = second.shape
    low, full = jnp.bfloat16, jnp.float32
    return whole_call(
        functools.partial(reduce_finish_kernel, grid.depth),
        "reduce_finish",
        [(place, pltpu.SMEM), active, partial, second, gains, output_grad, *corners],
        [(shape, low), (shape, full), (shape, low), ((2, shape[1]), full)],
    )


def reduce_back_kernel(depth, place, d_branch, slope, *refs):
    pieces, (d_inner, held, sems) = refs[:8], refs[8:]
    blocks, rows, width = pieces[0].shape[1:]
    arrivals = arrivals_of(depth, rows, place, in_last, pieces, held, sems, blocks=blocks)
    left = d_branch[...]
    step = 512 // rows
    tiles = 8 * blocks // step
    for k, column in enumerate(arrivals):
        for copy in column:
            copy.wait()
        for n in range(tiles):
            j = (place[0] ^ k) * tiles + n
            lanes = pl.ds(pl.multiple_of(j * 512, 512), 512)
            d_active = dot_rows(left, rows_of(held[pl.ds(j * step, step)]))
            d_inner[:, lanes] = (d_active * slope[:, lanes]).astype(jnp.bfloat16)


def reduce_back(grid, place, d_branch, slope, pieces):
    count, hidden = slope.shape
    blocks, rows, width = pieces[0].shape[1:]
    return whole_call(
        functools.partial(reduce_back_kernel, grid.depth),
        "reduce_back",
        [(place, pltpu.SMEM), d_branch, slope] + [(piece, pl.ANY) for piece in pieces],
        [((count, hidden), jnp.bfloat16)],
        [
            pltpu.VMEM((grid.count * blocks, rows, width), jnp.bfloat16),
            pltpu.SemaphoreType.DMA((grid.count,)),
        ],
    )[0]


def expand_back_kernel(d_inner, expand, d_sum_three, scaled, inverse, gains, out_weight, d_summed, d_branch, d_context, norm_terms):
    d_second = RESIDUAL_SCALE * d_sum_three[...]
    block = expand.shape[2]
    for n in range(expand.shape[0]):
        d_second += dot_rows(d_inner[:, n * block : (n + 1) * block], expand[n])
    d_sum, norm_terms[0:1, :], norm_terms[1:2, :] = norm_rows_back(
        d_second, scaled[...], inverse[...], gains[2:3, :]
    )
    d_summed[...] = d_sum
    d_branch[...] = d_sum.astype(jnp.bfloat16)
    d_context[...] = dot_rows(d_branch[...], out_weight[0]).astype(jnp.bfloat16)


def expand_back(d_inner, expand, d_sum_three, scaled, inverse, gains, second_full):
    shape = d_sum_three.shape
    width = shape[1]
    low, full = jnp.bfloat16, jnp.float32
    return whole_call(
        expand_back_kernel,
        "expand_back",
        [d_inner, expand, d_sum_three, scaled, inverse, gains]
        + [(second_full, (1, width, width), (3, 0, 0))],
        [(shape, full), (shape, low), (shape, low), ((2, width), full)],
    )


def cross_back_kernel(
    query, key, value, logsum, d_context, ids_column, ids_row, d_branch_two, d_sum_two, scaled, inverse, gains,
    query_weight, out_weight, back, d_summed, d_context_one, norm_terms, allowed,
):
    count, others = query.shape[0], key.shape[0]
    cross_allowed(ids_column, ids_row, allowed)
    rows = back.at[0]
    d_query = rows.at[count : 2 * count]
    d_key = rows.at[3 * count : 3 * count + others]
    d_value = rows.at[3 * count + others : 3 * count + 2 * others]
    attend_heads_back(query, key, value, allowed, logsum, d_context, d_query, d_key, d_value)
    d_first = RESIDUAL_SCALE * d_sum_two[...] + dot_rows(d_query[...], query_weight[0])
    d_sum, norm_terms[0:1, :], norm_terms[1:2, :] = norm_rows_back(
        d_first, scaled[...], inverse[...], gains[0:1, :]
    )
    d_summed[...] = d_sum
    d_branch = d_sum.astype(jnp.bfloat16)
    rows[0:count, :] = d_branch_two[...]
    rows[2 * count : 3 * count, :] = d_branch
    back[1] = rows[...]
    d_context_one[...] = dot_rows(d_branch, out_weight[0]).astype(jnp.bfloat16)


def cross_back(query, key, value, logsum, d_context, ids_column, ids_row, d_branch_two, d_sum_two, scaled, inverse, gains, second_full, first_full):
    shape, other_shape = query.shape, key.shape
    width = shape[1]
    low, full = jnp.bfloat16, jnp.float32
    block = (1, width, width)
    return whole_call(
        cross_back_kernel,
        "cross_back",
        [query, key, value, logsum, d_context, ids_column, ids_row, d_branch_two, d_sum_two, scaled, inverse, gains]
        + [(second_full, block, (0, 0, 0)), (first_full, block, (3, 0, 0))],
        [((2, 3 * shape[0] + 2 * other_shape[0], width), low), (shape, full), (shape, low), ((2, width), full)],
        [pltpu.VMEM((shape[0], other_shape[0]), full)],
    )


def self_back_kernel(query, key, value, logsum, d_context, ids_column, ids_row, d_rows, allowed):
    self_allowed(ids_column, ids_row, allowed)
    count = query.shape[0]
    outs = [d_rows.at[n * count : (n + 1) * count] for n in range(3)]
    attend_heads_back(query, key, value, allowed, logsum, d_context, *outs)


def self_back(query, key, value, logsum, d_context, ids_column, ids_row):
    count, width = query.shape
    return whole_call(
        self_back_kernel,
        "self_back",
        [query, key, value, logsum, d_context, ids_column, ids_row],
        [((3 * count, width), jnp.bfloat16)],
        [pltpu.VMEM((count, count), jnp.float32)],
    )[0]


def inputs_back_kernel(d_rows, d_key, d_value, d_sum_one, w_query, w_key, w_value, w_key_two, w_value_two, tokens_grad, memory_grad):
    count = d_sum_one.shape[0]
    total = RESIDUAL_SCALE * d_sum_one[...]
    for n, weight in enumerate((w_query, w_key, w_value)):
        total += dot_rows(d_rows[n * count : (n + 1) * count, :], weight[0])
    tokens_grad[...] = total
    memory_grad[...] = dot_rows(d_key[0], w_key_two[0]) + dot_rows(d_value[0], w_value_two[0])


def inputs_back(d_rows, back, d_sum_one, first_full, second_full):
    count, width = d_sum_one.shape
    others = (back.shape[1] - 3 * count) // 2
    first_row = 3 * count // others
    block = (1, width, width)
    return whole_call(
        inputs_back_kernel,
        "inputs_back",
        [d_rows]
        + [(back, (1, others, width), (0, first_row + n, 0)) for n in (0, 1)]
        + [d_sum_one]
        + [(first_full, block, (n, 0, 0)) for n in range(3)]
        + [(second_full, block, (n, 0, 0)) for n in (1, 2)],
        [((count, width), jnp.float32), ((others, width), jnp.float32)],
    )


def turn(depth, rows, place, sources, turned, spots=range(4)):
    z, c, y, x = place[0], place[1], place[2], place[3]
    tokens = sources[0].shape[0]
    for k in range(depth):
        there = z ^ k
        columns = pl.ds(pl.multiple_of((there * 2 + c) * (4 * rows), 4 * rows), 4 * rows)
        for side, source in enumerate(sources):
            block = source[:, columns].T
            named = [block[n * rows : (n + 1) * rows] for n in range(4)]
            named = [jnp.where(x == 0, named[n], named[n ^ 1]) for n in range(4)]
            named = [jnp.where(y == 0, named[n], named[n ^ 2]) for n in range(4)]
            for at, spot in enumerate(spots):
                turned[at, k * rows : (k + 1) * rows, side * tokens : (side + 1) * tokens] = named[spot]


def spread(depth, rows, turned, rights, outs, spots=range(4)):
    tokens = rights[0].shape[0]
    half = depth // 2
    for at, spot in enumerate(spots):
        part = turned[at]
        total = jnp.dot(part[:, :tokens], rights[0][...], preferred_element_type=jnp.float32)
        total += jnp.dot(
            part[:, tokens : 2 * tokens], rights[1][...], preferred_element_type=jnp.float32
        )
        total = total.astype(jnp.bfloat16).reshape(depth, rows, -1)
        if spot < 3:
            outs[at][...] = total
        else:
            outs[at][...] = total[:half]
            outs[at + 1][...] = total[half:]


def tiled_kernel(depth, rows, spots, place, left, left_far, right, right_far, *refs):
    outs, turned = refs[:-1], refs[-1]

    @pl.when(pl.program_id(0) == 0)
    def _():
        turn(depth, rows, place, (left, left_far), turned, spots)

    spread(depth, rows, turned, (right, right_far), outs, spots)


def group_kernel(depth, rows, count, by_core, place, *refs):
    each = 3 if by_core else 4
    core = place[1]
    inputs, outs, turned = refs[: each * count], refs[each * count : each * count + 5], refs[-1]
    for m in range(count):
        left, left_far, *rights = inputs[each * m : each * m + each]
        if by_core:
            rights = (rights[0].at[core], rights[0].at[1 - core])
        turn(depth, rows, place, (left, left_far), turned)
        spread(depth, rows, turned, rights, [out.at[:, m] for out in outs])


def piece_counts(depth, spots=range(4)):
    counts = []
    for spot in spots:
        counts += [depth] if spot < 3 else [depth // 2, depth // 2]
    return counts


def tiled_terms(grid, place, left, left_far, right, right_far, tile, spots=range(4)):
    tokens, features = left.shape
    width = right.shape[1]
    rows = features // grid.count
    left_row = 4 if left_far.shape[0] != tokens else 0
    counts = piece_counts(grid.depth, spots)
    return pl.pallas_call(
        functools.partial(tiled_kernel, grid.depth, rows, spots),
        grid=(width // tile,),
        out_shape=[jax.ShapeDtypeStruct((n, rows, width), jnp.bfloat16) for n in counts],
        in_specs=[
            pl.BlockSpec(memory_space=pltpu.SMEM),
            pl.BlockSpec((tokens, features), lambda j: (0, 0)),
            pl.BlockSpec((tokens, features), lambda j: (left_row, 0)),
        ]
        + [pl.BlockSpec((tokens, tile), lambda j: (0, j))] * 2,
        out_specs=[pl.BlockSpec((n, rows, tile), lambda j: (0, 0, j)) for n in counts],
        scratch_shapes=[pltpu.VMEM((len(spots), grid.depth * rows, 2 * tokens), jnp.bfloat16)],
        compiler_params=pltpu.CompilerParams(vmem_limit_bytes=40 * 2**20),
        cost_estimate=pl.CostEstimate(flops=1, bytes_accessed=1, transcendentals=0),
        name="terms",
    )(place, left, left_far, right, right_far)


def group_terms(grid, place, held, held_far, right, right_far, pairs):
    by_core = right_far is None
    width = held.shape[1]
    rows = width // grid.count
    arrays, specs = [], []
    for tokens, left_row, right_row in pairs:
        arrays += [held, held_far, right]
        specs += [pl.BlockSpec((tokens, width), lambda i, row=left_row: (row, 0))] * 2
        if by_core:
            specs += [pl.BlockSpec((2, tokens, width), lambda i, row=right_row: (0, row, 0))]
        else:
            arrays += [right_far]
            specs += [pl.BlockSpec((tokens, width), lambda i, row=right_row: (row, 0))] * 2
    most = max(tokens for tokens, _, _ in pairs)
    shapes = [(n, len(pairs), rows, width) for n in piece_counts(grid.depth)]
    return pl.pallas_call(
        functools.partial(group_kernel, grid.depth, rows, len(pairs), by_core),
        grid=(1,),
        out_shape=[jax.ShapeDtypeStruct(shape, jnp.bfloat16) for shape in shapes],
        in_specs=[pl.BlockSpec(memory_space=pltpu.SMEM)] + specs,
        out_specs=[pl.BlockSpec(shape, lambda i: (0, 0, 0, 0)) for shape in shapes],
        scratch_shapes=[pltpu.VMEM((4, grid.depth * rows, 2 * most), jnp.bfloat16)],
        compiler_params=pltpu.CompilerParams(vmem_limit_bytes=48 * 2**20),
        cost_estimate=pl.CostEstimate(flops=1, bytes_accessed=1, transcendentals=0),
        name="terms",
    )(place, *arrays)


def corner_added(grid, pieces, low, high):
    half = grid.depth // 2
    return pieces[1].at[:half].add(low), pieces[2].at[half:].add(high)


def plane_sum(own, over_x, over_y):
    wide = jnp.float32
    return (own.astype(wide) + over_x.astype(wide) + over_y.astype(wide)).astype(jnp.bfloat16)


def plane_sums(grid, pieces, over_x, over_y):
    half = grid.depth // 2
    return [
        plane_sum(pieces[0][part], over_x[part], over_y[part]) for part in (slice(0, half), slice(half, None))
    ]


def pair_sum(near, got):
    return (near[1].astype(jnp.float32) + got[1].astype(jnp.float32)).astype(jnp.bfloat16)


def total_of(*terms_of):
    return sum([term.astype(jnp.float32) for term in terms_of[1:]], terms_of[0].astype(jnp.float32))


def fetch(attention_rows, expand_rows, reduce_rows, norm_rows):
    gathered = (
        lax.all_gather(attention_rows, ("dp", "fsdp"), axis=1, tiled=True),
        lax.all_gather(expand_rows, ("dp", "fsdp"), axis=0, tiled=True),
        lax.all_gather(reduce_rows, ("dp", "fsdp"), axis=0, tiled=True),
        lax.all_gather(norm_rows, ("dp", "fsdp"), axis=1, tiled=True),
    )
    return gathered


def settle(attention_terms, expand_terms, reduce_terms, norm_terms):
    owned = (
        lax.psum_scatter(attention_terms, ("dp", "fsdp"), scatter_dimension=1, tiled=True),
        lax.psum_scatter(expand_terms, ("dp", "fsdp"), scatter_dimension=0, tiled=True),
        lax.psum_scatter(reduce_terms, ("dp", "fsdp"), scatter_dimension=0, tiled=True),
        lax.psum_scatter(norm_terms, ("dp", "fsdp"), scatter_dimension=1, tiled=True),
    )
    return owned


def matmul(left, right):
    return jnp.dot(left, right, preferred_element_type=jnp.float32)


def across(left, right):
    return jnp.einsum("ti,tj->ij", left, right, preferred_element_type=jnp.float32)


def against(left, right):
    return jnp.einsum("ti,ji->tj", left, right, preferred_element_type=jnp.float32)


def gelu_tanh(values):
    return jax.nn.gelu(values, approximate=True)


def normalize(summed, gain, shift):
    center = jnp.mean(summed, axis=-1, keepdims=True)
    centred = summed - center
    inverse = lax.rsqrt(jnp.mean(centred * centred, axis=-1, keepdims=True) + EPSILON)
    scaled = centred * inverse
    return (scaled * gain + shift, scaled, inverse)


def normalize_back(incoming, scaled, inverse, gain):
    spread = incoming * gain
    d_summed = inverse * (
        spread
        - jnp.mean(spread, axis=-1, keepdims=True)
        - scaled * jnp.mean(spread * scaled, axis=-1, keepdims=True)
    )
    return (d_summed, jnp.sum(incoming * scaled, axis=0), jnp.sum(incoming, axis=0))


def split_heads(matrix):
    return matrix.reshape(matrix.shape[0], HEADS, HEAD_DIM)


def scores_of(query_rows, key_rows, allowed):
    raw = jnp.einsum(
        "qhd,khd->hqk",
        split_heads(query_rows),
        split_heads(key_rows),
        preferred_element_type=jnp.float32,
    ) * HEAD_DIM ** (-0.5)
    return jnp.where(allowed[None], raw, NEGATIVE)


def attend_forward(query_rows, key_rows, value_rows, allowed):
    scores = scores_of(query_rows, key_rows, allowed)
    highest = jnp.max(scores, axis=-1, keepdims=True)
    weights = jnp.exp(scores - highest)
    totals = jnp.sum(weights, axis=-1, keepdims=True)
    chances = (weights / totals).astype(jnp.bfloat16)
    context = jnp.einsum(
        "hqk,khd->qhd", chances, split_heads(value_rows), preferred_element_type=jnp.float32
    )
    return (
        context.reshape(query_rows.shape[0], HEADS * HEAD_DIM).astype(jnp.bfloat16),
        highest + jnp.log(totals),
    )


def attend_back(query_rows, key_rows, value_rows, allowed, logsum, d_context):
    query_heads = split_heads(query_rows)
    key_heads = split_heads(key_rows)
    d_heads = split_heads(d_context)
    chances = jnp.exp(scores_of(query_rows, key_rows, allowed) - logsum)
    d_chances = jnp.einsum(
        "qhd,khd->hqk", d_heads, split_heads(value_rows), preferred_element_type=jnp.float32
    )
    d_value = jnp.einsum(
        "hqk,qhd->khd", chances.astype(jnp.bfloat16), d_heads, preferred_element_type=jnp.float32
    )
    centre = jnp.sum(d_chances * chances, axis=-1, keepdims=True)
    d_scores = (chances * (d_chances - centre)).astype(jnp.bfloat16)
    d_query = jnp.einsum(
        "hqk,khd->qhd", d_scores, key_heads, preferred_element_type=jnp.float32
    ) * HEAD_DIM ** (-0.5)
    d_key = jnp.einsum(
        "hqk,qhd->khd", d_scores, query_heads, preferred_element_type=jnp.float32
    ) * HEAD_DIM ** (-0.5)
    query_count = query_rows.shape[0]
    key_count = key_rows.shape[0]
    return (
        d_query.reshape(query_count, HEADS * HEAD_DIM).astype(jnp.bfloat16),
        d_key.reshape(key_count, HEADS * HEAD_DIM).astype(jnp.bfloat16),
        d_value.reshape(key_count, HEADS * HEAD_DIM).astype(jnp.bfloat16),
    )


def plain_device(
    tokens,
    memory,
    target_segments,
    source_segments,
    self_query,
    self_key,
    self_value,
    self_output,
    cross_query,
    cross_key,
    cross_value,
    cross_output,
    expand_weight,
    reduce_weight,
    self_gain,
    self_shift,
    cross_gain,
    cross_shift,
    final_gain,
    final_shift,
    output_grad,
):
    attention_rows = jnp.stack(
        [
            self_query,
            self_key,
            self_value,
            self_output,
            cross_query,
            cross_key,
            cross_value,
            cross_output,
        ]
    )
    norm_rows = jnp.stack([self_gain, self_shift, cross_gain, cross_shift, final_gain, final_shift])
    matrices, expand_full, reduce_full, norm_full = fetch(
        attention_rows, expand_weight, reduce_weight, norm_rows
    )
    gains = norm_full.astype(jnp.float32)
    target_ids = target_segments[0]
    source_ids = source_segments[0]
    positions = lax.iota(jnp.int32, tokens.shape[0])
    causal = (target_ids[:, None] == target_ids[None, :]) & (
        positions[None, :] <= positions[:, None]
    )
    crossing = target_ids[:, None] == source_ids[None, :]
    query_one = matmul(tokens, matrices[0]).astype(jnp.bfloat16)
    key_one = matmul(tokens, matrices[1]).astype(jnp.bfloat16)
    value_one = matmul(tokens, matrices[2]).astype(jnp.bfloat16)
    context_one, logsum_one = attend_forward(query_one, key_one, value_one, causal)
    branch_one = matmul(context_one, matrices[3])
    first, first_scaled, first_inverse = normalize(
        RESIDUAL_SCALE * tokens.astype(jnp.float32) + branch_one, gains[0], gains[1]
    )
    first_low = first.astype(jnp.bfloat16)
    query_two = matmul(first_low, matrices[4]).astype(jnp.bfloat16)
    key_two = matmul(memory, matrices[5]).astype(jnp.bfloat16)
    value_two = matmul(memory, matrices[6]).astype(jnp.bfloat16)
    context_two, logsum_two = attend_forward(query_two, key_two, value_two, crossing)
    branch_two = matmul(context_two, matrices[7])
    second, second_scaled, second_inverse = normalize(
        RESIDUAL_SCALE * first + branch_two, gains[2], gains[3]
    )
    second_low = second.astype(jnp.bfloat16)
    inner = matmul(second_low, expand_full)
    active = gelu_tanh(inner).astype(jnp.bfloat16)
    branch_three = matmul(active, reduce_full)
    final, final_scaled, final_inverse = normalize(
        RESIDUAL_SCALE * second + branch_three, gains[4], gains[5]
    )
    output = final.astype(jnp.bfloat16)
    matrices, expand_full, reduce_full, norm_full = fetch(
        attention_rows, expand_weight, reduce_weight, norm_rows
    )
    gains = norm_full.astype(jnp.float32)
    d_sum_three, final_gain_term, final_shift_term = normalize_back(
        output_grad.astype(jnp.float32), final_scaled, final_inverse, gains[4]
    )
    d_branch_three = d_sum_three.astype(jnp.bfloat16)
    reduce_term = across(active, d_branch_three)
    d_active = against(d_branch_three, reduce_full)
    d_inner = jax.vjp(gelu_tanh, inner)[1](d_active)[0].astype(jnp.bfloat16)
    expand_term = across(second_low, d_inner)
    d_second = RESIDUAL_SCALE * d_sum_three + against(d_inner, expand_full)
    d_sum_two, cross_gain_term, cross_shift_term = normalize_back(
        d_second, second_scaled, second_inverse, gains[2]
    )
    d_branch_two = d_sum_two.astype(jnp.bfloat16)
    cross_output_term = across(context_two, d_branch_two)
    d_context_two = against(d_branch_two, matrices[7]).astype(jnp.bfloat16)
    d_query_two, d_key_two, d_value_two = attend_back(
        query_two, key_two, value_two, crossing, logsum_two, d_context_two
    )
    cross_query_term = across(first_low, d_query_two)
    cross_key_term = across(memory, d_key_two)
    cross_value_term = across(memory, d_value_two)
    memory_grad = against(d_key_two, matrices[5]) + against(d_value_two, matrices[6])
    d_first = RESIDUAL_SCALE * d_sum_two + against(d_query_two, matrices[4])
    d_sum_one, self_gain_term, self_shift_term = normalize_back(
        d_first, first_scaled, first_inverse, gains[0]
    )
    d_branch_one = d_sum_one.astype(jnp.bfloat16)
    self_output_term = across(context_one, d_branch_one)
    d_context_one = against(d_branch_one, matrices[3]).astype(jnp.bfloat16)
    d_query_one, d_key_one, d_value_one = attend_back(
        query_one, key_one, value_one, causal, logsum_one, d_context_one
    )
    self_query_term = across(tokens, d_query_one)
    self_key_term = across(tokens, d_key_one)
    self_value_term = across(tokens, d_value_one)
    tokens_grad = (
        RESIDUAL_SCALE * d_sum_one
        + against(d_query_one, matrices[0])
        + against(d_key_one, matrices[1])
        + against(d_value_one, matrices[2])
    )
    attention_terms = jnp.stack(
        [
            self_query_term,
            self_key_term,
            self_value_term,
            self_output_term,
            cross_query_term,
            cross_key_term,
            cross_value_term,
            cross_output_term,
        ]
    )
    norm_terms = jnp.stack(
        [
            self_gain_term,
            self_shift_term,
            cross_gain_term,
            cross_shift_term,
            final_gain_term,
            final_shift_term,
        ]
    )
    attention_owned, expand_owned, reduce_owned, norm_owned = settle(
        attention_terms, expand_term, reduce_term, norm_terms
    )
    return (
        output,
        tokens_grad,
        memory_grad,
        attention_owned[0],
        attention_owned[1],
        attention_owned[2],
        attention_owned[3],
        attention_owned[4],
        attention_owned[5],
        attention_owned[6],
        attention_owned[7],
        expand_owned,
        reduce_owned,
        norm_owned[0],
        norm_owned[1],
        norm_owned[2],
        norm_owned[3],
        norm_owned[4],
        norm_owned[5],
    )


def per_device(
    grid,
    tokens,
    memory,
    target_segments,
    source_segments,
    self_query,
    self_key,
    self_value,
    self_output,
    cross_query,
    cross_key,
    cross_value,
    cross_output,
    expand_weight,
    reduce_weight,
    self_gain,
    self_shift,
    cross_gain,
    cross_shift,
    final_gain,
    final_shift,
    output_grad,
):
    if not grid.fast:
        return plain_device(
            tokens,
            memory,
            target_segments,
            source_segments,
            self_query,
            self_key,
            self_value,
            self_output,
            cross_query,
            cross_key,
            cross_value,
            cross_output,
            expand_weight,
            reduce_weight,
            self_gain,
            self_shift,
            cross_gain,
            cross_shift,
            final_gain,
            final_shift,
            output_grad,
        )
    place = grid.place()
    held_rows = self_gain.shape[0]
    norm_rows = jnp.stack([self_gain, self_shift, cross_gain, cross_shift, final_gain, final_shift])
    extra = jnp.zeros((16, held_rows * grid.count), jnp.bfloat16)
    extra = lax.dynamic_update_slice(extra, norm_rows, (0, grid.index() * held_rows))
    extra = extra.reshape(4, 32, 128)
    first_rows = jnp.concatenate([jnp.stack([self_query, self_key, self_value, self_output]), extra], axis=-1)
    second_rows = jnp.stack([cross_query, cross_key, cross_value, cross_output])
    target_column, target_row = target_segments.reshape(-1, 1), target_segments
    source_row = source_segments

    half = grid.depth // 2
    width = expand_weight.shape[1] // 4
    expand_rows = jnp.stack([expand_weight[:, n * width : (n + 1) * width] for n in range(4)])
    reduce_rows = reduce_weight.reshape(expand_rows.shape)

    first_z = [grid.move(first_rows, dz=k) for k in (2, 3, 1)]
    second_z = grid.move(second_rows, dz=1)
    first_own = jnp.stack([first_rows, first_z[2], first_z[0], first_z[1]])
    second_pair = jnp.stack([second_rows, second_z])
    first_own, second_pair, expand_rows, reduce_rows = after(
        (first_own, second_pair, expand_rows, reduce_rows)
    )
    first_x, first_y = grid.move(first_own, dx=1), grid.move(first_own, dy=1)
    second_z = grid.move(second_pair, dz=2)
    expand_z = grid.move(expand_rows, dz=1)
    reduce_z = grid.move(reduce_rows, dz=1)
    first_x, first_y, second_z, expand_z, reduce_z = after((first_x, first_y, second_z, expand_z, reduce_z))
    second_own = jnp.concatenate([second_pair, second_z])
    expand_pair = jnp.stack([expand_rows, expand_z])
    first_low, first_high, second_own, expand_pair = after(
        (first_x[:half], first_y[half:], second_own, expand_pair)
    )
    first_low, first_high = grid.move(first_low, dy=1), grid.move(first_high, dx=1)
    second_x, second_y = grid.move(second_own, dx=1), grid.move(second_own, dy=1)
    expand_z = grid.move(expand_pair, dz=2)
    first_low, first_high, second_x, second_y, expand_z = after(
        (first_low, first_high, second_x, second_y, expand_z)
    )
    reduce_pair = jnp.stack([reduce_rows, reduce_z])
    first_near = jnp.concatenate([first_own, first_x, first_y, first_low, first_high])
    sides = jnp.concatenate([second_own, second_x, second_y, expand_pair, expand_z])
    sent_y = jnp.concatenate([second_x[:half], expand_pair, expand_z])
    sent_x = jnp.concatenate([second_y[half:], expand_pair, expand_z])
    sent_x, sent_y, reduce_pair, first_near, sides = after((sent_x, sent_y, reduce_pair, first_near, sides))
    got_x, got_y = grid.move(sent_x, dx=1), grid.move(sent_y, dy=1)
    reduce_z = grid.move(reduce_pair, dz=2)
    first_far = grid.move(first_near, dc=1)
    sides_far = grid.move(sides, dc=1)
    first_out = self_forward(grid, place, tokens, target_column, target_row, (first_near, first_far))
    first_out, got_x, got_y, reduce_z, sides_far = after((first_out, got_x, got_y, reduce_z, sides_far))
    first_full, gains, query_one, key_one, value_one, context_one, logsum_one = first_out[:7]
    first, first_low, first_scaled, first_inverse = first_out[7:]
    reduce_own = jnp.concatenate([reduce_pair, reduce_z])
    sent_y = jnp.concatenate([got_x[half : 2 * half], reduce_pair, reduce_z])
    sent_x = jnp.concatenate([got_y[2 * half :], reduce_pair, reduce_z])
    sent_x, sent_y, got_x, got_y, reduce_own = after((sent_x, sent_y, got_x, got_y, reduce_own))
    last_x, last_y = grid.move(sent_x, dx=1), grid.move(sent_y, dy=1)
    got_x_far, got_y_far = grid.move(got_x, dc=1), grid.move(got_y, dc=1)
    reduce_own_far = grid.move(reduce_own, dc=1)
    second_out = cross_forward(
        grid, place, first, first_low, memory, gains, target_column, source_row,
        (sides, got_y, got_x, sides_far, got_y_far, got_x_far),
    )
    second_out, last_x, last_y, reduce_own_far = after((second_out, last_x, last_y, reduce_own_far))
    second_full, query_two, key_two, value_two, context_two, logsum_two = second_out[:6]
    second, second_low, second_scaled, second_inverse = second_out[6:]
    reduce_low, reduce_high, last_x, last_y = after(
        (last_x[half : 2 * half], last_y[2 * half :], last_x, last_y)
    )
    reduce_low, reduce_high = grid.move(reduce_low, dy=1), grid.move(reduce_high, dx=1)
    last_x_far, last_y_far = grid.move(last_x, dc=1), grid.move(last_y, dc=1)
    expand_full, active, slope = expand_forward(
        grid, place, second_low,
        (sides, got_x, got_y, last_y, last_x, sides_far, got_x_far, got_y_far, last_y_far, last_x_far),
    )
    held = jnp.concatenate([tokens, context_one, first_low, context_two, second_low, memory])
    held, active = after((held, active))
    held_far = grid.move(held, dc=1)
    active_far = grid.move(active, dc=1)
    reduce_low, reduce_high, active = after((reduce_low, reduce_high, active))
    reduce_corner, active = after((jnp.concatenate([reduce_low, reduce_high]), active))
    reduce_corner_far = grid.move(reduce_corner, dc=1)
    partial = reduce_first(
        grid, place, active, (reduce_own, last_x, last_y, reduce_own_far, last_x_far, last_y_far)
    )
    reduce_pieces = (
        reduce_own, last_x, last_y, reduce_corner, reduce_own_far, last_x_far, last_y_far, reduce_corner_far
    )
    reduce_corner = (reduce_corner, reduce_corner_far)
    output, d_sum_three, d_branch_three, final_norm_terms = reduce_finish(
        grid, place, active, partial, second, gains, output_grad, reduce_corner
    )
    d_branches = (d_branch_three, grid.move(d_branch_three, dc=1))
    reduce_low, reduce_high = after(
        tuple(tiled_terms(grid, place, active, active_far, *d_branches, 1024, (3,)))
    )
    reduce_terms = tiled_terms(
        grid, place, after(active, reduce_low), active_far, *d_branches, 512, (0, 1, 2)
    )
    d_inner = reduce_back(grid, place, after(d_branch_three, *reduce_terms), slope, reduce_pieces)
    reduce_low, reduce_high = grid.move(reduce_low, dy=1), grid.move(reduce_high, dx=1)
    reduce_low, reduce_high, d_inner = after((reduce_low, reduce_high, d_inner))
    reduce_sends = corner_added(grid, reduce_terms, reduce_low, reduce_high)
    reduce_sends, d_inner = after((reduce_sends, d_inner))
    reduce_x, reduce_y = grid.move(reduce_sends[0], dx=1), grid.move(reduce_sends[1], dy=1)
    d_inner_far = grid.move(d_inner, dc=1)
    d_sum_two, d_branch_two, d_context_two, cross_norm_terms = expand_back(
        d_inner, expand_full, d_sum_three, second_scaled, second_inverse, gains, second_full
    )
    expand_terms = tiled_terms(grid, place, second_low, held_far, after(d_inner, d_context_two), d_inner_far, 1024)
    expand_terms, d_context_two = after((expand_terms, d_context_two))
    expand_low, expand_high = grid.move(expand_terms[3], dy=1), grid.move(expand_terms[4], dx=1)
    back, d_sum_one, d_context_one, self_norm_terms = cross_back(
        query_two, key_two, value_two, logsum_two, d_context_two, target_column,
        source_row, d_branch_two, d_sum_two, first_scaled, first_inverse, gains, second_full, first_full,
    )
    norm_terms = jnp.concatenate([self_norm_terms, cross_norm_terms, final_norm_terms])
    expand_low, expand_high, reduce_x, reduce_y, back, norm_terms = after(
        (expand_low, expand_high, reduce_x, reduce_y, back, norm_terms)
    )
    expand_sends = corner_added(grid, expand_terms, expand_low, expand_high)
    expand_sends, back = after((expand_sends, back))
    expand_x, expand_y = grid.move(expand_sends[0], dx=1), grid.move(expand_sends[1], dy=1)
    reduce_near, reduce_pass = plane_sums(grid, reduce_terms, *after((reduce_x, reduce_y), expand_sends))
    reduce_near, reduce_pass, back = after((reduce_near, reduce_pass, back))
    reduce_got = grid.move(reduce_pass, dz=2)
    backs = grid.cores(back)
    pairs = [(256, 1, 2), (256, 2, 1), (128, 10, 6), (128, 10, 7), (256, 3, 0)]
    cross_terms = group_terms(grid, place, held, held_far, backs, None, pairs)
    cross_terms, d_context_one = after((cross_terms, d_context_one))
    cross_low, cross_high = grid.move(cross_terms[3], dy=1), grid.move(cross_terms[4], dx=1)
    back_one = self_back(
        query_one, key_one, value_one, logsum_one, d_context_one, target_column, target_row
    )
    cross_low, cross_high, back_one, reduce_got, expand_x, expand_y = after(
        (cross_low, cross_high, back_one, reduce_got, expand_x, expand_y)
    )
    cross_sends = corner_added(grid, cross_terms, cross_low, cross_high)
    reduce_leaving = pair_sum(reduce_near, reduce_got)
    cross_sends, back_one, reduce_leaving = after((cross_sends, back_one, reduce_leaving))
    cross_x, cross_y = grid.move(cross_sends[0], dx=1), grid.move(cross_sends[1], dy=1)
    back_one_far = grid.move(back_one, dc=1)
    reduce_last = grid.move(reduce_leaving, dz=1)
    expand_near, expand_pass = plane_sums(grid, expand_terms, *after((expand_x, expand_y), cross_sends))
    expand_near, expand_pass, back_one = after((expand_near, expand_pass, back_one))
    expand_got = grid.move(expand_pass, dz=2)
    self_terms = group_terms(
        grid, place, held, held_far, back_one, back_one_far, [(256, 0, n) for n in range(3)]
    )
    tokens_grad, memory_grad = inputs_back(
        after(back_one, *self_terms), back, d_sum_one, first_full, second_full
    )
    expand_got, reduce_last, self_low, self_high = after(
        (expand_got, reduce_last, self_terms[3], self_terms[4]), tokens_grad
    )
    expand_leaving = pair_sum(expand_near, expand_got)
    self_low, self_high, expand_leaving = after((self_low, self_high, expand_leaving))
    self_low, self_high = grid.move(self_low, dy=1), grid.move(self_high, dx=1)
    expand_last = grid.move(expand_leaving, dz=1)
    cross_x, cross_y = after((cross_x, cross_y), expand_leaving)
    cross_near, cross_pass = plane_sums(grid, cross_terms, cross_x, cross_y)
    cross_near, cross_pass = after((cross_near, cross_pass))
    cross_got = grid.move(cross_pass, dz=2)
    self_low, self_high, expand_last = after((self_low, self_high, expand_last), cross_pass)
    self_sends = corner_added(grid, self_terms, self_low, self_high)
    self_sends, norm_terms = after((self_sends, norm_terms))
    self_x, self_y = grid.move(self_sends[0], dx=1), grid.move(self_sends[1], dy=1)
    norm_got = lax.all_to_all(norm_terms.reshape(6, grid.count, held_rows), grid.axes, 1, 0, tiled=True)
    cross_got, norm_got, self_x, self_y = after((cross_got, norm_got, self_x, self_y))
    self_column = [plane_sum(self_terms[0][k], self_x[k], self_y[k]) for k in range(grid.depth)]
    cross_leaving = pair_sum(cross_near, cross_got)
    self_column, cross_leaving = after((self_column, cross_leaving))
    self_others = [grid.move(self_column[k], dz=k) for k in (2, 3, 1)]
    cross_last = grid.move(cross_leaving, dz=1)
    reduce_term = total_of(reduce_near[0], reduce_got[0], reduce_last)
    expand_term = total_of(expand_near[0], expand_got[0], expand_last)
    cross_owned = total_of(cross_near[0], cross_got[0], cross_last)
    self_owned = total_of(self_column[0], *self_others)
    norm_owned = jnp.sum(norm_got.reshape(grid.count, 6, held_rows), axis=0)
    return (
        output,
        tokens_grad,
        memory_grad,
        *[self_owned[i] for i in range(3)],
        *[cross_owned[i] for i in range(5)],
        expand_term,
        reduce_term,
        *[norm_owned[i] for i in range(6)],
    )


def solution(mesh):
    grid = Grid(mesh)
    rows = P(grid.axes, None)
    parts = P(grid.axes)
    return jax.shard_map(
        functools.partial(per_device, grid),
        mesh=grid.mesh,
        in_specs=(
            rows,
            rows,
            rows,
            rows,
            rows,
            rows,
            rows,
            rows,
            rows,
            rows,
            rows,
            rows,
            rows,
            rows,
            parts,
            parts,
            parts,
            parts,
            parts,
            parts,
            rows,
        ),
        out_specs=(
            rows,
            rows,
            rows,
            rows,
            rows,
            rows,
            rows,
            rows,
            rows,
            rows,
            rows,
            rows,
            rows,
            parts,
            parts,
            parts,
            parts,
            parts,
            parts,
        ),
        check_vma=False,
    )
```

```python
import functools

import jax
import jax.numpy as jnp
from jax import lax
from jax.experimental import pallas as pl
from jax.experimental.pallas import tpu as pltpu
from jax.sharding import PartitionSpec as P

HEADS = 16
HEAD_DIM = 64


RESIDUAL_SCALE = 300.0**0.25
EPSILON = 1e-05
NEGATIVE = -1e30
ALL = ("dp", "fsdp")


class Grid:
    def __init__(self, mesh):
        self.depth = mesh.shape["dp"] // 2
        self.count = mesh.size
        self.fast = mesh.shape["fsdp"] == 4 and mesh.shape["dp"] == 8
        self.axes = ("z", "core", "y", "x") if self.fast else ALL
        self.mesh = mesh
        if self.fast:
            self.mesh = jax.sharding.Mesh(mesh.devices.reshape(4, 2, 2, 2), self.axes)

    def place(self):
        return jnp.stack([lax.axis_index(axis) for axis in self.axes]).astype(jnp.int32)

    def index(self):
        return lax.axis_index(self.axes)

    def move(self, value, dz=0, dc=0, dy=0, dx=0):
        offset = ((dz * 2 + dc) * 2 + dy) * 2 + dx
        return lax.ppermute(value, self.axes, [(index ^ offset, index) for index in range(self.count)])

    def cores(self, twice):
        return lax.all_to_all(twice, "core", 0, 0, tiled=True)


def after(value, *others):
    return lax.optimization_barrier((value,) + others)[0]


def wide_dot(left, right):
    return jnp.dot(left, right, preferred_element_type=jnp.float32)


def dot_rows(left, right):
    return lax.dot_general(left, right, (((1,), (1,)), ((), ())), preferred_element_type=jnp.float32)


def dot_columns(left, right):
    return lax.dot_general(left, right, (((0,), (0,)), ((), ())), preferred_element_type=jnp.float32)


def whole_call(body, name, inputs, shapes, scratch=(), limit=56):
    arrays, specs = [], []
    for item in inputs:
        if not isinstance(item, tuple):
            item = (item, item.shape, (0,) * item.ndim)
        arrays.append(item[0])
        if len(item) == 2:
            specs.append(pl.BlockSpec(memory_space=item[1]))
        else:
            specs.append(pl.BlockSpec(item[1], lambda i, index=item[2]: index))
    outs, out_specs = [], []
    for item in shapes:
        outs.append(jax.ShapeDtypeStruct(item[0], item[1]))
        if len(item) == 3:
            out_specs.append(pl.BlockSpec(memory_space=item[2]))
        else:
            out_specs.append(pl.BlockSpec(item[0], lambda i, rank=len(item[0]): (0,) * rank))
    return pl.pallas_call(
        body,
        grid=(1,),
        out_shape=outs,
        in_specs=specs,
        out_specs=out_specs,
        scratch_shapes=list(scratch),
        compiler_params=pltpu.CompilerParams(vmem_limit_bytes=limit * 2**20),
        cost_estimate=pl.CostEstimate(flops=1, bytes_accessed=1, transcendentals=0),
        name=name,
    )(*arrays)


def in_two(depth, pieces, dc, side, k):
    return pieces[dc], side * depth + k


def in_rest(base):
    def locate(depth, pieces, dc, side, k):
        half = depth // 2
        own, over_x, over_y, low, high = pieces[5 * dc : 5 * dc + 5]
        if side == 0:
            return own, base + k
        if side < 3:
            return (over_x, over_y)[side - 1], half + k
        return (low, k) if k < half else (high, k - half)

    return locate


def in_last(depth, pieces, dc, side, k):
    own, over_x, over_y, corner = pieces[4 * dc : 4 * dc + 4]
    return (own, over_x, over_y, corner)[side], depth // 2 + k if side in (1, 2) else k


def in_second(depth, pieces, dc, side, k):
    half = depth // 2
    sides, low, high = pieces[3 * dc : 3 * dc + 3]
    if side < 3:
        return sides, side * depth + k
    return (low, k) if k < half else (high, k - half)


def arrivals_of(depth, rows, place, locate, pieces, held, sems, held_norms=None, these=range(8), blocks=0):
    z, c, y, x = place[0], place[1], place[2], place[3]
    width = held.shape[-1]
    arrivals = []
    for k in range(depth):
        column = []
        for n in these:
            dc, dy, dx = n // 4, n // 2 % 2, n % 2
            piece, spot = locate(depth, pieces, dc, n % 4, k)
            owner = (((z ^ k) * 2 + (c ^ dc)) * 2 + (y ^ dy)) * 2 + (x ^ dx)
            if blocks:
                target = held.at[pl.ds(owner * blocks, blocks)]
            else:
                target = held.at[..., pl.ds(pl.multiple_of(owner * rows, rows), rows), :]
            source = piece.at[spot]
            order = k * 8 + n
            if held_norms is None:
                column.append(pltpu.make_async_copy(source, target, sems.at[order]))
            else:
                column.append(pltpu.make_async_copy(source.at[..., :width], target, sems.at[order]))
                column.append(
                    pltpu.make_async_copy(
                        source.at[0:2, :, pl.ds(width, 128)],
                        held_norms.at[owner],
                        sems.at[8 * depth + order],
                    )
                )
        for copy in column:
            copy.start()
        arrivals.append(column)
    return arrivals


def pass_on(depth, rows, place, arrivals, held, whole, sems):
    leaving = []
    for k in range(depth):
        for copy in arrivals[k]:
            copy.wait()
        spot = pl.ds(pl.multiple_of((place[0] ^ k) * (8 * rows), 8 * rows), 8 * rows)
        leaving.append(pltpu.make_async_copy(held.at[..., spot, :], whole.at[..., spot, :], sems.at[k]))
        leaving[k].start()
    return leaving


def norm_rows_of(summed, gain, shift):
    center = jnp.mean(summed, axis=-1, keepdims=True)
    centred = summed - center
    inverse = lax.rsqrt(jnp.mean(centred * centred, axis=-1, keepdims=True) + EPSILON)
    scaled = centred * inverse
    return scaled * gain + shift, scaled, inverse


def norm_rows_back(incoming, scaled, inverse, gain):
    spread_out = incoming * gain
    d_summed = inverse * (
        spread_out
        - jnp.mean(spread_out, axis=-1, keepdims=True)
        - scaled * jnp.mean(spread_out * scaled, axis=-1, keepdims=True)
    )
    return d_summed, jnp.sum(incoming * scaled, axis=0, keepdims=True), jnp.sum(incoming, axis=0, keepdims=True)


def head_halves():
    lane = lax.broadcasted_iota(jnp.int32, (1, 2 * HEAD_DIM), 1)
    return [
        jnp.where(lane < HEAD_DIM, 1.0, 0.0).astype(jnp.bfloat16),
        jnp.where(lane < HEAD_DIM, 0.0, 1.0).astype(jnp.bfloat16),
    ]


def attend_heads(query, key, value, allowed, context, logsum):
    halves = head_halves()
    lane = lax.broadcasted_iota(jnp.int32, logsum.shape, 1)
    logsum[...] = jnp.zeros_like(logsum)

    def pair(p, carry):
        lanes = pl.ds(pl.multiple_of(p * 2 * HEAD_DIM, 2 * HEAD_DIM), 2 * HEAD_DIM)
        queries, keys, values = query[:, lanes], key[:, lanes], value[:, lanes]
        total = None
        for side, half in enumerate(halves):
            scores = dot_rows(queries * half, keys) * HEAD_DIM ** (-0.5)
            scores = jnp.where(allowed[...] > 0, scores, NEGATIVE)
            highest = jnp.max(scores, axis=-1, keepdims=True)
            weights = jnp.exp(scores - highest)
            totals = jnp.sum(weights, axis=-1, keepdims=True)
            chances = (weights * (1.0 / totals)).astype(jnp.bfloat16)
            part = wide_dot(chances, values * half)
            total = part if total is None else total + part
            logsum[...] = jnp.where(lane == 2 * p + side, highest + jnp.log(totals), logsum[...])
        context[:, lanes] = total.astype(jnp.bfloat16)
        return carry

    lax.fori_loop(0, HEADS // 2, pair, 0)


def attend_heads_back(query, key, value, allowed, logsum, d_context, d_query, d_key, d_value):
    halves = head_halves()
    lane = lax.broadcasted_iota(jnp.int32, logsum.shape, 1)
    scale = HEAD_DIM ** (-0.5)

    def pair(p, carry):
        lanes = pl.ds(pl.multiple_of(p * 2 * HEAD_DIM, 2 * HEAD_DIM), 2 * HEAD_DIM)
        queries, keys, values, d_outs = query[:, lanes], key[:, lanes], value[:, lanes], d_context[:, lanes]
        sums = [None, None, None]
        for side, half in enumerate(halves):
            own_sum = jnp.sum(jnp.where(lane == 2 * p + side, logsum[...], 0.0), axis=-1, keepdims=True)
            own_queries, own_outs = queries * half, d_outs * half
            scores = dot_rows(own_queries, keys) * scale
            scores = jnp.where(allowed[...] > 0, scores, NEGATIVE)
            chances = jnp.exp(scores - own_sum)
            d_chances = dot_rows(own_outs, values)
            centre = jnp.sum(d_chances * chances, axis=-1, keepdims=True)
            d_scores = (chances * (d_chances - centre)).astype(jnp.bfloat16)
            parts = (
                wide_dot(d_scores, keys * half),
                dot_columns(d_scores, own_queries),
                dot_columns(chances.astype(jnp.bfloat16), own_outs),
            )
            sums = [part if old is None else old + part for old, part in zip(sums, parts)]
        d_query[:, lanes] = (sums[0] * scale).astype(jnp.bfloat16)
        d_key[:, lanes] = (sums[1] * scale).astype(jnp.bfloat16)
        d_value[:, lanes] = sums[2].astype(jnp.bfloat16)
        return carry

    lax.fori_loop(0, HEADS // 2, pair, 0)


def self_allowed(ids_column, ids_row, allowed):
    rows, columns = allowed.shape
    later = lax.broadcasted_iota(jnp.int32, (rows, columns), 0) >= lax.broadcasted_iota(
        jnp.int32, (rows, columns), 1
    )
    same = ids_column[...] == ids_row[...]
    allowed[...] = jnp.where(later & same, 1.0, 0.0)


def cross_allowed(ids_column, ids_row, allowed):
    allowed[...] = jnp.where(ids_column[...] == ids_row[...], 1.0, 0.0)


def self_forward_kernel(depth, rows, place, tokens, ids_column, ids_row, *refs):
    pieces, refs = refs[:2], refs[2:]
    whole, gains, query, key, value, context, logsum, first, first_low, scaled, inverse = refs[:11]
    held, held_norms, allowed, in_sems, out_sems = refs[11:]
    arrivals = arrivals_of(depth, rows, place, in_two, pieces, held, in_sems, held_norms)
    self_allowed(ids_column, ids_row, allowed)
    leaving = pass_on(depth, rows, place, arrivals, held, whole, out_sems)
    packed = held_norms[0].astype(jnp.float32)
    for owner in range(1, 8 * depth):
        packed += held_norms[owner].astype(jnp.float32)
    gains[...] = jnp.zeros_like(gains)
    for n in range(6):
        for j in range(8):
            r = n * 8 + j
            gains[n : n + 1, j * 128 : (j + 1) * 128] = packed[r // rows, r % rows : r % rows + 1, :]
    for n, out in enumerate((query, key, value)):
        out[...] = wide_dot(tokens[...], held[n]).astype(jnp.bfloat16)
    attend_heads(query, key, value, allowed, context, logsum)
    branch = wide_dot(context[...], held[3])
    summed = RESIDUAL_SCALE * tokens[...].astype(jnp.float32) + branch
    first[...], scaled[...], inverse[...] = norm_rows_of(summed, gains[0:1, :], gains[1:2, :])
    first_low[...] = first[...].astype(jnp.bfloat16)
    for copy in leaving:
        copy.wait()


def self_forward(grid, place, tokens, ids_column, ids_row, pieces):
    count, width = tokens.shape
    rows = pieces[0].shape[2]
    low, full = jnp.bfloat16, jnp.float32
    shape = (count, width)
    return whole_call(
        functools.partial(self_forward_kernel, grid.depth, rows),
        "self_forward",
        [(place, pltpu.SMEM), tokens, ids_column, ids_row] + [(piece, pl.ANY) for piece in pieces],
        [((4, width, width), low, pl.ANY), ((8, width), full)]
        + [(shape, low)] * 4
        + [((count, 128), full), (shape, full), (shape, low), (shape, full), ((count, 1), full)],
        [
            pltpu.VMEM((4, width, width), low),
            pltpu.VMEM((grid.count, 2, rows, 128), low),
            pltpu.VMEM((count, count), full),
            pltpu.SemaphoreType.DMA((2 * grid.count,)),
            pltpu.SemaphoreType.DMA((grid.depth,)),
        ],
    )


def cross_forward_kernel(depth, rows, place, first, first_low, memory, gains, ids_column, ids_row, *refs):
    pieces, refs = refs[:6], refs[6:]
    whole, query, key, value, context, logsum, second, second_low, scaled, inverse = refs[:10]
    held, allowed, in_sems, out_sems = refs[10:]
    arrivals = arrivals_of(depth, rows, place, in_second, pieces, held, in_sems)
    cross_allowed(ids_column, ids_row, allowed)
    leaving = pass_on(depth, rows, place, arrivals, held, whole, out_sems)
    query[...] = wide_dot(first_low[...], held[0]).astype(jnp.bfloat16)
    key[...] = wide_dot(memory[...], held[1]).astype(jnp.bfloat16)
    value[...] = wide_dot(memory[...], held[2]).astype(jnp.bfloat16)
    attend_heads(query, key, value, allowed, context, logsum)
    summed = RESIDUAL_SCALE * first[...] + wide_dot(context[...], held[3])
    second[...], scaled[...], inverse[...] = norm_rows_of(summed, gains[2:3, :], gains[3:4, :])
    second_low[...] = second[...].astype(jnp.bfloat16)
    for copy in leaving:
        copy.wait()


def cross_forward(grid, place, first, first_low, memory, gains, ids_column, ids_row, pieces):
    count, width = first.shape
    others = memory.shape[0]
    rows = pieces[0].shape[2]
    low, full = jnp.bfloat16, jnp.float32
    shape, other_shape = (count, width), (others, width)
    return whole_call(
        functools.partial(cross_forward_kernel, grid.depth, rows),
        "cross_forward",
        [(place, pltpu.SMEM), first, first_low, memory, gains, ids_column, ids_row]
        + [(piece, pl.ANY) for piece in pieces],
        [((4, width, width), low, pl.ANY), (shape, low), (other_shape, low), (other_shape, low), (shape, low)]
        + [((count, 128), full), (shape, full), (shape, low), (shape, full), ((count, 1), full)],
        [
            pltpu.VMEM((4, width, width), low),
            pltpu.VMEM((count, others), full),
            pltpu.SemaphoreType.DMA((grid.count,)),
            pltpu.SemaphoreType.DMA((grid.depth,)),
        ],
    )


TANH_SCALE = 0.7978845608028654
TANH_CUBE = 0.044715


def expand_forward_kernel(depth, rows, place, second_low, *refs):
    pieces, refs = refs[:10], refs[10:]
    whole, active, slope, held, in_sems, out_sems = refs
    arrivals = arrivals_of(depth, rows, place, in_rest(3 * depth), pieces, held, in_sems)
    leaving = pass_on(depth, rows, place, arrivals, held, whole, out_sems)
    left = second_low[...]
    block = held.shape[2]

    def tile(j, carry):
        for part in range(block // 512):
            lanes = pl.ds(pl.multiple_of(j * block + part * 512, 512), 512)
            inner = wide_dot(left, held[j, :, part * 512 : (part + 1) * 512])
            square = inner * inner
            bend = jnp.tanh(TANH_SCALE * (inner * (1.0 + TANH_CUBE * square)))
            half = 0.5 + 0.5 * bend
            active[:, lanes] = (inner * half).astype(jnp.bfloat16)
            slope[:, lanes] = half + (0.5 * TANH_SCALE) * inner * (1.0 - bend * bend) * (
                1.0 + (3.0 * TANH_CUBE) * square
            )
        return carry

    lax.fori_loop(0, held.shape[0], tile, 0)
    for copy in leaving:
        copy.wait()


def expand_forward(grid, place, second_low, pieces):
    count, width = second_low.shape
    blocks, rows, block = pieces[0].shape[1:]
    hidden = blocks * block
    low = jnp.bfloat16
    return whole_call(
        functools.partial(expand_forward_kernel, grid.depth, rows),
        "expand_forward",
        [(place, pltpu.SMEM), second_low] + [(piece, pl.ANY) for piece in pieces],
        [((blocks, width, block), low, pl.ANY), ((count, hidden), low), ((count, hidden), jnp.float32)],
        [
            pltpu.VMEM((blocks, width, block), low),
            pltpu.SemaphoreType.DMA((grid.count,)),
            pltpu.SemaphoreType.DMA((grid.depth,)),
        ],
    )


def rows_of(held):
    return held.reshape(held.shape[0] * held.shape[1], held.shape[2])


def reduce_first_kernel(depth, place, active, *refs):
    pieces, (partial, held, sems) = refs[:6], refs[6:]
    z, c, y, x = place[0], place[1], place[2], place[3]
    blocks, rows, width = pieces[0].shape[1:]

    def locate(depth, pieces, dc, side, k):
        return (pieces[3 * dc], k) if side == 0 else (pieces[3 * dc + side], depth // 2 + k)

    arrivals = arrivals_of(
        depth, rows, place, locate, pieces, held, sems, these=(0, 1, 2, 4, 5, 6), blocks=blocks
    )
    for there in range(depth):
        for core in range(2):
            owner = ((there * 2 + core) * 2 + (1 - y)) * 2 + (1 - x)
            held[pl.ds(owner * blocks, blocks)] = jnp.zeros((blocks, rows, width), held.dtype)
    span = 8 * blocks
    for k, column in enumerate(arrivals):
        for copy in column:
            copy.wait()
        there = z ^ k
        lanes = pl.ds(pl.multiple_of(there * (span * rows), span * rows), span * rows)
        part = wide_dot(active[:, lanes], rows_of(held[pl.ds(there * span, span)]))
        partial[...] = part if k == 0 else partial[...] + part


def reduce_first(grid, place, active, pieces):
    count, hidden = active.shape
    blocks, rows, width = pieces[0].shape[1:]
    return whole_call(
        functools.partial(reduce_first_kernel, grid.depth),
        "reduce_first",
        [(place, pltpu.SMEM), active] + [(piece, pl.ANY) for piece in pieces],
        [((count, width), jnp.float32)],
        [
            pltpu.VMEM((grid.count * blocks, rows, width), jnp.bfloat16),
            pltpu.SemaphoreType.DMA((grid.count,)),
        ],
    )[0]


def reduce_finish_kernel(depth, place, active, partial, second, gains, output_grad, *refs):
    corners, (output, d_summed, d_branch, norm_terms) = refs[:2], refs[2:]
    z, c, y, x = place[0], place[1], place[2], place[3]
    summed = RESIDUAL_SCALE * second[...] + partial[...]
    for k in range(depth):
        for dc in range(2):
            piece = rows_of(corners[dc][k])
            rows = piece.shape[0]
            owner = (((z ^ k) * 2 + (c ^ dc)) * 2 + (1 - y)) * 2 + (1 - x)
            summed += wide_dot(active[:, pl.ds(pl.multiple_of(owner * rows, rows), rows)], piece)
    final, scaled, inverse = norm_rows_of(summed, gains[4:5, :], gains[5:6, :])
    output[...] = final.astype(jnp.bfloat16)
    d_sum, norm_terms[0:1, :], norm_terms[1:2, :] = norm_rows_back(
        output_grad[...].astype(jnp.float32), scaled, inverse, gains[4:5, :]
    )
    d_summed[...] = d_sum
    d_branch[...] = d_sum.astype(jnp.bfloat16)


def reduce_finish(grid, place, active, partial, second, gains, output_grad, corners):
    shape = second.shape
    low, full = jnp.bfloat16, jnp.float32
    return whole_call(
        functools.partial(reduce_finish_kernel, grid.depth),
        "reduce_finish",
        [(place, pltpu.SMEM), active, partial, second, gains, output_grad, *corners],
        [(shape, low), (shape, full), (shape, low), ((2, shape[1]), full)],
    )


def reduce_back_kernel(depth, place, d_branch, slope, *refs):
    pieces, (d_inner, held, sems) = refs[:8], refs[8:]
    blocks, rows, width = pieces[0].shape[1:]
    arrivals = arrivals_of(depth, rows, place, in_last, pieces, held, sems, blocks=blocks)
    left = d_branch[...]
    step = 512 // rows
    tiles = 8 * blocks // step
    for k, column in enumerate(arrivals):
        for copy in column:
            copy.wait()
        for n in range(tiles):
            j = (place[0] ^ k) * tiles + n
            lanes = pl.ds(pl.multiple_of(j * 512, 512), 512)
            d_active = dot_rows(left, rows_of(held[pl.ds(j * step, step)]))
            d_inner[:, lanes] = (d_active * slope[:, lanes]).astype(jnp.bfloat16)


def reduce_back(grid, place, d_branch, slope, pieces):
    count, hidden = slope.shape
    blocks, rows, width = pieces[0].shape[1:]
    return whole_call(
        functools.partial(reduce_back_kernel, grid.depth),
        "reduce_back",
        [(place, pltpu.SMEM), d_branch, slope] + [(piece, pl.ANY) for piece in pieces],
        [((count, hidden), jnp.bfloat16)],
        [
            pltpu.VMEM((grid.count * blocks, rows, width), jnp.bfloat16),
            pltpu.SemaphoreType.DMA((grid.count,)),
        ],
    )[0]


def expand_back_kernel(d_inner, expand, d_sum_three, scaled, inverse, gains, out_weight, d_summed, d_branch, d_context, norm_terms):
    d_second = RESIDUAL_SCALE * d_sum_three[...]
    block = expand.shape[2]
    for n in range(expand.shape[0]):
        d_second += dot_rows(d_inner[:, n * block : (n + 1) * block], expand[n])
    d_sum, norm_terms[0:1, :], norm_terms[1:2, :] = norm_rows_back(
        d_second, scaled[...], inverse[...], gains[2:3, :]
    )
    d_summed[...] = d_sum
    d_branch[...] = d_sum.astype(jnp.bfloat16)
    d_context[...] = dot_rows(d_branch[...], out_weight[0]).astype(jnp.bfloat16)


def expand_back(d_inner, expand, d_sum_three, scaled, inverse, gains, second_full):
    shape = d_sum_three.shape
    width = shape[1]
    low, full = jnp.bfloat16, jnp.float32
    return whole_call(
        expand_back_kernel,
        "expand_back",
        [d_inner, expand, d_sum_three, scaled, inverse, gains]
        + [(second_full, (1, width, width), (3, 0, 0))],
        [(shape, full), (shape, low), (shape, low), ((2, width), full)],
    )


def cross_back_kernel(
    query, key, value, logsum, d_context, ids_column, ids_row, d_branch_two, d_sum_two, scaled, inverse, gains,
    query_weight, out_weight, back, d_summed, d_context_one, norm_terms, allowed,
):
    count, others = query.shape[0], key.shape[0]
    cross_allowed(ids_column, ids_row, allowed)
    rows = back.at[0]
    d_query = rows.at[count : 2 * count]
    d_key = rows.at[3 * count : 3 * count + others]
    d_value = rows.at[3 * count + others : 3 * count + 2 * others]
    attend_heads_back(query, key, value, allowed, logsum, d_context, d_query, d_key, d_value)
    d_first = RESIDUAL_SCALE * d_sum_two[...] + dot_rows(d_query[...], query_weight[0])
    d_sum, norm_terms[0:1, :], norm_terms[1:2, :] = norm_rows_back(
        d_first, scaled[...], inverse[...], gains[0:1, :]
    )
    d_summed[...] = d_sum
    d_branch = d_sum.astype(jnp.bfloat16)
    rows[0:count, :] = d_branch_two[...]
    rows[2 * count : 3 * count, :] = d_branch
    back[1] = rows[...]
    d_context_one[...] = dot_rows(d_branch, out_weight[0]).astype(jnp.bfloat16)


def cross_back(query, key, value, logsum, d_context, ids_column, ids_row, d_branch_two, d_sum_two, scaled, inverse, gains, second_full, first_full):
    shape, other_shape = query.shape, key.shape
    width = shape[1]
    low, full = jnp.bfloat16, jnp.float32
    block = (1, width, width)
    return whole_call(
        cross_back_kernel,
        "cross_back",
        [query, key, value, logsum, d_context, ids_column, ids_row, d_branch_two, d_sum_two, scaled, inverse, gains]
        + [(second_full, block, (0, 0, 0)), (first_full, block, (3, 0, 0))],
        [((2, 3 * shape[0] + 2 * other_shape[0], width), low), (shape, full), (shape, low), ((2, width), full)],
        [pltpu.VMEM((shape[0], other_shape[0]), full)],
    )


def self_back_kernel(query, key, value, logsum, d_context, ids_column, ids_row, d_rows, allowed):
    self_allowed(ids_column, ids_row, allowed)
    count = query.shape[0]
    outs = [d_rows.at[n * count : (n + 1) * count] for n in range(3)]
    attend_heads_back(query, key, value, allowed, logsum, d_context, *outs)


def self_back(query, key, value, logsum, d_context, ids_column, ids_row):
    count, width = query.shape
    return whole_call(
        self_back_kernel,
        "self_back",
        [query, key, value, logsum, d_context, ids_column, ids_row],
        [((3 * count, width), jnp.bfloat16)],
        [pltpu.VMEM((count, count), jnp.float32)],
    )[0]


def inputs_back_kernel(d_rows, d_key, d_value, d_sum_one, w_query, w_key, w_value, w_key_two, w_value_two, tokens_grad, memory_grad):
    count = d_sum_one.shape[0]
    total = RESIDUAL_SCALE * d_sum_one[...]
    for n, weight in enumerate((w_query, w_key, w_value)):
        total += dot_rows(d_rows[n * count : (n + 1) * count, :], weight[0])
    tokens_grad[...] = total
    memory_grad[...] = dot_rows(d_key[0], w_key_two[0]) + dot_rows(d_value[0], w_value_two[0])


def inputs_back(d_rows, back, d_sum_one, first_full, second_full):
    count, width = d_sum_one.shape
    others = (back.shape[1] - 3 * count) // 2
    first_row = 3 * count // others
    block = (1, width, width)
    return whole_call(
        inputs_back_kernel,
        "inputs_back",
        [d_rows]
        + [(back, (1, others, width), (0, first_row + n, 0)) for n in (0, 1)]
        + [d_sum_one]
        + [(first_full, block, (n, 0, 0)) for n in range(3)]
        + [(second_full, block, (n, 0, 0)) for n in (1, 2)],
        [((count, width), jnp.float32), ((others, width), jnp.float32)],
    )


def turn(depth, rows, place, sources, turned, spots=range(4)):
    z, c, y, x = place[0], place[1], place[2], place[3]
    tokens = sources[0].shape[0]
    for k in range(depth):
        there = z ^ k
        columns = pl.ds(pl.multiple_of((there * 2 + c) * (4 * rows), 4 * rows), 4 * rows)
        for side, source in enumerate(sources):
            block = source[:, columns].T
            named = [block[n * rows : (n + 1) * rows] for n in range(4)]
            named = [jnp.where(x == 0, named[n], named[n ^ 1]) for n in range(4)]
            named = [jnp.where(y == 0, named[n], named[n ^ 2]) for n in range(4)]
            for at, spot in enumerate(spots):
                turned[at, k * rows : (k + 1) * rows, side * tokens : (side + 1) * tokens] = named[spot]


def spread(depth, rows, turned, rights, outs, spots=range(4)):
    tokens = rights[0].shape[0]
    half = depth // 2
    for at, spot in enumerate(spots):
        part = turned[at]
        total = jnp.dot(part[:, :tokens], rights[0][...], preferred_element_type=jnp.float32)
        total += jnp.dot(
            part[:, tokens : 2 * tokens], rights[1][...], preferred_element_type=jnp.float32
        )
        total = total.astype(jnp.bfloat16).reshape(depth, rows, -1)
        if spot < 3:
            outs[at][...] = total
        else:
            outs[at][...] = total[:half]
            outs[at + 1][...] = total[half:]


def tiled_kernel(depth, rows, spots, place, left, left_far, right, right_far, *refs):
    outs, turned = refs[:-1], refs[-1]

    @pl.when(pl.program_id(0) == 0)
    def _():
        turn(depth, rows, place, (left, left_far), turned, spots)

    spread(depth, rows, turned, (right, right_far), outs, spots)


def group_kernel(depth, rows, count, by_core, place, *refs):
    each = 3 if by_core else 4
    core = place[1]
    inputs, outs, turned = refs[: each * count], refs[each * count : each * count + 5], refs[-1]
    for m in range(count):
        left, left_far, *rights = inputs[each * m : each * m + each]
        if by_core:
            rights = (rights[0].at[core], rights[0].at[1 - core])
        turn(depth, rows, place, (left, left_far), turned)
        spread(depth, rows, turned, rights, [out.at[:, m] for out in outs])


def piece_counts(depth, spots=range(4)):
    counts = []
    for spot in spots:
        counts += [depth] if spot < 3 else [depth // 2, depth // 2]
    return counts


def tiled_terms(grid, place, left, left_far, right, right_far, tile, spots=range(4)):
    tokens, features = left.shape
    width = right.shape[1]
    rows = features // grid.count
    left_row = 4 if left_far.shape[0] != tokens else 0
    counts = piece_counts(grid.depth, spots)
    return pl.pallas_call(
        functools.partial(tiled_kernel, grid.depth, rows, spots),
        grid=(width // tile,),
        out_shape=[jax.ShapeDtypeStruct((n, rows, width), jnp.bfloat16) for n in counts],
        in_specs=[
            pl.BlockSpec(memory_space=pltpu.SMEM),
            pl.BlockSpec((tokens, features), lambda j: (0, 0)),
            pl.BlockSpec((tokens, features), lambda j: (left_row, 0)),
        ]
        + [pl.BlockSpec((tokens, tile), lambda j: (0, j))] * 2,
        out_specs=[pl.BlockSpec((n, rows, tile), lambda j: (0, 0, j)) for n in counts],
        scratch_shapes=[pltpu.VMEM((len(spots), grid.depth * rows, 2 * tokens), jnp.bfloat16)],
        compiler_params=pltpu.CompilerParams(vmem_limit_bytes=40 * 2**20),
        cost_estimate=pl.CostEstimate(flops=1, bytes_accessed=1, transcendentals=0),
        name="terms",
    )(place, left, left_far, right, right_far)


def group_terms(grid, place, held, held_far, right, right_far, pairs):
    by_core = right_far is None
    width = held.shape[1]
    rows = width // grid.count
    arrays, specs = [], []
    for tokens, left_row, right_row in pairs:
        arrays += [held, held_far, right]
        specs += [pl.BlockSpec((tokens, width), lambda i, row=left_row: (row, 0))] * 2
        if by_core:
            specs += [pl.BlockSpec((2, tokens, width), lambda i, row=right_row: (0, row, 0))]
        else:
            arrays += [right_far]
            specs += [pl.BlockSpec((tokens, width), lambda i, row=right_row: (row, 0))] * 2
    most = max(tokens for tokens, _, _ in pairs)
    shapes = [(n, len(pairs), rows, width) for n in piece_counts(grid.depth)]
    return pl.pallas_call(
        functools.partial(group_kernel, grid.depth, rows, len(pairs), by_core),
        grid=(1,),
        out_shape=[jax.ShapeDtypeStruct(shape, jnp.bfloat16) for shape in shapes],
        in_specs=[pl.BlockSpec(memory_space=pltpu.SMEM)] + specs,
        out_specs=[pl.BlockSpec(shape, lambda i: (0, 0, 0, 0)) for shape in shapes],
        scratch_shapes=[pltpu.VMEM((4, grid.depth * rows, 2 * most), jnp.bfloat16)],
        compiler_params=pltpu.CompilerParams(vmem_limit_bytes=48 * 2**20),
        cost_estimate=pl.CostEstimate(flops=1, bytes_accessed=1, transcendentals=0),
        name="terms",
    )(place, *arrays)


def corner_kernel(over_x, low, over_y, high, sent_x, sent_y):
    wide = jnp.float32
    sent_x[...] = (over_x[...].astype(wide) + low[...].astype(wide)).astype(jnp.bfloat16)
    sent_y[...] = (over_y[...].astype(wide) + high[...].astype(wide)).astype(jnp.bfloat16)


def corner_added(grid, pieces, low, high):
    zeros = (0,) * (low.ndim - 1)
    first = pl.BlockSpec(low.shape, lambda i: (0,) + zeros)
    second = pl.BlockSpec(low.shape, lambda i: (1,) + zeros)
    return pl.pallas_call(
        corner_kernel,
        grid=(1,),
        out_shape=[jax.ShapeDtypeStruct(pieces[n].shape, jnp.bfloat16) for n in (1, 2)],
        in_specs=[first, first, second, first],
        out_specs=[first, second],
        input_output_aliases={0: 0, 2: 1},
        compiler_params=pltpu.CompilerParams(vmem_limit_bytes=32 * 2**20),
        cost_estimate=pl.CostEstimate(flops=1, bytes_accessed=1, transcendentals=0),
        name="corner_added",
    )(pieces[1], low, pieces[2], high)


def plane_sum(own, over_x, over_y):
    wide = jnp.float32
    return (own.astype(wide) + over_x.astype(wide) + over_y.astype(wide)).astype(jnp.bfloat16)


def plane_sums(grid, pieces, over_x, over_y):
    half = grid.depth // 2
    return [
        plane_sum(pieces[0][part], over_x[part], over_y[part]) for part in (slice(0, half), slice(half, None))
    ]


def pair_sum(near, got):
    return (near[1].astype(jnp.float32) + got[1].astype(jnp.float32)).astype(jnp.bfloat16)


def total_of(*terms_of):
    return sum([term.astype(jnp.float32) for term in terms_of[1:]], terms_of[0].astype(jnp.float32))


def fetch(attention_rows, expand_rows, reduce_rows, norm_rows):
    gathered = (
        lax.all_gather(attention_rows, ("dp", "fsdp"), axis=1, tiled=True),
        lax.all_gather(expand_rows, ("dp", "fsdp"), axis=0, tiled=True),
        lax.all_gather(reduce_rows, ("dp", "fsdp"), axis=0, tiled=True),
        lax.all_gather(norm_rows, ("dp", "fsdp"), axis=1, tiled=True),
    )
    return gathered


def settle(attention_terms, expand_terms, reduce_terms, norm_terms):
    owned = (
        lax.psum_scatter(attention_terms, ("dp", "fsdp"), scatter_dimension=1, tiled=True),
        lax.psum_scatter(expand_terms, ("dp", "fsdp"), scatter_dimension=0, tiled=True),
        lax.psum_scatter(reduce_terms, ("dp", "fsdp"), scatter_dimension=0, tiled=True),
        lax.psum_scatter(norm_terms, ("dp", "fsdp"), scatter_dimension=1, tiled=True),
    )
    return owned


def matmul(left, right):
    return jnp.dot(left, right, preferred_element_type=jnp.float32)


def across(left, right):
    return jnp.einsum("ti,tj->ij", left, right, preferred_element_type=jnp.float32)


def against(left, right):
    return jnp.einsum("ti,ji->tj", left, right, preferred_element_type=jnp.float32)


def gelu_tanh(values):
    return jax.nn.gelu(values, approximate=True)


def normalize(summed, gain, shift):
    center = jnp.mean(summed, axis=-1, keepdims=True)
    centred = summed - center
    inverse = lax.rsqrt(jnp.mean(centred * centred, axis=-1, keepdims=True) + EPSILON)
    scaled = centred * inverse
    return (scaled * gain + shift, scaled, inverse)


def normalize_back(incoming, scaled, inverse, gain):
    spread = incoming * gain
    d_summed = inverse * (
        spread
        - jnp.mean(spread, axis=-1, keepdims=True)
        - scaled * jnp.mean(spread * scaled, axis=-1, keepdims=True)
    )
    return (d_summed, jnp.sum(incoming * scaled, axis=0), jnp.sum(incoming, axis=0))


def split_heads(matrix):
    return matrix.reshape(matrix.shape[0], HEADS, HEAD_DIM)


def scores_of(query_rows, key_rows, allowed):
    raw = jnp.einsum(
        "qhd,khd->hqk",
        split_heads(query_rows),
        split_heads(key_rows),
        preferred_element_type=jnp.float32,
    ) * HEAD_DIM ** (-0.5)
    return jnp.where(allowed[None], raw, NEGATIVE)


def attend_forward(query_rows, key_rows, value_rows, allowed):
    scores = scores_of(query_rows, key_rows, allowed)
    highest = jnp.max(scores, axis=-1, keepdims=True)
    weights = jnp.exp(scores - highest)
    totals = jnp.sum(weights, axis=-1, keepdims=True)
    chances = (weights / totals).astype(jnp.bfloat16)
    context = jnp.einsum(
        "hqk,khd->qhd", chances, split_heads(value_rows), preferred_element_type=jnp.float32
    )
    return (
        context.reshape(query_rows.shape[0], HEADS * HEAD_DIM).astype(jnp.bfloat16),
        highest + jnp.log(totals),
    )


def attend_back(query_rows, key_rows, value_rows, allowed, logsum, d_context):
    query_heads = split_heads(query_rows)
    key_heads = split_heads(key_rows)
    d_heads = split_heads(d_context)
    chances = jnp.exp(scores_of(query_rows, key_rows, allowed) - logsum)
    d_chances = jnp.einsum(
        "qhd,khd->hqk", d_heads, split_heads(value_rows), preferred_element_type=jnp.float32
    )
    d_value = jnp.einsum(
        "hqk,qhd->khd", chances.astype(jnp.bfloat16), d_heads, preferred_element_type=jnp.float32
    )
    centre = jnp.sum(d_chances * chances, axis=-1, keepdims=True)
    d_scores = (chances * (d_chances - centre)).astype(jnp.bfloat16)
    d_query = jnp.einsum(
        "hqk,khd->qhd", d_scores, key_heads, preferred_element_type=jnp.float32
    ) * HEAD_DIM ** (-0.5)
    d_key = jnp.einsum(
        "hqk,qhd->khd", d_scores, query_heads, preferred_element_type=jnp.float32
    ) * HEAD_DIM ** (-0.5)
    query_count = query_rows.shape[0]
    key_count = key_rows.shape[0]
    return (
        d_query.reshape(query_count, HEADS * HEAD_DIM).astype(jnp.bfloat16),
        d_key.reshape(key_count, HEADS * HEAD_DIM).astype(jnp.bfloat16),
        d_value.reshape(key_count, HEADS * HEAD_DIM).astype(jnp.bfloat16),
    )


def plain_device(
    tokens,
    memory,
    target_segments,
    source_segments,
    self_query,
    self_key,
    self_value,
    self_output,
    cross_query,
    cross_key,
    cross_value,
    cross_output,
    expand_weight,
    reduce_weight,
    self_gain,
    self_shift,
    cross_gain,
    cross_shift,
    final_gain,
    final_shift,
    output_grad,
):
    attention_rows = jnp.stack(
        [
            self_query,
            self_key,
            self_value,
            self_output,
            cross_query,
            cross_key,
            cross_value,
            cross_output,
        ]
    )
    norm_rows = jnp.stack([self_gain, self_shift, cross_gain, cross_shift, final_gain, final_shift])
    matrices, expand_full, reduce_full, norm_full = fetch(
        attention_rows, expand_weight, reduce_weight, norm_rows
    )
    gains = norm_full.astype(jnp.float32)
    target_ids = target_segments[0]
    source_ids = source_segments[0]
    positions = lax.iota(jnp.int32, tokens.shape[0])
    causal = (target_ids[:, None] == target_ids[None, :]) & (
        positions[None, :] <= positions[:, None]
    )
    crossing = target_ids[:, None] == source_ids[None, :]
    query_one = matmul(tokens, matrices[0]).astype(jnp.bfloat16)
    key_one = matmul(tokens, matrices[1]).astype(jnp.bfloat16)
    value_one = matmul(tokens, matrices[2]).astype(jnp.bfloat16)
    context_one, logsum_one = attend_forward(query_one, key_one, value_one, causal)
    branch_one = matmul(context_one, matrices[3])
    first, first_scaled, first_inverse = normalize(
        RESIDUAL_SCALE * tokens.astype(jnp.float32) + branch_one, gains[0], gains[1]
    )
    first_low = first.astype(jnp.bfloat16)
    query_two = matmul(first_low, matrices[4]).astype(jnp.bfloat16)
    key_two = matmul(memory, matrices[5]).astype(jnp.bfloat16)
    value_two = matmul(memory, matrices[6]).astype(jnp.bfloat16)
    context_two, logsum_two = attend_forward(query_two, key_two, value_two, crossing)
    branch_two = matmul(context_two, matrices[7])
    second, second_scaled, second_inverse = normalize(
        RESIDUAL_SCALE * first + branch_two, gains[2], gains[3]
    )
    second_low = second.astype(jnp.bfloat16)
    inner = matmul(second_low, expand_full)
    active = gelu_tanh(inner).astype(jnp.bfloat16)
    branch_three = matmul(active, reduce_full)
    final, final_scaled, final_inverse = normalize(
        RESIDUAL_SCALE * second + branch_three, gains[4], gains[5]
    )
    output = final.astype(jnp.bfloat16)
    matrices, expand_full, reduce_full, norm_full = fetch(
        attention_rows, expand_weight, reduce_weight, norm_rows
    )
    gains = norm_full.astype(jnp.float32)
    d_sum_three, final_gain_term, final_shift_term = normalize_back(
        output_grad.astype(jnp.float32), final_scaled, final_inverse, gains[4]
    )
    d_branch_three = d_sum_three.astype(jnp.bfloat16)
    reduce_term = across(active, d_branch_three)
    d_active = against(d_branch_three, reduce_full)
    d_inner = jax.vjp(gelu_tanh, inner)[1](d_active)[0].astype(jnp.bfloat16)
    expand_term = across(second_low, d_inner)
    d_second = RESIDUAL_SCALE * d_sum_three + against(d_inner, expand_full)
    d_sum_two, cross_gain_term, cross_shift_term = normalize_back(
        d_second, second_scaled, second_inverse, gains[2]
    )
    d_branch_two = d_sum_two.astype(jnp.bfloat16)
    cross_output_term = across(context_two, d_branch_two)
    d_context_two = against(d_branch_two, matrices[7]).astype(jnp.bfloat16)
    d_query_two, d_key_two, d_value_two = attend_back(
        query_two, key_two, value_two, crossing, logsum_two, d_context_two
    )
    cross_query_term = across(first_low, d_query_two)
    cross_key_term = across(memory, d_key_two)
    cross_value_term = across(memory, d_value_two)
    memory_grad = against(d_key_two, matrices[5]) + against(d_value_two, matrices[6])
    d_first = RESIDUAL_SCALE * d_sum_two + against(d_query_two, matrices[4])
    d_sum_one, self_gain_term, self_shift_term = normalize_back(
        d_first, first_scaled, first_inverse, gains[0]
    )
    d_branch_one = d_sum_one.astype(jnp.bfloat16)
    self_output_term = across(context_one, d_branch_one)
    d_context_one = against(d_branch_one, matrices[3]).astype(jnp.bfloat16)
    d_query_one, d_key_one, d_value_one = attend_back(
        query_one, key_one, value_one, causal, logsum_one, d_context_one
    )
    self_query_term = across(tokens, d_query_one)
    self_key_term = across(tokens, d_key_one)
    self_value_term = across(tokens, d_value_one)
    tokens_grad = (
        RESIDUAL_SCALE * d_sum_one
        + against(d_query_one, matrices[0])
        + against(d_key_one, matrices[1])
        + against(d_value_one, matrices[2])
    )
    attention_terms = jnp.stack(
        [
            self_query_term,
            self_key_term,
            self_value_term,
            self_output_term,
            cross_query_term,
            cross_key_term,
            cross_value_term,
            cross_output_term,
        ]
    )
    norm_terms = jnp.stack(
        [
            self_gain_term,
            self_shift_term,
            cross_gain_term,
            cross_shift_term,
            final_gain_term,
            final_shift_term,
        ]
    )
    attention_owned, expand_owned, reduce_owned, norm_owned = settle(
        attention_terms, expand_term, reduce_term, norm_terms
    )
    return (
        output,
        tokens_grad,
        memory_grad,
        attention_owned[0],
        attention_owned[1],
        attention_owned[2],
        attention_owned[3],
        attention_owned[4],
        attention_owned[5],
        attention_owned[6],
        attention_owned[7],
        expand_owned,
        reduce_owned,
        norm_owned[0],
        norm_owned[1],
        norm_owned[2],
        norm_owned[3],
        norm_owned[4],
        norm_owned[5],
    )


def per_device(
    grid,
    tokens,
    memory,
    target_segments,
    source_segments,
    self_query,
    self_key,
    self_value,
    self_output,
    cross_query,
    cross_key,
    cross_value,
    cross_output,
    expand_weight,
    reduce_weight,
    self_gain,
    self_shift,
    cross_gain,
    cross_shift,
    final_gain,
    final_shift,
    output_grad,
):
    if not grid.fast:
        return plain_device(
            tokens,
            memory,
            target_segments,
            source_segments,
            self_query,
            self_key,
            self_value,
            self_output,
            cross_query,
            cross_key,
            cross_value,
            cross_output,
            expand_weight,
            reduce_weight,
            self_gain,
            self_shift,
            cross_gain,
            cross_shift,
            final_gain,
            final_shift,
            output_grad,
        )
    place = grid.place()
    held_rows = self_gain.shape[0]
    norm_rows = jnp.stack([self_gain, self_shift, cross_gain, cross_shift, final_gain, final_shift])
    extra = jnp.zeros((16, held_rows * grid.count), jnp.bfloat16)
    extra = lax.dynamic_update_slice(extra, norm_rows, (0, grid.index() * held_rows))
    extra = extra.reshape(4, 32, 128)
    first_rows = jnp.concatenate([jnp.stack([self_query, self_key, self_value, self_output]), extra], axis=-1)
    second_rows = jnp.stack([cross_query, cross_key, cross_value, cross_output])
    target_column, target_row = target_segments.reshape(-1, 1), target_segments
    source_row = source_segments

    half = grid.depth // 2
    width = expand_weight.shape[1] // 4
    expand_rows = jnp.stack([expand_weight[:, n * width : (n + 1) * width] for n in range(4)])
    reduce_rows = reduce_weight.reshape(expand_rows.shape)

    first_z = [grid.move(first_rows, dz=k) for k in (2, 3, 1)]
    second_z = grid.move(second_rows, dz=1)
    first_own = jnp.stack([first_rows, first_z[2], first_z[0], first_z[1]])
    second_pair = jnp.stack([second_rows, second_z])
    first_own, second_pair, expand_rows, reduce_rows = after(
        (first_own, second_pair, expand_rows, reduce_rows)
    )
    first_x, first_y = grid.move(first_own, dx=1), grid.move(first_own, dy=1)
    second_z = grid.move(second_pair, dz=2)
    expand_z = grid.move(expand_rows, dz=1)
    reduce_z = grid.move(reduce_rows, dz=1)
    first_x, first_y, second_z, expand_z, reduce_z = after((first_x, first_y, second_z, expand_z, reduce_z))
    second_own = jnp.concatenate([second_pair, second_z])
    expand_pair = jnp.stack([expand_rows, expand_z])
    first_low, first_high, second_own, expand_pair = after(
        (first_x[:half], first_y[half:], second_own, expand_pair)
    )
    first_low, first_high = grid.move(first_low, dy=1), grid.move(first_high, dx=1)
    second_x, second_y = grid.move(second_own, dx=1), grid.move(second_own, dy=1)
    expand_z = grid.move(expand_pair, dz=2)
    first_low, first_high, second_x, second_y, expand_z = after(
        (first_low, first_high, second_x, second_y, expand_z)
    )
    reduce_pair = jnp.stack([reduce_rows, reduce_z])
    first_near = jnp.concatenate([first_own, first_x, first_y, first_low, first_high])
    sides = jnp.concatenate([second_own, second_x, second_y, expand_pair, expand_z])
    sent_y = jnp.concatenate([second_x[:half], expand_pair, expand_z])
    sent_x = jnp.concatenate([second_y[half:], expand_pair, expand_z])
    sent_x, sent_y, reduce_pair, first_near, sides = after((sent_x, sent_y, reduce_pair, first_near, sides))
    got_x, got_y = grid.move(sent_x, dx=1), grid.move(sent_y, dy=1)
    reduce_z = grid.move(reduce_pair, dz=2)
    first_far = grid.move(first_near, dc=1)
    sides_far = grid.move(sides, dc=1)
    first_out = self_forward(grid, place, tokens, target_column, target_row, (first_near, first_far))
    first_out, got_x, got_y, reduce_z, sides_far = after((first_out, got_x, got_y, reduce_z, sides_far))
    first_full, gains, query_one, key_one, value_one, context_one, logsum_one = first_out[:7]
    first, first_low, first_scaled, first_inverse = first_out[7:]
    reduce_own = jnp.concatenate([reduce_pair, reduce_z])
    sent_y = jnp.concatenate([got_x[half : 2 * half], reduce_pair, reduce_z])
    sent_x = jnp.concatenate([got_y[2 * half :], reduce_pair, reduce_z])
    sent_x, sent_y, got_x, got_y, reduce_own = after((sent_x, sent_y, got_x, got_y, reduce_own))
    last_x, last_y = grid.move(sent_x, dx=1), grid.move(sent_y, dy=1)
    got_x_far, got_y_far = grid.move(got_x, dc=1), grid.move(got_y, dc=1)
    reduce_own_far = grid.move(reduce_own, dc=1)
    second_out = cross_forward(
        grid, place, first, first_low, memory, gains, target_column, source_row,
        (sides, got_y, got_x, sides_far, got_y_far, got_x_far),
    )
    second_out, last_x, last_y, reduce_own_far = after((second_out, last_x, last_y, reduce_own_far))
    second_full, query_two, key_two, value_two, context_two, logsum_two = second_out[:6]
    second, second_low, second_scaled, second_inverse = second_out[6:]
    reduce_low, reduce_high, last_x, last_y = after(
        (last_x[half : 2 * half], last_y[2 * half :], last_x, last_y)
    )
    reduce_low, reduce_high = grid.move(reduce_low, dy=1), grid.move(reduce_high, dx=1)
    last_x_far, last_y_far = grid.move(last_x, dc=1), grid.move(last_y, dc=1)
    expand_full, active, slope = expand_forward(
        grid, place, second_low,
        (sides, got_x, got_y, last_y, last_x, sides_far, got_x_far, got_y_far, last_y_far, last_x_far),
    )
    held = jnp.concatenate([tokens, context_one, first_low, context_two, second_low, memory])
    held, active = after((held, active))
    held_far = grid.move(held, dc=1)
    active_far = grid.move(active, dc=1)
    reduce_low, reduce_high, active = after((reduce_low, reduce_high, active))
    reduce_corner, active = after((jnp.concatenate([reduce_low, reduce_high]), active))
    reduce_corner_far = grid.move(reduce_corner, dc=1)
    partial = reduce_first(
        grid, place, active, (reduce_own, last_x, last_y, reduce_own_far, last_x_far, last_y_far)
    )
    reduce_pieces = (
        reduce_own, last_x, last_y, reduce_corner, reduce_own_far, last_x_far, last_y_far, reduce_corner_far
    )
    reduce_corner = (reduce_corner, reduce_corner_far)
    output, d_sum_three, d_branch_three, final_norm_terms = reduce_finish(
        grid, place, active, partial, second, gains, output_grad, reduce_corner
    )
    d_branches = (d_branch_three, grid.move(d_branch_three, dc=1))
    reduce_low, reduce_high = after(
        tuple(tiled_terms(grid, place, active, active_far, *d_branches, 1024, (3,)))
    )
    reduce_terms = tiled_terms(
        grid, place, after(active, reduce_low), active_far, *d_branches, 512, (0, 1, 2)
    )
    d_inner = reduce_back(grid, place, after(d_branch_three, *reduce_terms), slope, reduce_pieces)
    reduce_low, reduce_high = grid.move(reduce_low, dy=1), grid.move(reduce_high, dx=1)
    reduce_low, reduce_high, d_inner = after((reduce_low, reduce_high, d_inner))
    reduce_sends = corner_added(grid, reduce_terms, reduce_low, reduce_high)
    reduce_sends, d_inner = after((reduce_sends, d_inner))
    reduce_x, reduce_y = grid.move(reduce_sends[0], dx=1), grid.move(reduce_sends[1], dy=1)
    d_inner_far = grid.move(d_inner, dc=1)
    d_sum_two, d_branch_two, d_context_two, cross_norm_terms = expand_back(
        d_inner, expand_full, d_sum_three, second_scaled, second_inverse, gains, second_full
    )
    expand_terms = tiled_terms(grid, place, second_low, held_far, after(d_inner, d_context_two), d_inner_far, 1024)
    expand_terms, d_context_two = after((expand_terms, d_context_two))
    expand_low, expand_high = grid.move(expand_terms[3], dy=1), grid.move(expand_terms[4], dx=1)
    back, d_sum_one, d_context_one, self_norm_terms = cross_back(
        query_two, key_two, value_two, logsum_two, d_context_two, target_column,
        source_row, d_branch_two, d_sum_two, first_scaled, first_inverse, gains, second_full, first_full,
    )
    norm_terms = jnp.concatenate([self_norm_terms, cross_norm_terms, final_norm_terms])
    expand_low, expand_high, reduce_x, reduce_y, back, norm_terms = after(
        (expand_low, expand_high, reduce_x, reduce_y, back, norm_terms)
    )
    expand_sends = corner_added(grid, expand_terms, expand_low, expand_high)
    expand_sends, back = after((expand_sends, back))
    expand_x, expand_y = grid.move(expand_sends[0], dx=1), grid.move(expand_sends[1], dy=1)
    reduce_near, reduce_pass = plane_sums(grid, reduce_terms, *after((reduce_x, reduce_y), expand_sends))
    reduce_near, reduce_pass, back = after((reduce_near, reduce_pass, back))
    reduce_got = grid.move(reduce_pass, dz=2)
    backs = grid.cores(back)
    pairs = [(256, 1, 2), (256, 2, 1), (128, 10, 6), (128, 10, 7), (256, 3, 0)]
    cross_terms = group_terms(grid, place, held, held_far, backs, None, pairs)
    cross_terms, d_context_one = after((cross_terms, d_context_one))
    cross_low, cross_high = grid.move(cross_terms[3], dy=1), grid.move(cross_terms[4], dx=1)
    back_one = self_back(
        query_one, key_one, value_one, logsum_one, d_context_one, target_column, target_row
    )
    cross_low, cross_high, back_one, reduce_got, expand_x, expand_y = after(
        (cross_low, cross_high, back_one, reduce_got, expand_x, expand_y)
    )
    cross_sends = corner_added(grid, cross_terms, cross_low, cross_high)
    reduce_leaving = pair_sum(reduce_near, reduce_got)
    cross_sends, back_one, reduce_leaving = after((cross_sends, back_one, reduce_leaving))
    cross_x, cross_y = grid.move(cross_sends[0], dx=1), grid.move(cross_sends[1], dy=1)
    back_one_far = grid.move(back_one, dc=1)
    reduce_last = grid.move(reduce_leaving, dz=1)
    expand_near, expand_pass = plane_sums(grid, expand_terms, *after((expand_x, expand_y), cross_sends))
    expand_near, expand_pass, back_one = after((expand_near, expand_pass, back_one))
    expand_got = grid.move(expand_pass, dz=2)
    self_terms = group_terms(
        grid, place, held, held_far, back_one, back_one_far, [(256, 0, n) for n in range(3)]
    )
    tokens_grad, memory_grad = inputs_back(
        after(back_one, *self_terms), back, d_sum_one, first_full, second_full
    )
    expand_got, reduce_last, self_low, self_high = after(
        (expand_got, reduce_last, self_terms[3], self_terms[4]), tokens_grad
    )
    expand_leaving = pair_sum(expand_near, expand_got)
    self_low, self_high, expand_leaving = after((self_low, self_high, expand_leaving))
    self_low, self_high = grid.move(self_low, dy=1), grid.move(self_high, dx=1)
    expand_last = grid.move(expand_leaving, dz=1)
    cross_x, cross_y = after((cross_x, cross_y), expand_leaving)
    cross_near, cross_pass = plane_sums(grid, cross_terms, cross_x, cross_y)
    cross_near, cross_pass = after((cross_near, cross_pass))
    cross_got = grid.move(cross_pass, dz=2)
    self_low, self_high, expand_last = after((self_low, self_high, expand_last), cross_pass)
    self_sends = corner_added(grid, self_terms, self_low, self_high)
    self_sends, norm_terms = after((self_sends, norm_terms))
    self_x, self_y = grid.move(self_sends[0], dx=1), grid.move(self_sends[1], dy=1)
    norm_got = lax.all_to_all(norm_terms.reshape(6, grid.count, held_rows), grid.axes, 1, 0, tiled=True)
    cross_got, norm_got, self_x, self_y = after((cross_got, norm_got, self_x, self_y))
    self_column = [plane_sum(self_terms[0][k], self_x[k], self_y[k]) for k in range(grid.depth)]
    cross_leaving = pair_sum(cross_near, cross_got)
    self_column, cross_leaving = after((self_column, cross_leaving))
    self_others = [grid.move(self_column[k], dz=k) for k in (2, 3, 1)]
    cross_last = grid.move(cross_leaving, dz=1)
    reduce_term = total_of(reduce_near[0], reduce_got[0], reduce_last)
    expand_term = total_of(expand_near[0], expand_got[0], expand_last)
    cross_owned = total_of(cross_near[0], cross_got[0], cross_last)
    self_owned = total_of(self_column[0], *self_others)
    norm_owned = jnp.sum(norm_got.reshape(grid.count, 6, held_rows), axis=0)
    return (
        output,
        tokens_grad,
        memory_grad,
        *[self_owned[i] for i in range(3)],
        *[cross_owned[i] for i in range(5)],
        expand_term,
        reduce_term,
        *[norm_owned[i] for i in range(6)],
    )


def solution(mesh):
    grid = Grid(mesh)
    rows = P(grid.axes, None)
    parts = P(grid.axes)
    return jax.shard_map(
        functools.partial(per_device, grid),
        mesh=grid.mesh,
        in_specs=(
            rows,
            rows,
            rows,
            rows,
            rows,
            rows,
            rows,
            rows,
            rows,
            rows,
            rows,
            rows,
            rows,
            rows,
            parts,
            parts,
            parts,
            parts,
            parts,
            parts,
            rows,
        ),
        out_specs=(
            rows,
            rows,
            rows,
            rows,
            rows,
            rows,
            rows,
            rows,
            rows,
            rows,
            rows,
            rows,
            rows,
            parts,
            parts,
            parts,
            parts,
            parts,
            parts,
        ),
        check_vma=False,
    )
```

```python
import functools

import jax
import jax.numpy as jnp
from jax import lax
from jax.experimental import pallas as pl
from jax.experimental.pallas import tpu as pltpu
from jax.sharding import PartitionSpec as P

HEADS = 16
HEAD_DIM = 64


RESIDUAL_SCALE = 300.0**0.25
EPSILON = 1e-05
NEGATIVE = -1e30
ALL = ("dp", "fsdp")


class Grid:
    def __init__(self, mesh):
        self.depth = mesh.shape["dp"] // 2
        self.count = mesh.size
        self.fast = mesh.shape["fsdp"] == 4 and mesh.shape["dp"] == 8
        self.axes = ("z", "core", "y", "x") if self.fast else ALL
        self.mesh = mesh
        if self.fast:
            self.mesh = jax.sharding.Mesh(mesh.devices.reshape(4, 2, 2, 2), self.axes)

    def place(self):
        return jnp.stack([lax.axis_index(axis) for axis in self.axes]).astype(jnp.int32)

    def index(self):
        return lax.axis_index(self.axes)

    def move(self, value, dz=0, dc=0, dy=0, dx=0):
        offset = ((dz * 2 + dc) * 2 + dy) * 2 + dx
        return lax.ppermute(value, self.axes, [(index ^ offset, index) for index in range(self.count)])

    def cores(self, twice):
        return lax.all_to_all(twice, "core", 0, 0, tiled=True)


def after(value, *others):
    return lax.optimization_barrier((value,) + others)[0]


def wide_dot(left, right):
    return jnp.dot(left, right, preferred_element_type=jnp.float32)


def dot_rows(left, right):
    return lax.dot_general(left, right, (((1,), (1,)), ((), ())), preferred_element_type=jnp.float32)


def dot_columns(left, right):
    return lax.dot_general(left, right, (((0,), (0,)), ((), ())), preferred_element_type=jnp.float32)


def whole_call(body, name, inputs, shapes, scratch=(), limit=56):
    arrays, specs = [], []
    for item in inputs:
        if not isinstance(item, tuple):
            item = (item, item.shape, (0,) * item.ndim)
        arrays.append(item[0])
        if len(item) == 2:
            specs.append(pl.BlockSpec(memory_space=item[1]))
        else:
            specs.append(pl.BlockSpec(item[1], lambda i, index=item[2]: index))
    outs, out_specs = [], []
    for item in shapes:
        outs.append(jax.ShapeDtypeStruct(item[0], item[1]))
        if len(item) == 3:
            out_specs.append(pl.BlockSpec(memory_space=item[2]))
        else:
            out_specs.append(pl.BlockSpec(item[0], lambda i, rank=len(item[0]): (0,) * rank))
    return pl.pallas_call(
        body,
        grid=(1,),
        out_shape=outs,
        in_specs=specs,
        out_specs=out_specs,
        scratch_shapes=list(scratch),
        compiler_params=pltpu.CompilerParams(vmem_limit_bytes=limit * 2**20),
        cost_estimate=pl.CostEstimate(flops=1, bytes_accessed=1, transcendentals=0),
        name=name,
    )(*arrays)


def in_two(depth, pieces, dc, side, k):
    return pieces[dc], side * depth + k


def in_rest(base):
    def locate(depth, pieces, dc, side, k):
        half = depth // 2
        own, over_x, over_y, low, high = pieces[5 * dc : 5 * dc + 5]
        if side == 0:
            return own, base + k
        if side < 3:
            return (over_x, over_y)[side - 1], half + k
        return (low, k) if k < half else (high, k - half)

    return locate


def in_last(depth, pieces, dc, side, k):
    own, over_x, over_y, corner = pieces[4 * dc : 4 * dc + 4]
    return (own, over_x, over_y, corner)[side], depth // 2 + k if side in (1, 2) else k


def in_second(depth, pieces, dc, side, k):
    half = depth // 2
    sides, low, high = pieces[3 * dc : 3 * dc + 3]
    if side < 3:
        return sides, side * depth + k
    return (low, k) if k < half else (high, k - half)


def arrivals_of(depth, rows, place, locate, pieces, held, sems, held_norms=None, these=range(8), blocks=0):
    z, c, y, x = place[0], place[1], place[2], place[3]
    width = held.shape[-1]
    arrivals = []
    for k in range(depth):
        column = []
        for n in these:
            dc, dy, dx = n // 4, n // 2 % 2, n % 2
            piece, spot = locate(depth, pieces, dc, n % 4, k)
            owner = (((z ^ k) * 2 + (c ^ dc)) * 2 + (y ^ dy)) * 2 + (x ^ dx)
            if blocks:
                target = held.at[pl.ds(owner * blocks, blocks)]
            else:
                target = held.at[..., pl.ds(pl.multiple_of(owner * rows, rows), rows), :]
            source = piece.at[spot]
            order = k * 8 + n
            if held_norms is None:
                column.append(pltpu.make_async_copy(source, target, sems.at[order]))
            else:
                column.append(pltpu.make_async_copy(source.at[..., :width], target, sems.at[order]))
                column.append(
                    pltpu.make_async_copy(
                        source.at[0:2, :, pl.ds(width, 128)],
                        held_norms.at[owner],
                        sems.at[8 * depth + order],
                    )
                )
        for copy in column:
            copy.start()
        arrivals.append(column)
    return arrivals


def pass_on(depth, rows, place, arrivals, held, whole, sems):
    leaving = []
    for k in range(depth):
        for copy in arrivals[k]:
            copy.wait()
        spot = pl.ds(pl.multiple_of((place[0] ^ k) * (8 * rows), 8 * rows), 8 * rows)
        leaving.append(pltpu.make_async_copy(held.at[..., spot, :], whole.at[..., spot, :], sems.at[k]))
        leaving[k].start()
    return leaving


def norm_rows_of(summed, gain, shift):
    center = jnp.mean(summed, axis=-1, keepdims=True)
    centred = summed - center
    inverse = lax.rsqrt(jnp.mean(centred * centred, axis=-1, keepdims=True) + EPSILON)
    scaled = centred * inverse
    return scaled * gain + shift, scaled, inverse


def norm_rows_back(incoming, scaled, inverse, gain):
    spread_out = incoming * gain
    d_summed = inverse * (
        spread_out
        - jnp.mean(spread_out, axis=-1, keepdims=True)
        - scaled * jnp.mean(spread_out * scaled, axis=-1, keepdims=True)
    )
    return d_summed, jnp.sum(incoming * scaled, axis=0, keepdims=True), jnp.sum(incoming, axis=0, keepdims=True)


def head_halves():
    lane = lax.broadcasted_iota(jnp.int32, (1, 2 * HEAD_DIM), 1)
    return [
        jnp.where(lane < HEAD_DIM, 1.0, 0.0).astype(jnp.bfloat16),
        jnp.where(lane < HEAD_DIM, 0.0, 1.0).astype(jnp.bfloat16),
    ]


def attend_heads(query, key, value, allowed, context, logsum):
    halves = head_halves()
    lane = lax.broadcasted_iota(jnp.int32, logsum.shape, 1)
    logsum[...] = jnp.zeros_like(logsum)

    def pair(p, carry):
        lanes = pl.ds(pl.multiple_of(p * 2 * HEAD_DIM, 2 * HEAD_DIM), 2 * HEAD_DIM)
        queries, keys, values = query[:, lanes], key[:, lanes], value[:, lanes]
        total = None
        for side, half in enumerate(halves):
            scores = dot_rows(queries * half, keys) * HEAD_DIM ** (-0.5)
            scores = jnp.where(allowed[...] > 0, scores, NEGATIVE)
            highest = jnp.max(scores, axis=-1, keepdims=True)
            weights = jnp.exp(scores - highest)
            totals = jnp.sum(weights, axis=-1, keepdims=True)
            chances = (weights * (1.0 / totals)).astype(jnp.bfloat16)
            part = wide_dot(chances, values * half)
            total = part if total is None else total + part
            logsum[...] = jnp.where(lane == 2 * p + side, highest + jnp.log(totals), logsum[...])
        context[:, lanes] = total.astype(jnp.bfloat16)
        return carry

    lax.fori_loop(0, HEADS // 2, pair, 0)


def attend_heads_back(query, key, value, allowed, logsum, d_context, d_query, d_key, d_value):
    halves = head_halves()
    lane = lax.broadcasted_iota(jnp.int32, logsum.shape, 1)
    scale = HEAD_DIM ** (-0.5)

    def pair(p, carry):
        lanes = pl.ds(pl.multiple_of(p * 2 * HEAD_DIM, 2 * HEAD_DIM), 2 * HEAD_DIM)
        queries, keys, values, d_outs = query[:, lanes], key[:, lanes], value[:, lanes], d_context[:, lanes]
        sums = [None, None, None]
        for side, half in enumerate(halves):
            own_sum = jnp.sum(jnp.where(lane == 2 * p + side, logsum[...], 0.0), axis=-1, keepdims=True)
            own_queries, own_outs = queries * half, d_outs * half
            scores = dot_rows(own_queries, keys) * scale
            scores = jnp.where(allowed[...] > 0, scores, NEGATIVE)
            chances = jnp.exp(scores - own_sum)
            d_chances = dot_rows(own_outs, values)
            centre = jnp.sum(d_chances * chances, axis=-1, keepdims=True)
            d_scores = (chances * (d_chances - centre)).astype(jnp.bfloat16)
            parts = (
                wide_dot(d_scores, keys * half),
                dot_columns(d_scores, own_queries),
                dot_columns(chances.astype(jnp.bfloat16), own_outs),
            )
            sums = [part if old is None else old + part for old, part in zip(sums, parts)]
        d_query[:, lanes] = (sums[0] * scale).astype(jnp.bfloat16)
        d_key[:, lanes] = (sums[1] * scale).astype(jnp.bfloat16)
        d_value[:, lanes] = sums[2].astype(jnp.bfloat16)
        return carry

    lax.fori_loop(0, HEADS // 2, pair, 0)


def self_allowed(ids_column, ids_row, allowed):
    rows, columns = allowed.shape
    later = lax.broadcasted_iota(jnp.int32, (rows, columns), 0) >= lax.broadcasted_iota(
        jnp.int32, (rows, columns), 1
    )
    same = ids_column[...] == ids_row[...]
    allowed[...] = jnp.where(later & same, 1.0, 0.0)


def cross_allowed(ids_column, ids_row, allowed):
    allowed[...] = jnp.where(ids_column[...] == ids_row[...], 1.0, 0.0)


def self_forward_kernel(depth, rows, place, tokens, ids_column, ids_row, *refs):
    pieces, refs = refs[:2], refs[2:]
    whole, gains, query, key, value, context, logsum, first, first_low, scaled, inverse = refs[:11]
    held, held_norms, allowed, in_sems, out_sems = refs[11:]
    arrivals = arrivals_of(depth, rows, place, in_two, pieces, held, in_sems, held_norms)
    self_allowed(ids_column, ids_row, allowed)
    leaving = pass_on(depth, rows, place, arrivals, held, whole, out_sems)
    packed = held_norms[0].astype(jnp.float32)
    for owner in range(1, 8 * depth):
        packed += held_norms[owner].astype(jnp.float32)
    gains[...] = jnp.zeros_like(gains)
    for n in range(6):
        for j in range(8):
            r = n * 8 + j
            gains[n : n + 1, j * 128 : (j + 1) * 128] = packed[r // rows, r % rows : r % rows + 1, :]
    for n, out in enumerate((query, key, value)):
        out[...] = wide_dot(tokens[...], held[n]).astype(jnp.bfloat16)
    attend_heads(query, key, value, allowed, context, logsum)
    branch = wide_dot(context[...], held[3])
    summed = RESIDUAL_SCALE * tokens[...].astype(jnp.float32) + branch
    first[...], scaled[...], inverse[...] = norm_rows_of(summed, gains[0:1, :], gains[1:2, :])
    first_low[...] = first[...].astype(jnp.bfloat16)
    for copy in leaving:
        copy.wait()


def self_forward(grid, place, tokens, ids_column, ids_row, pieces):
    count, width = tokens.shape
    rows = pieces[0].shape[2]
    low, full = jnp.bfloat16, jnp.float32
    shape = (count, width)
    return whole_call(
        functools.partial(self_forward_kernel, grid.depth, rows),
        "self_forward",
        [(place, pltpu.SMEM), tokens, ids_column, ids_row] + [(piece, pl.ANY) for piece in pieces],
        [((4, width, width), low, pl.ANY), ((8, width), full)]
        + [(shape, low)] * 4
        + [((count, 128), full), (shape, full), (shape, low), (shape, full), ((count, 1), full)],
        [
            pltpu.VMEM((4, width, width), low),
            pltpu.VMEM((grid.count, 2, rows, 128), low),
            pltpu.VMEM((count, count), full),
            pltpu.SemaphoreType.DMA((2 * grid.count,)),
            pltpu.SemaphoreType.DMA((grid.depth,)),
        ],
    )


def cross_forward_kernel(depth, rows, place, first, first_low, memory, gains, ids_column, ids_row, *refs):
    pieces, refs = refs[:6], refs[6:]
    whole, query, key, value, context, logsum, second, second_low, scaled, inverse = refs[:10]
    held, allowed, in_sems, out_sems = refs[10:]
    arrivals = arrivals_of(depth, rows, place, in_second, pieces, held, in_sems)
    cross_allowed(ids_column, ids_row, allowed)
    leaving = pass_on(depth, rows, place, arrivals, held, whole, out_sems)
    query[...] = wide_dot(first_low[...], held[0]).astype(jnp.bfloat16)
    key[...] = wide_dot(memory[...], held[1]).astype(jnp.bfloat16)
    value[...] = wide_dot(memory[...], held[2]).astype(jnp.bfloat16)
    attend_heads(query, key, value, allowed, context, logsum)
    summed = RESIDUAL_SCALE * first[...] + wide_dot(context[...], held[3])
    second[...], scaled[...], inverse[...] = norm_rows_of(summed, gains[2:3, :], gains[3:4, :])
    second_low[...] = second[...].astype(jnp.bfloat16)
    for copy in leaving:
        copy.wait()


def cross_forward(grid, place, first, first_low, memory, gains, ids_column, ids_row, pieces):
    count, width = first.shape
    others = memory.shape[0]
    rows = pieces[0].shape[2]
    low, full = jnp.bfloat16, jnp.float32
    shape, other_shape = (count, width), (others, width)
    return whole_call(
        functools.partial(cross_forward_kernel, grid.depth, rows),
        "cross_forward",
        [(place, pltpu.SMEM), first, first_low, memory, gains, ids_column, ids_row]
        + [(piece, pl.ANY) for piece in pieces],
        [((4, width, width), low, pl.ANY), (shape, low), (other_shape, low), (other_shape, low), (shape, low)]
        + [((count, 128), full), (shape, full), (shape, low), (shape, full), ((count, 1), full)],
        [
            pltpu.VMEM((4, width, width), low),
            pltpu.VMEM((count, others), full),
            pltpu.SemaphoreType.DMA((grid.count,)),
            pltpu.SemaphoreType.DMA((grid.depth,)),
        ],
    )


TANH_SCALE = 0.7978845608028654
TANH_CUBE = 0.044715


def expand_forward_kernel(depth, rows, place, second_low, *refs):
    pieces, refs = refs[:10], refs[10:]
    whole, active, slope, held, in_sems, out_sems = refs
    arrivals = arrivals_of(depth, rows, place, in_rest(3 * depth), pieces, held, in_sems)
    leaving = pass_on(depth, rows, place, arrivals, held, whole, out_sems)
    left = second_low[...]
    block = held.shape[2]

    def tile(j, carry):
        for part in range(block // 512):
            lanes = pl.ds(pl.multiple_of(j * block + part * 512, 512), 512)
            inner = wide_dot(left, held[j, :, part * 512 : (part + 1) * 512])
            square = inner * inner
            bend = jnp.tanh(TANH_SCALE * (inner * (1.0 + TANH_CUBE * square)))
            half = 0.5 + 0.5 * bend
            active[:, lanes] = (inner * half).astype(jnp.bfloat16)
            slope[:, lanes] = half + (0.5 * TANH_SCALE) * inner * (1.0 - bend * bend) * (
                1.0 + (3.0 * TANH_CUBE) * square
            )
        return carry

    lax.fori_loop(0, held.shape[0], tile, 0)
    for copy in leaving:
        copy.wait()


def expand_forward(grid, place, second_low, pieces):
    count, width = second_low.shape
    blocks, rows, block = pieces[0].shape[1:]
    hidden = blocks * block
    low = jnp.bfloat16
    return whole_call(
        functools.partial(expand_forward_kernel, grid.depth, rows),
        "expand_forward",
        [(place, pltpu.SMEM), second_low] + [(piece, pl.ANY) for piece in pieces],
        [((blocks, width, block), low, pl.ANY), ((count, hidden), low), ((count, hidden), jnp.float32)],
        [
            pltpu.VMEM((blocks, width, block), low),
            pltpu.SemaphoreType.DMA((grid.count,)),
            pltpu.SemaphoreType.DMA((grid.depth,)),
        ],
    )


def rows_of(held):
    return held.reshape(held.shape[0] * held.shape[1], held.shape[2])


def reduce_first_kernel(depth, place, active, *refs):
    pieces, (partial, held, sems) = refs[:6], refs[6:]
    z, c, y, x = place[0], place[1], place[2], place[3]
    blocks, rows, width = pieces[0].shape[1:]

    def locate(depth, pieces, dc, side, k):
        return (pieces[3 * dc], k) if side == 0 else (pieces[3 * dc + side], depth // 2 + k)

    arrivals = arrivals_of(
        depth, rows, place, locate, pieces, held, sems, these=(0, 1, 2, 4, 5, 6), blocks=blocks
    )
    for there in range(depth):
        for core in range(2):
            owner = ((there * 2 + core) * 2 + (1 - y)) * 2 + (1 - x)
            held[pl.ds(owner * blocks, blocks)] = jnp.zeros((blocks, rows, width), held.dtype)
    span = 8 * blocks
    for k, column in enumerate(arrivals):
        for copy in column:
            copy.wait()
        there = z ^ k
        lanes = pl.ds(pl.multiple_of(there * (span * rows), span * rows), span * rows)
        part = wide_dot(active[:, lanes], rows_of(held[pl.ds(there * span, span)]))
        partial[...] = part if k == 0 else partial[...] + part


def reduce_first(grid, place, active, pieces):
    count, hidden = active.shape
    blocks, rows, width = pieces[0].shape[1:]
    return whole_call(
        functools.partial(reduce_first_kernel, grid.depth),
        "reduce_first",
        [(place, pltpu.SMEM), active] + [(piece, pl.ANY) for piece in pieces],
        [((count, width), jnp.float32)],
        [
            pltpu.VMEM((grid.count * blocks, rows, width), jnp.bfloat16),
            pltpu.SemaphoreType.DMA((grid.count,)),
        ],
    )[0]


def reduce_finish_kernel(depth, place, active, partial, second, gains, output_grad, *refs):
    corners, (output, d_summed, d_branch, norm_terms) = refs[:2], refs[2:]
    z, c, y, x = place[0], place[1], place[2], place[3]
    summed = RESIDUAL_SCALE * second[...] + partial[...]
    for k in range(depth):
        for dc in range(2):
            piece = rows_of(corners[dc][k])
            rows = piece.shape[0]
            owner = (((z ^ k) * 2 + (c ^ dc)) * 2 + (1 - y)) * 2 + (1 - x)
            summed += wide_dot(active[:, pl.ds(pl.multiple_of(owner * rows, rows), rows)], piece)
    final, scaled, inverse = norm_rows_of(summed, gains[4:5, :], gains[5:6, :])
    output[...] = final.astype(jnp.bfloat16)
    d_sum, norm_terms[0:1, :], norm_terms[1:2, :] = norm_rows_back(
        output_grad[...].astype(jnp.float32), scaled, inverse, gains[4:5, :]
    )
    d_summed[...] = d_sum
    d_branch[...] = d_sum.astype(jnp.bfloat16)


def reduce_finish(grid, place, active, partial, second, gains, output_grad, corners):
    shape = second.shape
    low, full = jnp.bfloat16, jnp.float32
    return whole_call(
        functools.partial(reduce_finish_kernel, grid.depth),
        "reduce_finish",
        [(place, pltpu.SMEM), active, partial, second, gains, output_grad, *corners],
        [(shape, low), (shape, full), (shape, low), ((2, shape[1]), full)],
    )


def reduce_back_kernel(depth, place, d_branch, slope, *refs):
    pieces, (d_inner, held, sems) = refs[:8], refs[8:]
    blocks, rows, width = pieces[0].shape[1:]
    arrivals = arrivals_of(depth, rows, place, in_last, pieces, held, sems, blocks=blocks)
    left = d_branch[...]
    step = 512 // rows
    tiles = 8 * blocks // step
    for k, column in enumerate(arrivals):
        for copy in column:
            copy.wait()
        for n in range(tiles):
            j = (place[0] ^ k) * tiles + n
            lanes = pl.ds(pl.multiple_of(j * 512, 512), 512)
            d_active = dot_rows(left, rows_of(held[pl.ds(j * step, step)]))
            d_inner[:, lanes] = (d_active * slope[:, lanes]).astype(jnp.bfloat16)


def reduce_back(grid, place, d_branch, slope, pieces):
    count, hidden = slope.shape
    blocks, rows, width = pieces[0].shape[1:]
    return whole_call(
        functools.partial(reduce_back_kernel, grid.depth),
        "reduce_back",
        [(place, pltpu.SMEM), d_branch, slope] + [(piece, pl.ANY) for piece in pieces],
        [((count, hidden), jnp.bfloat16)],
        [
            pltpu.VMEM((grid.count * blocks, rows, width), jnp.bfloat16),
            pltpu.SemaphoreType.DMA((grid.count,)),
        ],
    )[0]


def expand_back_kernel(d_inner, expand, d_sum_three, scaled, inverse, gains, out_weight, d_summed, d_branch, d_context, norm_terms):
    d_second = RESIDUAL_SCALE * d_sum_three[...]
    block = expand.shape[2]
    for n in range(expand.shape[0]):
        d_second += dot_rows(d_inner[:, n * block : (n + 1) * block], expand[n])
    d_sum, norm_terms[0:1, :], norm_terms[1:2, :] = norm_rows_back(
        d_second, scaled[...], inverse[...], gains[2:3, :]
    )
    d_summed[...] = d_sum
    d_branch[...] = d_sum.astype(jnp.bfloat16)
    d_context[...] = dot_rows(d_branch[...], out_weight[0]).astype(jnp.bfloat16)


def expand_back(d_inner, expand, d_sum_three, scaled, inverse, gains, second_full):
    shape = d_sum_three.shape
    width = shape[1]
    low, full = jnp.bfloat16, jnp.float32
    return whole_call(
        expand_back_kernel,
        "expand_back",
        [d_inner, expand, d_sum_three, scaled, inverse, gains]
        + [(second_full, (1, width, width), (3, 0, 0))],
        [(shape, full), (shape, low), (shape, low), ((2, width), full)],
    )


def cross_back_kernel(
    query, key, value, logsum, d_context, ids_column, ids_row, d_branch_two, d_sum_two, scaled, inverse, gains,
    query_weight, out_weight, back, d_summed, d_context_one, norm_terms, allowed,
):
    count, others = query.shape[0], key.shape[0]
    cross_allowed(ids_column, ids_row, allowed)
    rows = back.at[0]
    d_query = rows.at[count : 2 * count]
    d_key = rows.at[3 * count : 3 * count + others]
    d_value = rows.at[3 * count + others : 3 * count + 2 * others]
    attend_heads_back(query, key, value, allowed, logsum, d_context, d_query, d_key, d_value)
    d_first = RESIDUAL_SCALE * d_sum_two[...] + dot_rows(d_query[...], query_weight[0])
    d_sum, norm_terms[0:1, :], norm_terms[1:2, :] = norm_rows_back(
        d_first, scaled[...], inverse[...], gains[0:1, :]
    )
    d_summed[...] = d_sum
    d_branch = d_sum.astype(jnp.bfloat16)
    rows[0:count, :] = d_branch_two[...]
    rows[2 * count : 3 * count, :] = d_branch
    back[1] = rows[...]
    d_context_one[...] = dot_rows(d_branch, out_weight[0]).astype(jnp.bfloat16)


def cross_back(query, key, value, logsum, d_context, ids_column, ids_row, d_branch_two, d_sum_two, scaled, inverse, gains, second_full, first_full):
    shape, other_shape = query.shape, key.shape
    width = shape[1]
    low, full = jnp.bfloat16, jnp.float32
    block = (1, width, width)
    return whole_call(
        cross_back_kernel,
        "cross_back",
        [query, key, value, logsum, d_context, ids_column, ids_row, d_branch_two, d_sum_two, scaled, inverse, gains]
        + [(second_full, block, (0, 0, 0)), (first_full, block, (3, 0, 0))],
        [((2, 3 * shape[0] + 2 * other_shape[0], width), low), (shape, full), (shape, low), ((2, width), full)],
        [pltpu.VMEM((shape[0], other_shape[0]), full)],
    )


def self_back_kernel(query, key, value, logsum, d_context, ids_column, ids_row, d_rows, allowed):
    self_allowed(ids_column, ids_row, allowed)
    count = query.shape[0]
    outs = [d_rows.at[n * count : (n + 1) * count] for n in range(3)]
    attend_heads_back(query, key, value, allowed, logsum, d_context, *outs)


def self_back(query, key, value, logsum, d_context, ids_column, ids_row):
    count, width = query.shape
    return whole_call(
        self_back_kernel,
        "self_back",
        [query, key, value, logsum, d_context, ids_column, ids_row],
        [((3 * count, width), jnp.bfloat16)],
        [pltpu.VMEM((count, count), jnp.float32)],
    )[0]


def inputs_back_kernel(d_rows, d_key, d_value, d_sum_one, w_query, w_key, w_value, w_key_two, w_value_two, tokens_grad, memory_grad):
    count = d_sum_one.shape[0]
    total = RESIDUAL_SCALE * d_sum_one[...]
    for n, weight in enumerate((w_query, w_key, w_value)):
        total += dot_rows(d_rows[n * count : (n + 1) * count, :], weight[0])
    tokens_grad[...] = total
    memory_grad[...] = dot_rows(d_key[0], w_key_two[0]) + dot_rows(d_value[0], w_value_two[0])


def inputs_back(d_rows, back, d_sum_one, first_full, second_full):
    count, width = d_sum_one.shape
    others = (back.shape[1] - 3 * count) // 2
    first_row = 3 * count // others
    block = (1, width, width)
    return whole_call(
        inputs_back_kernel,
        "inputs_back",
        [d_rows]
        + [(back, (1, others, width), (0, first_row + n, 0)) for n in (0, 1)]
        + [d_sum_one]
        + [(first_full, block, (n, 0, 0)) for n in range(3)]
        + [(second_full, block, (n, 0, 0)) for n in (1, 2)],
        [((count, width), jnp.float32), ((others, width), jnp.float32)],
    )


def turn(depth, rows, place, sources, turned, spots=range(4)):
    z, c, y, x = place[0], place[1], place[2], place[3]
    tokens = sources[0].shape[0]
    for k in range(depth):
        there = z ^ k
        columns = pl.ds(pl.multiple_of((there * 2 + c) * (4 * rows), 4 * rows), 4 * rows)
        for side, source in enumerate(sources):
            block = source[:, columns].T
            named = [block[n * rows : (n + 1) * rows] for n in range(4)]
            named = [jnp.where(x == 0, named[n], named[n ^ 1]) for n in range(4)]
            named = [jnp.where(y == 0, named[n], named[n ^ 2]) for n in range(4)]
            for at, spot in enumerate(spots):
                turned[at, k * rows : (k + 1) * rows, side * tokens : (side + 1) * tokens] = named[spot]


def spread(depth, rows, turned, rights, outs, spots=range(4)):
    tokens = rights[0].shape[0]
    half = depth // 2
    for at, spot in enumerate(spots):
        part = turned[at]
        total = jnp.dot(part[:, :tokens], rights[0][...], preferred_element_type=jnp.float32)
        total += jnp.dot(
            part[:, tokens : 2 * tokens], rights[1][...], preferred_element_type=jnp.float32
        )
        total = total.astype(jnp.bfloat16).reshape(depth, rows, -1)
        if spot < 3:
            outs[at][...] = total
        else:
            outs[at][...] = total[:half]
            outs[at + 1][...] = total[half:]


def tiled_kernel(depth, rows, spots, place, left, left_far, right, right_far, *refs):
    outs, turned = refs[:-1], refs[-1]

    @pl.when(pl.program_id(0) == 0)
    def _():
        turn(depth, rows, place, (left, left_far), turned, spots)

    spread(depth, rows, turned, (right, right_far), outs, spots)


def group_kernel(depth, rows, count, by_core, place, *refs):
    each = 3 if by_core else 4
    core = place[1]
    inputs, outs, turned = refs[: each * count], refs[each * count : each * count + 5], refs[-1]
    for m in range(count):
        left, left_far, *rights = inputs[each * m : each * m + each]
        if by_core:
            rights = (rights[0].at[core], rights[0].at[1 - core])
        turn(depth, rows, place, (left, left_far), turned)
        spread(depth, rows, turned, rights, [out.at[:, m] for out in outs])


def piece_counts(depth, spots=range(4)):
    counts = []
    for spot in spots:
        counts += [depth] if spot < 3 else [depth // 2, depth // 2]
    return counts


def tiled_terms(grid, place, left, left_far, right, right_far, tile, spots=range(4)):
    tokens, features = left.shape
    width = right.shape[1]
    rows = features // grid.count
    left_row = 4 if left_far.shape[0] != tokens else 0
    counts = piece_counts(grid.depth, spots)
    return pl.pallas_call(
        functools.partial(tiled_kernel, grid.depth, rows, spots),
        grid=(width // tile,),
        out_shape=[jax.ShapeDtypeStruct((n, rows, width), jnp.bfloat16) for n in counts],
        in_specs=[
            pl.BlockSpec(memory_space=pltpu.SMEM),
            pl.BlockSpec((tokens, features), lambda j: (0, 0)),
            pl.BlockSpec((tokens, features), lambda j: (left_row, 0)),
        ]
        + [pl.BlockSpec((tokens, tile), lambda j: (0, j))] * 2,
        out_specs=[pl.BlockSpec((n, rows, tile), lambda j: (0, 0, j)) for n in counts],
        scratch_shapes=[pltpu.VMEM((len(spots), grid.depth * rows, 2 * tokens), jnp.bfloat16)],
        compiler_params=pltpu.CompilerParams(vmem_limit_bytes=40 * 2**20),
        cost_estimate=pl.CostEstimate(flops=1, bytes_accessed=1, transcendentals=0),
        name="terms",
    )(place, left, left_far, right, right_far)


def group_terms(grid, place, held, held_far, right, right_far, pairs):
    by_core = right_far is None
    width = held.shape[1]
    rows = width // grid.count
    arrays, specs = [], []
    for tokens, left_row, right_row in pairs:
        arrays += [held, held_far, right]
        specs += [pl.BlockSpec((tokens, width), lambda i, row=left_row: (row, 0))] * 2
        if by_core:
            specs += [pl.BlockSpec((2, tokens, width), lambda i, row=right_row: (0, row, 0))]
        else:
            arrays += [right_far]
            specs += [pl.BlockSpec((tokens, width), lambda i, row=right_row: (row, 0))] * 2
    most = max(tokens for tokens, _, _ in pairs)
    shapes = [(n, len(pairs), rows, width) for n in piece_counts(grid.depth)]
    return pl.pallas_call(
        functools.partial(group_kernel, grid.depth, rows, len(pairs), by_core),
        grid=(1,),
        out_shape=[jax.ShapeDtypeStruct(shape, jnp.bfloat16) for shape in shapes],
        in_specs=[pl.BlockSpec(memory_space=pltpu.SMEM)] + specs,
        out_specs=[pl.BlockSpec(shape, lambda i: (0, 0, 0, 0)) for shape in shapes],
        scratch_shapes=[pltpu.VMEM((4, grid.depth * rows, 2 * most), jnp.bfloat16)],
        compiler_params=pltpu.CompilerParams(vmem_limit_bytes=48 * 2**20),
        cost_estimate=pl.CostEstimate(flops=1, bytes_accessed=1, transcendentals=0),
        name="terms",
    )(place, *arrays)


def corner_kernel(over_x, low, over_y, high, sent_x, sent_y):
    wide = jnp.float32
    sent_x[...] = (over_x[...].astype(wide) + low[...].astype(wide)).astype(jnp.bfloat16)
    sent_y[...] = (over_y[...].astype(wide) + high[...].astype(wide)).astype(jnp.bfloat16)


def corner_added(grid, pieces, low, high):
    zeros = (0,) * (low.ndim - 1)
    first = pl.BlockSpec(low.shape, lambda i: (0,) + zeros)
    second = pl.BlockSpec(low.shape, lambda i: (1,) + zeros)
    return pl.pallas_call(
        corner_kernel,
        grid=(1,),
        out_shape=[jax.ShapeDtypeStruct(pieces[n].shape, jnp.bfloat16) for n in (1, 2)],
        in_specs=[first, first, second, first],
        out_specs=[first, second],
        input_output_aliases={0: 0, 2: 1},
        compiler_params=pltpu.CompilerParams(vmem_limit_bytes=32 * 2**20),
        cost_estimate=pl.CostEstimate(flops=1, bytes_accessed=1, transcendentals=0),
        name="corner_added",
    )(pieces[1], low, pieces[2], high)


def plane_sum(own, over_x, over_y):
    wide = jnp.float32
    return (own.astype(wide) + over_x.astype(wide) + over_y.astype(wide)).astype(jnp.bfloat16)


def plane_sums(grid, pieces, over_x, over_y):
    half = grid.depth // 2
    return [
        plane_sum(pieces[0][part], over_x[part], over_y[part]) for part in (slice(0, half), slice(half, None))
    ]


def pair_sum(near, got):
    return (near[1].astype(jnp.float32) + got[1].astype(jnp.float32)).astype(jnp.bfloat16)


def total_of(*terms_of):
    return sum([term.astype(jnp.float32) for term in terms_of[1:]], terms_of[0].astype(jnp.float32))


def fetch(attention_rows, expand_rows, reduce_rows, norm_rows):
    gathered = (
        lax.all_gather(attention_rows, ("dp", "fsdp"), axis=1, tiled=True),
        lax.all_gather(expand_rows, ("dp", "fsdp"), axis=0, tiled=True),
        lax.all_gather(reduce_rows, ("dp", "fsdp"), axis=0, tiled=True),
        lax.all_gather(norm_rows, ("dp", "fsdp"), axis=1, tiled=True),
    )
    return gathered


def settle(attention_terms, expand_terms, reduce_terms, norm_terms):
    owned = (
        lax.psum_scatter(attention_terms, ("dp", "fsdp"), scatter_dimension=1, tiled=True),
        lax.psum_scatter(expand_terms, ("dp", "fsdp"), scatter_dimension=0, tiled=True),
        lax.psum_scatter(reduce_terms, ("dp", "fsdp"), scatter_dimension=0, tiled=True),
        lax.psum_scatter(norm_terms, ("dp", "fsdp"), scatter_dimension=1, tiled=True),
    )
    return owned


def matmul(left, right):
    return jnp.dot(left, right, preferred_element_type=jnp.float32)


def across(left, right):
    return jnp.einsum("ti,tj->ij", left, right, preferred_element_type=jnp.float32)


def against(left, right):
    return jnp.einsum("ti,ji->tj", left, right, preferred_element_type=jnp.float32)


def gelu_tanh(values):
    return jax.nn.gelu(values, approximate=True)


def normalize(summed, gain, shift):
    center = jnp.mean(summed, axis=-1, keepdims=True)
    centred = summed - center
    inverse = lax.rsqrt(jnp.mean(centred * centred, axis=-1, keepdims=True) + EPSILON)
    scaled = centred * inverse
    return (scaled * gain + shift, scaled, inverse)


def normalize_back(incoming, scaled, inverse, gain):
    spread = incoming * gain
    d_summed = inverse * (
        spread
        - jnp.mean(spread, axis=-1, keepdims=True)
        - scaled * jnp.mean(spread * scaled, axis=-1, keepdims=True)
    )
    return (d_summed, jnp.sum(incoming * scaled, axis=0), jnp.sum(incoming, axis=0))


def split_heads(matrix):
    return matrix.reshape(matrix.shape[0], HEADS, HEAD_DIM)


def scores_of(query_rows, key_rows, allowed):
    raw = jnp.einsum(
        "qhd,khd->hqk",
        split_heads(query_rows),
        split_heads(key_rows),
        preferred_element_type=jnp.float32,
    ) * HEAD_DIM ** (-0.5)
    return jnp.where(allowed[None], raw, NEGATIVE)


def attend_forward(query_rows, key_rows, value_rows, allowed):
    scores = scores_of(query_rows, key_rows, allowed)
    highest = jnp.max(scores, axis=-1, keepdims=True)
    weights = jnp.exp(scores - highest)
    totals = jnp.sum(weights, axis=-1, keepdims=True)
    chances = (weights / totals).astype(jnp.bfloat16)
    context = jnp.einsum(
        "hqk,khd->qhd", chances, split_heads(value_rows), preferred_element_type=jnp.float32
    )
    return (
        context.reshape(query_rows.shape[0], HEADS * HEAD_DIM).astype(jnp.bfloat16),
        highest + jnp.log(totals),
    )


def attend_back(query_rows, key_rows, value_rows, allowed, logsum, d_context):
    query_heads = split_heads(query_rows)
    key_heads = split_heads(key_rows)
    d_heads = split_heads(d_context)
    chances = jnp.exp(scores_of(query_rows, key_rows, allowed) - logsum)
    d_chances = jnp.einsum(
        "qhd,khd->hqk", d_heads, split_heads(value_rows), preferred_element_type=jnp.float32
    )
    d_value = jnp.einsum(
        "hqk,qhd->khd", chances.astype(jnp.bfloat16), d_heads, preferred_element_type=jnp.float32
    )
    centre = jnp.sum(d_chances * chances, axis=-1, keepdims=True)
    d_scores = (chances * (d_chances - centre)).astype(jnp.bfloat16)
    d_query = jnp.einsum(
        "hqk,khd->qhd", d_scores, key_heads, preferred_element_type=jnp.float32
    ) * HEAD_DIM ** (-0.5)
    d_key = jnp.einsum(
        "hqk,qhd->khd", d_scores, query_heads, preferred_element_type=jnp.float32
    ) * HEAD_DIM ** (-0.5)
    query_count = query_rows.shape[0]
    key_count = key_rows.shape[0]
    return (
        d_query.reshape(query_count, HEADS * HEAD_DIM).astype(jnp.bfloat16),
        d_key.reshape(key_count, HEADS * HEAD_DIM).astype(jnp.bfloat16),
        d_value.reshape(key_count, HEADS * HEAD_DIM).astype(jnp.bfloat16),
    )


def plain_device(
    tokens,
    memory,
    target_segments,
    source_segments,
    self_query,
    self_key,
    self_value,
    self_output,
    cross_query,
    cross_key,
    cross_value,
    cross_output,
    expand_weight,
    reduce_weight,
    self_gain,
    self_shift,
    cross_gain,
    cross_shift,
    final_gain,
    final_shift,
    output_grad,
):
    attention_rows = jnp.stack(
        [
            self_query,
            self_key,
            self_value,
            self_output,
            cross_query,
            cross_key,
            cross_value,
            cross_output,
        ]
    )
    norm_rows = jnp.stack([self_gain, self_shift, cross_gain, cross_shift, final_gain, final_shift])
    matrices, expand_full, reduce_full, norm_full = fetch(
        attention_rows, expand_weight, reduce_weight, norm_rows
    )
    gains = norm_full.astype(jnp.float32)
    target_ids = target_segments[0]
    source_ids = source_segments[0]
    positions = lax.iota(jnp.int32, tokens.shape[0])
    causal = (target_ids[:, None] == target_ids[None, :]) & (
        positions[None, :] <= positions[:, None]
    )
    crossing = target_ids[:, None] == source_ids[None, :]
    query_one = matmul(tokens, matrices[0]).astype(jnp.bfloat16)
    key_one = matmul(tokens, matrices[1]).astype(jnp.bfloat16)
    value_one = matmul(tokens, matrices[2]).astype(jnp.bfloat16)
    context_one, logsum_one = attend_forward(query_one, key_one, value_one, causal)
    branch_one = matmul(context_one, matrices[3])
    first, first_scaled, first_inverse = normalize(
        RESIDUAL_SCALE * tokens.astype(jnp.float32) + branch_one, gains[0], gains[1]
    )
    first_low = first.astype(jnp.bfloat16)
    query_two = matmul(first_low, matrices[4]).astype(jnp.bfloat16)
    key_two = matmul(memory, matrices[5]).astype(jnp.bfloat16)
    value_two = matmul(memory, matrices[6]).astype(jnp.bfloat16)
    context_two, logsum_two = attend_forward(query_two, key_two, value_two, crossing)
    branch_two = matmul(context_two, matrices[7])
    second, second_scaled, second_inverse = normalize(
        RESIDUAL_SCALE * first + branch_two, gains[2], gains[3]
    )
    second_low = second.astype(jnp.bfloat16)
    inner = matmul(second_low, expand_full)
    active = gelu_tanh(inner).astype(jnp.bfloat16)
    branch_three = matmul(active, reduce_full)
    final, final_scaled, final_inverse = normalize(
        RESIDUAL_SCALE * second + branch_three, gains[4], gains[5]
    )
    output = final.astype(jnp.bfloat16)
    matrices, expand_full, reduce_full, norm_full = fetch(
        attention_rows, expand_weight, reduce_weight, norm_rows
    )
    gains = norm_full.astype(jnp.float32)
    d_sum_three, final_gain_term, final_shift_term = normalize_back(
        output_grad.astype(jnp.float32), final_scaled, final_inverse, gains[4]
    )
    d_branch_three = d_sum_three.astype(jnp.bfloat16)
    reduce_term = across(active, d_branch_three)
    d_active = against(d_branch_three, reduce_full)
    d_inner = jax.vjp(gelu_tanh, inner)[1](d_active)[0].astype(jnp.bfloat16)
    expand_term = across(second_low, d_inner)
    d_second = RESIDUAL_SCALE * d_sum_three + against(d_inner, expand_full)
    d_sum_two, cross_gain_term, cross_shift_term = normalize_back(
        d_second, second_scaled, second_inverse, gains[2]
    )
    d_branch_two = d_sum_two.astype(jnp.bfloat16)
    cross_output_term = across(context_two, d_branch_two)
    d_context_two = against(d_branch_two, matrices[7]).astype(jnp.bfloat16)
    d_query_two, d_key_two, d_value_two = attend_back(
        query_two, key_two, value_two, crossing, logsum_two, d_context_two
    )
    cross_query_term = across(first_low, d_query_two)
    cross_key_term = across(memory, d_key_two)
    cross_value_term = across(memory, d_value_two)
    memory_grad = against(d_key_two, matrices[5]) + against(d_value_two, matrices[6])
    d_first = RESIDUAL_SCALE * d_sum_two + against(d_query_two, matrices[4])
    d_sum_one, self_gain_term, self_shift_term = normalize_back(
        d_first, first_scaled, first_inverse, gains[0]
    )
    d_branch_one = d_sum_one.astype(jnp.bfloat16)
    self_output_term = across(context_one, d_branch_one)
    d_context_one = against(d_branch_one, matrices[3]).astype(jnp.bfloat16)
    d_query_one, d_key_one, d_value_one = attend_back(
        query_one, key_one, value_one, causal, logsum_one, d_context_one
    )
    self_query_term = across(tokens, d_query_one)
    self_key_term = across(tokens, d_key_one)
    self_value_term = across(tokens, d_value_one)
    tokens_grad = (
        RESIDUAL_SCALE * d_sum_one
        + against(d_query_one, matrices[0])
        + against(d_key_one, matrices[1])
        + against(d_value_one, matrices[2])
    )
    attention_terms = jnp.stack(
        [
            self_query_term,
            self_key_term,
            self_value_term,
            self_output_term,
            cross_query_term,
            cross_key_term,
            cross_value_term,
            cross_output_term,
        ]
    )
    norm_terms = jnp.stack(
        [
            self_gain_term,
            self_shift_term,
            cross_gain_term,
            cross_shift_term,
            final_gain_term,
            final_shift_term,
        ]
    )
    attention_owned, expand_owned, reduce_owned, norm_owned = settle(
        attention_terms, expand_term, reduce_term, norm_terms
    )
    return (
        output,
        tokens_grad,
        memory_grad,
        attention_owned[0],
        attention_owned[1],
        attention_owned[2],
        attention_owned[3],
        attention_owned[4],
        attention_owned[5],
        attention_owned[6],
        attention_owned[7],
        expand_owned,
        reduce_owned,
        norm_owned[0],
        norm_owned[1],
        norm_owned[2],
        norm_owned[3],
        norm_owned[4],
        norm_owned[5],
    )


def per_device(
    grid,
    tokens,
    memory,
    target_segments,
    source_segments,
    self_query,
    self_key,
    self_value,
    self_output,
    cross_query,
    cross_key,
    cross_value,
    cross_output,
    expand_weight,
    reduce_weight,
    self_gain,
    self_shift,
    cross_gain,
    cross_shift,
    final_gain,
    final_shift,
    output_grad,
):
    if not grid.fast:
        return plain_device(
            tokens,
            memory,
            target_segments,
            source_segments,
            self_query,
            self_key,
            self_value,
            self_output,
            cross_query,
            cross_key,
            cross_value,
            cross_output,
            expand_weight,
            reduce_weight,
            self_gain,
            self_shift,
            cross_gain,
            cross_shift,
            final_gain,
            final_shift,
            output_grad,
        )
    place = grid.place()
    held_rows = self_gain.shape[0]
    norm_rows = jnp.stack([self_gain, self_shift, cross_gain, cross_shift, final_gain, final_shift])
    extra = jnp.zeros((16, held_rows * grid.count), jnp.bfloat16)
    extra = lax.dynamic_update_slice(extra, norm_rows, (0, grid.index() * held_rows))
    extra = extra.reshape(4, 32, 128)
    first_rows = jnp.concatenate([jnp.stack([self_query, self_key, self_value, self_output]), extra], axis=-1)
    second_rows = jnp.stack([cross_query, cross_key, cross_value, cross_output])
    target_column, target_row = target_segments.reshape(-1, 1), target_segments
    source_row = source_segments

    half = grid.depth // 2
    width = expand_weight.shape[1] // 4
    expand_rows = jnp.stack([expand_weight[:, n * width : (n + 1) * width] for n in range(4)])
    reduce_rows = reduce_weight.reshape(expand_rows.shape)

    first_z = [grid.move(first_rows, dz=k) for k in (2, 3, 1)]
    second_z = grid.move(second_rows, dz=1)
    first_own = jnp.stack([first_rows, first_z[2], first_z[0], first_z[1]])
    second_pair = jnp.stack([second_rows, second_z])
    first_own, second_pair, expand_rows, reduce_rows = after(
        (first_own, second_pair, expand_rows, reduce_rows)
    )
    first_x, first_y = grid.move(first_own, dx=1), grid.move(first_own, dy=1)
    second_z = grid.move(second_pair, dz=2)
    expand_z = grid.move(expand_rows, dz=1)
    reduce_z = grid.move(reduce_rows, dz=1)
    first_x, first_y, second_z, expand_z, reduce_z = after((first_x, first_y, second_z, expand_z, reduce_z))
    second_own = jnp.concatenate([second_pair, second_z])
    expand_pair = jnp.stack([expand_rows, expand_z])
    first_low, first_high, second_own, expand_pair = after(
        (first_x[:half], first_y[half:], second_own, expand_pair)
    )
    first_low, first_high = grid.move(first_low, dy=1), grid.move(first_high, dx=1)
    second_x, second_y = grid.move(second_own, dx=1), grid.move(second_own, dy=1)
    expand_z = grid.move(expand_pair, dz=2)
    first_low, first_high, second_x, second_y, expand_z = after(
        (first_low, first_high, second_x, second_y, expand_z)
    )
    reduce_pair = jnp.stack([reduce_rows, reduce_z])
    first_near = jnp.concatenate([first_own, first_x, first_y, first_low, first_high])
    sides = jnp.concatenate([second_own, second_x, second_y, expand_pair, expand_z])
    sent_y = jnp.concatenate([second_x[:half], expand_pair, expand_z])
    sent_x = jnp.concatenate([second_y[half:], expand_pair, expand_z])
    sent_x, sent_y, reduce_pair, first_near, sides = after((sent_x, sent_y, reduce_pair, first_near, sides))
    got_x, got_y = grid.move(sent_x, dx=1), grid.move(sent_y, dy=1)
    reduce_z = grid.move(reduce_pair, dz=2)
    first_far = grid.move(first_near, dc=1)
    sides_far = grid.move(sides, dc=1)
    first_out = self_forward(grid, place, tokens, target_column, target_row, (first_near, first_far))
    first_out, got_x, got_y, reduce_z, sides_far = after((first_out, got_x, got_y, reduce_z, sides_far))
    first_full, gains, query_one, key_one, value_one, context_one, logsum_one = first_out[:7]
    first, first_low, first_scaled, first_inverse = first_out[7:]
    reduce_own = jnp.concatenate([reduce_pair, reduce_z])
    sent_y = jnp.concatenate([got_x[half : 2 * half], reduce_pair, reduce_z])
    sent_x = jnp.concatenate([got_y[2 * half :], reduce_pair, reduce_z])
    sent_x, sent_y, got_x, got_y, reduce_own = after((sent_x, sent_y, got_x, got_y, reduce_own))
    last_x, last_y = grid.move(sent_x, dx=1), grid.move(sent_y, dy=1)
    got_x_far, got_y_far = grid.move(got_x, dc=1), grid.move(got_y, dc=1)
    reduce_own_far = grid.move(reduce_own, dc=1)
    second_out = cross_forward(
        grid, place, first, first_low, memory, gains, target_column, source_row,
        (sides, got_y, got_x, sides_far, got_y_far, got_x_far),
    )
    second_out, last_x, last_y, reduce_own_far = after((second_out, last_x, last_y, reduce_own_far))
    second_full, query_two, key_two, value_two, context_two, logsum_two = second_out[:6]
    second, second_low, second_scaled, second_inverse = second_out[6:]
    reduce_low, reduce_high, last_x, last_y = after(
        (last_x[half : 2 * half], last_y[2 * half :], last_x, last_y)
    )
    reduce_low, reduce_high = grid.move(reduce_low, dy=1), grid.move(reduce_high, dx=1)
    last_x_far, last_y_far = grid.move(last_x, dc=1), grid.move(last_y, dc=1)
    expand_full, active, slope = expand_forward(
        grid, place, second_low,
        (sides, got_x, got_y, last_y, last_x, sides_far, got_x_far, got_y_far, last_y_far, last_x_far),
    )
    held = jnp.concatenate([tokens, context_one, first_low, context_two, second_low, memory])
    held, active = after((held, active))
    held_far = grid.move(held, dc=1)
    active_far = grid.move(active, dc=1)
    reduce_low, reduce_high, active = after((reduce_low, reduce_high, active))
    reduce_corner, active = after((jnp.concatenate([reduce_low, reduce_high]), active))
    reduce_corner_far = grid.move(reduce_corner, dc=1)
    partial = reduce_first(
        grid, place, active, (reduce_own, last_x, last_y, reduce_own_far, last_x_far, last_y_far)
    )
    reduce_pieces = (
        reduce_own, last_x, last_y, reduce_corner, reduce_own_far, last_x_far, last_y_far, reduce_corner_far
    )
    reduce_corner = (reduce_corner, reduce_corner_far)
    output, d_sum_three, d_branch_three, final_norm_terms = reduce_finish(
        grid, place, active, partial, second, gains, output_grad, reduce_corner
    )
    d_branches = (d_branch_three, grid.move(d_branch_three, dc=1))
    reduce_low, reduce_high = after(
        tuple(tiled_terms(grid, place, active, active_far, *d_branches, 1024, (3,)))
    )
    reduce_terms = tiled_terms(
        grid, place, after(active, reduce_low), active_far, *d_branches, 512, (0, 1, 2)
    )
    d_inner = reduce_back(grid, place, after(d_branch_three, *reduce_terms), slope, reduce_pieces)
    reduce_low, reduce_high = grid.move(reduce_low, dy=1), grid.move(reduce_high, dx=1)
    reduce_low, reduce_high, d_inner = after((reduce_low, reduce_high, d_inner))
    reduce_sends = corner_added(grid, reduce_terms, reduce_low, reduce_high)
    reduce_sends, d_inner = after((reduce_sends, d_inner))
    reduce_x, reduce_y = grid.move(reduce_sends[0], dx=1), grid.move(reduce_sends[1], dy=1)
    d_inner_far = grid.move(d_inner, dc=1)
    d_sum_two, d_branch_two, d_context_two, cross_norm_terms = expand_back(
        d_inner, expand_full, d_sum_three, second_scaled, second_inverse, gains, second_full
    )
    expand_terms = tiled_terms(grid, place, second_low, held_far, after(d_inner, d_context_two), d_inner_far, 1024)
    expand_terms, d_context_two = after((expand_terms, d_context_two))
    expand_low, expand_high = grid.move(expand_terms[3], dy=1), grid.move(expand_terms[4], dx=1)
    back, d_sum_one, d_context_one, self_norm_terms = cross_back(
        query_two, key_two, value_two, logsum_two, d_context_two, target_column,
        source_row, d_branch_two, d_sum_two, first_scaled, first_inverse, gains, second_full, first_full,
    )
    norm_terms = jnp.concatenate([self_norm_terms, cross_norm_terms, final_norm_terms])
    expand_low, expand_high, reduce_x, reduce_y, back, norm_terms = after(
        (expand_low, expand_high, reduce_x, reduce_y, back, norm_terms)
    )
    expand_sends = corner_added(grid, expand_terms, expand_low, expand_high)
    expand_sends, back = after((expand_sends, back))
    expand_x, expand_y = grid.move(expand_sends[0], dx=1), grid.move(expand_sends[1], dy=1)
    reduce_near, reduce_pass = plane_sums(grid, reduce_terms, *after((reduce_x, reduce_y), expand_sends))
    reduce_near, reduce_pass, back = after((reduce_near, reduce_pass, back))
    reduce_got = grid.move(reduce_pass, dz=2)
    backs = grid.cores(back)
    pairs = [(256, 1, 2), (256, 2, 1), (128, 10, 6), (128, 10, 7), (256, 3, 0)]
    cross_terms = group_terms(grid, place, held, held_far, backs, None, pairs)
    cross_terms, d_context_one = after((cross_terms, d_context_one))
    cross_low, cross_high = grid.move(cross_terms[3], dy=1), grid.move(cross_terms[4], dx=1)
    back_one = self_back(
        query_one, key_one, value_one, logsum_one, d_context_one, target_column, target_row
    )
    cross_low, cross_high, back_one, reduce_got, expand_x, expand_y = after(
        (cross_low, cross_high, back_one, reduce_got, expand_x, expand_y)
    )
    cross_sends = corner_added(grid, cross_terms, cross_low, cross_high)
    reduce_leaving = pair_sum(reduce_near, reduce_got)
    cross_sends, back_one, reduce_leaving = after((cross_sends, back_one, reduce_leaving))
    cross_x, cross_y = grid.move(cross_sends[0], dx=1), grid.move(cross_sends[1], dy=1)
    back_one_far = grid.move(back_one, dc=1)
    reduce_last = grid.move(reduce_leaving, dz=1)
    expand_near, expand_pass = plane_sums(grid, expand_terms, *after((expand_x, expand_y), cross_sends))
    expand_near, expand_pass, back_one = after((expand_near, expand_pass, back_one))
    expand_got = grid.move(expand_pass, dz=2)
    self_terms = group_terms(
        grid, place, held, held_far, back_one, back_one_far, [(256, 0, n) for n in range(3)]
    )
    tokens_grad, memory_grad = inputs_back(
        after(back_one, *self_terms), back, d_sum_one, first_full, second_full
    )
    expand_got, reduce_last, self_low, self_high = after(
        (expand_got, reduce_last, self_terms[3], self_terms[4]), tokens_grad
    )
    expand_leaving = pair_sum(expand_near, expand_got)
    self_low, self_high, expand_leaving = after((self_low, self_high, expand_leaving))
    self_low, self_high = grid.move(self_low, dy=1), grid.move(self_high, dx=1)
    expand_last = grid.move(expand_leaving, dz=1)
    cross_x, cross_y = after((cross_x, cross_y), expand_leaving)
    cross_pass = after(plane_sum(cross_terms[0][half:], cross_x[half:], cross_y[half:]))
    cross_got = grid.move(cross_pass, dz=2)
    cross_x, cross_y = after((cross_x, cross_y), cross_pass)
    cross_near = after(plane_sum(cross_terms[0][:half], cross_x[:half], cross_y[:half]))
    self_low, self_high, expand_last = after((self_low, self_high, expand_last), cross_pass)
    self_sends = corner_added(grid, self_terms, self_low, self_high)
    self_sends, norm_terms = after((self_sends, norm_terms))
    self_x, self_y = grid.move(self_sends[0], dx=1), grid.move(self_sends[1], dy=1)
    norm_got = lax.all_to_all(norm_terms.reshape(6, grid.count, held_rows), grid.axes, 1, 0, tiled=True)
    cross_got, norm_got, self_x, self_y = after((cross_got, norm_got, self_x, self_y))
    self_column = [plane_sum(self_terms[0][k], self_x[k], self_y[k]) for k in range(grid.depth)]
    cross_leaving = pair_sum(cross_near, cross_got)
    self_column, cross_leaving = after((self_column, cross_leaving))
    self_others = [grid.move(self_column[k], dz=k) for k in (2, 3, 1)]
    cross_last = grid.move(cross_leaving, dz=1)
    reduce_term = total_of(reduce_near[0], reduce_got[0], reduce_last)
    expand_term = total_of(expand_near[0], expand_got[0], expand_last)
    cross_owned = total_of(cross_near[0], cross_got[0], cross_last)
    self_owned = total_of(self_column[0], *self_others)
    norm_owned = jnp.sum(norm_got.reshape(grid.count, 6, held_rows), axis=0)
    return (
        output,
        tokens_grad,
        memory_grad,
        *[self_owned[i] for i in range(3)],
        *[cross_owned[i] for i in range(5)],
        expand_term,
        reduce_term,
        *[norm_owned[i] for i in range(6)],
    )


def solution(mesh):
    grid = Grid(mesh)
    rows = P(grid.axes, None)
    parts = P(grid.axes)
    return jax.shard_map(
        functools.partial(per_device, grid),
        mesh=grid.mesh,
        in_specs=(
            rows,
            rows,
            rows,
            rows,
            rows,
            rows,
            rows,
            rows,
            rows,
            rows,
            rows,
            rows,
            rows,
            rows,
            parts,
            parts,
            parts,
            parts,
            parts,
            parts,
            rows,
        ),
        out_specs=(
            rows,
            rows,
            rows,
            rows,
            rows,
            rows,
            rows,
            rows,
            rows,
            rows,
            rows,
            rows,
            rows,
            parts,
            parts,
            parts,
            parts,
            parts,
            parts,
        ),
        check_vma=False,
    )
```

```python
import functools

import jax
import jax.numpy as jnp
from jax import lax
from jax.experimental import pallas as pl
from jax.experimental.pallas import tpu as pltpu
from jax.sharding import PartitionSpec as P

HEADS = 16
HEAD_DIM = 64


RESIDUAL_SCALE = 300.0**0.25
EPSILON = 1e-05
NEGATIVE = -1e30
ALL = ("dp", "fsdp")


class Grid:
    def __init__(self, mesh):
        self.depth = mesh.shape["dp"] // 2
        self.count = mesh.size
        self.fast = mesh.shape["fsdp"] == 4 and mesh.shape["dp"] == 8
        self.axes = ("z", "core", "y", "x") if self.fast else ALL
        self.mesh = mesh
        if self.fast:
            self.mesh = jax.sharding.Mesh(mesh.devices.reshape(4, 2, 2, 2), self.axes)

    def place(self):
        return jnp.stack([lax.axis_index(axis) for axis in self.axes]).astype(jnp.int32)

    def index(self):
        return lax.axis_index(self.axes)

    def move(self, value, dz=0, dc=0, dy=0, dx=0):
        offset = ((dz * 2 + dc) * 2 + dy) * 2 + dx
        return lax.ppermute(value, self.axes, [(index ^ offset, index) for index in range(self.count)])

    def cores(self, twice):
        return lax.all_to_all(twice, "core", 0, 0, tiled=True)


def after(value, *others):
    return lax.optimization_barrier((value,) + others)[0]


def wide_dot(left, right):
    return jnp.dot(left, right, preferred_element_type=jnp.float32)


def dot_rows(left, right):
    return lax.dot_general(left, right, (((1,), (1,)), ((), ())), preferred_element_type=jnp.float32)


def dot_columns(left, right):
    return lax.dot_general(left, right, (((0,), (0,)), ((), ())), preferred_element_type=jnp.float32)


def whole_call(body, name, inputs, shapes, scratch=(), limit=56):
    arrays, specs = [], []
    for item in inputs:
        if not isinstance(item, tuple):
            item = (item, item.shape, (0,) * item.ndim)
        arrays.append(item[0])
        if len(item) == 2:
            specs.append(pl.BlockSpec(memory_space=item[1]))
        else:
            specs.append(pl.BlockSpec(item[1], lambda i, index=item[2]: index))
    outs, out_specs = [], []
    for item in shapes:
        outs.append(jax.ShapeDtypeStruct(item[0], item[1]))
        if len(item) == 3:
            out_specs.append(pl.BlockSpec(memory_space=item[2]))
        else:
            out_specs.append(pl.BlockSpec(item[0], lambda i, rank=len(item[0]): (0,) * rank))
    return pl.pallas_call(
        body,
        grid=(1,),
        out_shape=outs,
        in_specs=specs,
        out_specs=out_specs,
        scratch_shapes=list(scratch),
        compiler_params=pltpu.CompilerParams(vmem_limit_bytes=limit * 2**20),
        cost_estimate=pl.CostEstimate(flops=1, bytes_accessed=1, transcendentals=0),
        name=name,
    )(*arrays)


def in_two(depth, pieces, dc, side, k):
    return pieces[dc], side * depth + k


def in_rest(base):
    def locate(depth, pieces, dc, side, k):
        half = depth // 2
        own, over_x, over_y, low, high = pieces[5 * dc : 5 * dc + 5]
        if side == 0:
            return own, base + k
        if side < 3:
            return (over_x, over_y)[side - 1], half + k
        return (low, k) if k < half else (high, k - half)

    return locate


def in_last(depth, pieces, dc, side, k):
    own, over_x, over_y, corner = pieces[4 * dc : 4 * dc + 4]
    return (own, over_x, over_y, corner)[side], depth // 2 + k if side in (1, 2) else k


def in_second(depth, pieces, dc, side, k):
    half = depth // 2
    sides, low, high = pieces[3 * dc : 3 * dc + 3]
    if side < 3:
        return sides, side * depth + k
    return (low, k) if k < half else (high, k - half)


def arrivals_of(depth, rows, place, locate, pieces, held, sems, held_norms=None, these=range(8), blocks=0):
    z, c, y, x = place[0], place[1], place[2], place[3]
    width = held.shape[-1]
    arrivals = []
    for k in range(depth):
        column = []
        for n in these:
            dc, dy, dx = n // 4, n // 2 % 2, n % 2
            piece, spot = locate(depth, pieces, dc, n % 4, k)
            owner = (((z ^ k) * 2 + (c ^ dc)) * 2 + (y ^ dy)) * 2 + (x ^ dx)
            if blocks:
                target = held.at[pl.ds(owner * blocks, blocks)]
            else:
                target = held.at[..., pl.ds(pl.multiple_of(owner * rows, rows), rows), :]
            source = piece.at[spot]
            order = k * 8 + n
            if held_norms is None:
                column.append(pltpu.make_async_copy(source, target, sems.at[order]))
            else:
                column.append(pltpu.make_async_copy(source.at[..., :width], target, sems.at[order]))
                column.append(
                    pltpu.make_async_copy(
                        source.at[0:2, :, pl.ds(width, 128)],
                        held_norms.at[owner],
                        sems.at[8 * depth + order],
                    )
                )
        for copy in column:
            copy.start()
        arrivals.append(column)
    return arrivals


def pass_on(depth, rows, place, arrivals, held, whole, sems):
    leaving = []
    for k in range(depth):
        for copy in arrivals[k]:
            copy.wait()
        spot = pl.ds(pl.multiple_of((place[0] ^ k) * (8 * rows), 8 * rows), 8 * rows)
        leaving.append(pltpu.make_async_copy(held.at[..., spot, :], whole.at[..., spot, :], sems.at[k]))
        leaving[k].start()
    return leaving


def norm_rows_of(summed, gain, shift):
    center = jnp.mean(summed, axis=-1, keepdims=True)
    centred = summed - center
    inverse = lax.rsqrt(jnp.mean(centred * centred, axis=-1, keepdims=True) + EPSILON)
    scaled = centred * inverse
    return scaled * gain + shift, scaled, inverse


def norm_rows_back(incoming, scaled, inverse, gain):
    spread_out = incoming * gain
    d_summed = inverse * (
        spread_out
        - jnp.mean(spread_out, axis=-1, keepdims=True)
        - scaled * jnp.mean(spread_out * scaled, axis=-1, keepdims=True)
    )
    return d_summed, jnp.sum(incoming * scaled, axis=0, keepdims=True), jnp.sum(incoming, axis=0, keepdims=True)


def head_halves():
    lane = lax.broadcasted_iota(jnp.int32, (1, 2 * HEAD_DIM), 1)
    return [
        jnp.where(lane < HEAD_DIM, 1.0, 0.0).astype(jnp.bfloat16),
        jnp.where(lane < HEAD_DIM, 0.0, 1.0).astype(jnp.bfloat16),
    ]


def attend_heads(query, key, value, allowed, context, logsum):
    halves = head_halves()
    lane = lax.broadcasted_iota(jnp.int32, logsum.shape, 1)
    logsum[...] = jnp.zeros_like(logsum)

    def pair(p, carry):
        lanes = pl.ds(pl.multiple_of(p * 2 * HEAD_DIM, 2 * HEAD_DIM), 2 * HEAD_DIM)
        queries, keys, values = query[:, lanes], key[:, lanes], value[:, lanes]
        total = None
        for side, half in enumerate(halves):
            scores = dot_rows(queries * half, keys) * HEAD_DIM ** (-0.5)
            scores = jnp.where(allowed[...] > 0, scores, NEGATIVE)
            highest = jnp.max(scores, axis=-1, keepdims=True)
            weights = jnp.exp(scores - highest)
            totals = jnp.sum(weights, axis=-1, keepdims=True)
            chances = (weights * (1.0 / totals)).astype(jnp.bfloat16)
            part = wide_dot(chances, values * half)
            total = part if total is None else total + part
            logsum[...] = jnp.where(lane == 2 * p + side, highest + jnp.log(totals), logsum[...])
        context[:, lanes] = total.astype(jnp.bfloat16)
        return carry

    lax.fori_loop(0, HEADS // 2, pair, 0)


def attend_heads_back(query, key, value, allowed, logsum, d_context, d_query, d_key, d_value):
    halves = head_halves()
    lane = lax.broadcasted_iota(jnp.int32, logsum.shape, 1)
    scale = HEAD_DIM ** (-0.5)

    def pair(p, carry):
        lanes = pl.ds(pl.multiple_of(p * 2 * HEAD_DIM, 2 * HEAD_DIM), 2 * HEAD_DIM)
        queries, keys, values, d_outs = query[:, lanes], key[:, lanes], value[:, lanes], d_context[:, lanes]
        sums = [None, None, None]
        for side, half in enumerate(halves):
            own_sum = jnp.sum(jnp.where(lane == 2 * p + side, logsum[...], 0.0), axis=-1, keepdims=True)
            own_queries, own_outs = queries * half, d_outs * half
            scores = dot_rows(own_queries, keys) * scale
            scores = jnp.where(allowed[...] > 0, scores, NEGATIVE)
            chances = jnp.exp(scores - own_sum)
            d_chances = dot_rows(own_outs, values)
            centre = jnp.sum(d_chances * chances, axis=-1, keepdims=True)
            d_scores = (chances * (d_chances - centre)).astype(jnp.bfloat16)
            parts = (
                wide_dot(d_scores, keys * half),
                dot_columns(d_scores, own_queries),
                dot_columns(chances.astype(jnp.bfloat16), own_outs),
            )
            sums = [part if old is None else old + part for old, part in zip(sums, parts)]
        d_query[:, lanes] = (sums[0] * scale).astype(jnp.bfloat16)
        d_key[:, lanes] = (sums[1] * scale).astype(jnp.bfloat16)
        d_value[:, lanes] = sums[2].astype(jnp.bfloat16)
        return carry

    lax.fori_loop(0, HEADS // 2, pair, 0)


def self_allowed(ids_column, ids_row, allowed):
    rows, columns = allowed.shape
    later = lax.broadcasted_iota(jnp.int32, (rows, columns), 0) >= lax.broadcasted_iota(
        jnp.int32, (rows, columns), 1
    )
    same = ids_column[...] == ids_row[...]
    allowed[...] = jnp.where(later & same, 1.0, 0.0)


def cross_allowed(ids_column, ids_row, allowed):
    allowed[...] = jnp.where(ids_column[...] == ids_row[...], 1.0, 0.0)


def self_forward_kernel(depth, rows, place, tokens, ids_column, ids_row, *refs):
    pieces, refs = refs[:2], refs[2:]
    whole, gains, query, key, value, context, logsum, first, first_low, scaled, inverse = refs[:11]
    held, held_norms, allowed, in_sems, out_sems = refs[11:]
    arrivals = arrivals_of(depth, rows, place, in_two, pieces, held, in_sems, held_norms)
    self_allowed(ids_column, ids_row, allowed)
    leaving = pass_on(depth, rows, place, arrivals, held, whole, out_sems)
    packed = held_norms[0].astype(jnp.float32)
    for owner in range(1, 8 * depth):
        packed += held_norms[owner].astype(jnp.float32)
    gains[...] = jnp.zeros_like(gains)
    for n in range(6):
        for j in range(8):
            r = n * 8 + j
            gains[n : n + 1, j * 128 : (j + 1) * 128] = packed[r // rows, r % rows : r % rows + 1, :]
    for n, out in enumerate((query, key, value)):
        out[...] = wide_dot(tokens[...], held[n]).astype(jnp.bfloat16)
    attend_heads(query, key, value, allowed, context, logsum)
    branch = wide_dot(context[...], held[3])
    summed = RESIDUAL_SCALE * tokens[...].astype(jnp.float32) + branch
    first[...], scaled[...], inverse[...] = norm_rows_of(summed, gains[0:1, :], gains[1:2, :])
    first_low[...] = first[...].astype(jnp.bfloat16)
    for copy in leaving:
        copy.wait()


def self_forward(grid, place, tokens, ids_column, ids_row, pieces):
    count, width = tokens.shape
    rows = pieces[0].shape[2]
    low, full = jnp.bfloat16, jnp.float32
    shape = (count, width)
    return whole_call(
        functools.partial(self_forward_kernel, grid.depth, rows),
        "self_forward",
        [(place, pltpu.SMEM), tokens, ids_column, ids_row] + [(piece, pl.ANY) for piece in pieces],
        [((4, width, width), low, pl.ANY), ((8, width), full)]
        + [(shape, low)] * 4
        + [((count, 128), full), (shape, full), (shape, low), (shape, full), ((count, 1), full)],
        [
            pltpu.VMEM((4, width, width), low),
            pltpu.VMEM((grid.count, 2, rows, 128), low),
            pltpu.VMEM((count, count), full),
            pltpu.SemaphoreType.DMA((2 * grid.count,)),
            pltpu.SemaphoreType.DMA((grid.depth,)),
        ],
    )


def cross_forward_kernel(depth, rows, place, first, first_low, memory, gains, ids_column, ids_row, *refs):
    pieces, refs = refs[:6], refs[6:]
    whole, query, key, value, context, logsum, second, second_low, scaled, inverse = refs[:10]
    held, allowed, in_sems, out_sems = refs[10:]
    arrivals = arrivals_of(depth, rows, place, in_second, pieces, held, in_sems)
    cross_allowed(ids_column, ids_row, allowed)
    leaving = pass_on(depth, rows, place, arrivals, held, whole, out_sems)
    query[...] = wide_dot(first_low[...], held[0]).astype(jnp.bfloat16)
    key[...] = wide_dot(memory[...], held[1]).astype(jnp.bfloat16)
    value[...] = wide_dot(memory[...], held[2]).astype(jnp.bfloat16)
    attend_heads(query, key, value, allowed, context, logsum)
    summed = RESIDUAL_SCALE * first[...] + wide_dot(context[...], held[3])
    second[...], scaled[...], inverse[...] = norm_rows_of(summed, gains[2:3, :], gains[3:4, :])
    second_low[...] = second[...].astype(jnp.bfloat16)
    for copy in leaving:
        copy.wait()


def cross_forward(grid, place, first, first_low, memory, gains, ids_column, ids_row, pieces):
    count, width = first.shape
    others = memory.shape[0]
    rows = pieces[0].shape[2]
    low, full = jnp.bfloat16, jnp.float32
    shape, other_shape = (count, width), (others, width)
    return whole_call(
        functools.partial(cross_forward_kernel, grid.depth, rows),
        "cross_forward",
        [(place, pltpu.SMEM), first, first_low, memory, gains, ids_column, ids_row]
        + [(piece, pl.ANY) for piece in pieces],
        [((4, width, width), low, pl.ANY), (shape, low), (other_shape, low), (other_shape, low), (shape, low)]
        + [((count, 128), full), (shape, full), (shape, low), (shape, full), ((count, 1), full)],
        [
            pltpu.VMEM((4, width, width), low),
            pltpu.VMEM((count, others), full),
            pltpu.SemaphoreType.DMA((grid.count,)),
            pltpu.SemaphoreType.DMA((grid.depth,)),
        ],
    )


TANH_SCALE = 0.7978845608028654
TANH_CUBE = 0.044715


def expand_forward_kernel(depth, rows, place, second_low, *refs):
    pieces, refs = refs[:10], refs[10:]
    whole, active, slope, held, in_sems, out_sems = refs
    arrivals = arrivals_of(depth, rows, place, in_rest(3 * depth), pieces, held, in_sems)
    leaving = pass_on(depth, rows, place, arrivals, held, whole, out_sems)
    left = second_low[...]
    block = held.shape[2]

    def tile(j, carry):
        for part in range(block // 512):
            lanes = pl.ds(pl.multiple_of(j * block + part * 512, 512), 512)
            inner = wide_dot(left, held[j, :, part * 512 : (part + 1) * 512])
            square = inner * inner
            bend = jnp.tanh(TANH_SCALE * (inner * (1.0 + TANH_CUBE * square)))
            half = 0.5 + 0.5 * bend
            active[:, lanes] = (inner * half).astype(jnp.bfloat16)
            slope[:, lanes] = half + (0.5 * TANH_SCALE) * inner * (1.0 - bend * bend) * (
                1.0 + (3.0 * TANH_CUBE) * square
            )
        return carry

    lax.fori_loop(0, held.shape[0], tile, 0)
    for copy in leaving:
        copy.wait()


def expand_forward(grid, place, second_low, pieces):
    count, width = second_low.shape
    blocks, rows, block = pieces[0].shape[1:]
    hidden = blocks * block
    low = jnp.bfloat16
    return whole_call(
        functools.partial(expand_forward_kernel, grid.depth, rows),
        "expand_forward",
        [(place, pltpu.SMEM), second_low] + [(piece, pl.ANY) for piece in pieces],
        [((blocks, width, block), low, pl.ANY), ((count, hidden), low), ((count, hidden), jnp.float32)],
        [
            pltpu.VMEM((blocks, width, block), low),
            pltpu.SemaphoreType.DMA((grid.count,)),
            pltpu.SemaphoreType.DMA((grid.depth,)),
        ],
    )


def rows_of(held):
    return held.reshape(held.shape[0] * held.shape[1], held.shape[2])


def reduce_first_kernel(depth, place, active, *refs):
    pieces, (partial, held, sems) = refs[:6], refs[6:]
    z, c, y, x = place[0], place[1], place[2], place[3]
    blocks, rows, width = pieces[0].shape[1:]

    def locate(depth, pieces, dc, side, k):
        return (pieces[3 * dc], k) if side == 0 else (pieces[3 * dc + side], depth // 2 + k)

    arrivals = arrivals_of(
        depth, rows, place, locate, pieces, held, sems, these=(0, 1, 2, 4, 5, 6), blocks=blocks
    )
    for there in range(depth):
        for core in range(2):
            owner = ((there * 2 + core) * 2 + (1 - y)) * 2 + (1 - x)
            held[pl.ds(owner * blocks, blocks)] = jnp.zeros((blocks, rows, width), held.dtype)
    span = 8 * blocks
    for k, column in enumerate(arrivals):
        for copy in column:
            copy.wait()
        there = z ^ k
        lanes = pl.ds(pl.multiple_of(there * (span * rows), span * rows), span * rows)
        part = wide_dot(active[:, lanes], rows_of(held[pl.ds(there * span, span)]))
        partial[...] = part if k == 0 else partial[...] + part


def reduce_first(grid, place, active, pieces):
    count, hidden = active.shape
    blocks, rows, width = pieces[0].shape[1:]
    return whole_call(
        functools.partial(reduce_first_kernel, grid.depth),
        "reduce_first",
        [(place, pltpu.SMEM), active] + [(piece, pl.ANY) for piece in pieces],
        [((count, width), jnp.float32)],
        [
            pltpu.VMEM((grid.count * blocks, rows, width), jnp.bfloat16),
            pltpu.SemaphoreType.DMA((grid.count,)),
        ],
    )[0]


def reduce_finish_kernel(depth, place, active, partial, second, gains, output_grad, *refs):
    corners, (output, d_summed, d_branch, norm_terms) = refs[:2], refs[2:]
    z, c, y, x = place[0], place[1], place[2], place[3]
    summed = RESIDUAL_SCALE * second[...] + partial[...]
    for k in range(depth):
        for dc in range(2):
            piece = rows_of(corners[dc][k])
            rows = piece.shape[0]
            owner = (((z ^ k) * 2 + (c ^ dc)) * 2 + (1 - y)) * 2 + (1 - x)
            summed += wide_dot(active[:, pl.ds(pl.multiple_of(owner * rows, rows), rows)], piece)
    final, scaled, inverse = norm_rows_of(summed, gains[4:5, :], gains[5:6, :])
    output[...] = final.astype(jnp.bfloat16)
    d_sum, norm_terms[0:1, :], norm_terms[1:2, :] = norm_rows_back(
        output_grad[...].astype(jnp.float32), scaled, inverse, gains[4:5, :]
    )
    d_summed[...] = d_sum
    d_branch[...] = d_sum.astype(jnp.bfloat16)


def reduce_finish(grid, place, active, partial, second, gains, output_grad, corners):
    shape = second.shape
    low, full = jnp.bfloat16, jnp.float32
    return whole_call(
        functools.partial(reduce_finish_kernel, grid.depth),
        "reduce_finish",
        [(place, pltpu.SMEM), active, partial, second, gains, output_grad, *corners],
        [(shape, low), (shape, full), (shape, low), ((2, shape[1]), full)],
    )


def reduce_back_kernel(depth, place, d_branch, slope, *refs):
    pieces, (d_inner, held, sems) = refs[:8], refs[8:]
    blocks, rows, width = pieces[0].shape[1:]
    arrivals = arrivals_of(depth, rows, place, in_last, pieces, held, sems, blocks=blocks)
    left = d_branch[...]
    step = 512 // rows
    tiles = 8 * blocks // step
    for k, column in enumerate(arrivals):
        for copy in column:
            copy.wait()
        for n in range(tiles):
            j = (place[0] ^ k) * tiles + n
            lanes = pl.ds(pl.multiple_of(j * 512, 512), 512)
            d_active = dot_rows(left, rows_of(held[pl.ds(j * step, step)]))
            d_inner[:, lanes] = (d_active * slope[:, lanes]).astype(jnp.bfloat16)


def reduce_back(grid, place, d_branch, slope, pieces):
    count, hidden = slope.shape
    blocks, rows, width = pieces[0].shape[1:]
    return whole_call(
        functools.partial(reduce_back_kernel, grid.depth),
        "reduce_back",
        [(place, pltpu.SMEM), d_branch, slope] + [(piece, pl.ANY) for piece in pieces],
        [((count, hidden), jnp.bfloat16)],
        [
            pltpu.VMEM((grid.count * blocks, rows, width), jnp.bfloat16),
            pltpu.SemaphoreType.DMA((grid.count,)),
        ],
    )[0]


def expand_back_kernel(d_inner, expand, d_sum_three, scaled, inverse, gains, out_weight, d_summed, d_branch, d_context, norm_terms):
    d_second = RESIDUAL_SCALE * d_sum_three[...]
    block = expand.shape[2]
    for n in range(expand.shape[0]):
        d_second += dot_rows(d_inner[:, n * block : (n + 1) * block], expand[n])
    d_sum, norm_terms[0:1, :], norm_terms[1:2, :] = norm_rows_back(
        d_second, scaled[...], inverse[...], gains[2:3, :]
    )
    d_summed[...] = d_sum
    d_branch[...] = d_sum.astype(jnp.bfloat16)
    d_context[...] = dot_rows(d_branch[...], out_weight[0]).astype(jnp.bfloat16)


def expand_back(d_inner, expand, d_sum_three, scaled, inverse, gains, second_full):
    shape = d_sum_three.shape
    width = shape[1]
    low, full = jnp.bfloat16, jnp.float32
    return whole_call(
        expand_back_kernel,
        "expand_back",
        [d_inner, expand, d_sum_three, scaled, inverse, gains]
        + [(second_full, (1, width, width), (3, 0, 0))],
        [(shape, full), (shape, low), (shape, low), ((2, width), full)],
    )


def cross_back_kernel(
    query, key, value, logsum, d_context, ids_column, ids_row, d_branch_two, d_sum_two, scaled, inverse, gains,
    query_weight, out_weight, back, d_summed, d_context_one, norm_terms, allowed,
):
    count, others = query.shape[0], key.shape[0]
    cross_allowed(ids_column, ids_row, allowed)
    rows = back.at[0]
    d_query = rows.at[count : 2 * count]
    d_key = rows.at[3 * count : 3 * count + others]
    d_value = rows.at[3 * count + others : 3 * count + 2 * others]
    attend_heads_back(query, key, value, allowed, logsum, d_context, d_query, d_key, d_value)
    d_first = RESIDUAL_SCALE * d_sum_two[...] + dot_rows(d_query[...], query_weight[0])
    d_sum, norm_terms[0:1, :], norm_terms[1:2, :] = norm_rows_back(
        d_first, scaled[...], inverse[...], gains[0:1, :]
    )
    d_summed[...] = d_sum
    d_branch = d_sum.astype(jnp.bfloat16)
    rows[0:count, :] = d_branch_two[...]
    rows[2 * count : 3 * count, :] = d_branch
    back[1] = rows[...]
    d_context_one[...] = dot_rows(d_branch, out_weight[0]).astype(jnp.bfloat16)


def cross_back(query, key, value, logsum, d_context, ids_column, ids_row, d_branch_two, d_sum_two, scaled, inverse, gains, second_full, first_full):
    shape, other_shape = query.shape, key.shape
    width = shape[1]
    low, full = jnp.bfloat16, jnp.float32
    block = (1, width, width)
    return whole_call(
        cross_back_kernel,
        "cross_back",
        [query, key, value, logsum, d_context, ids_column, ids_row, d_branch_two, d_sum_two, scaled, inverse, gains]
        + [(second_full, block, (0, 0, 0)), (first_full, block, (3, 0, 0))],
        [((2, 3 * shape[0] + 2 * other_shape[0], width), low), (shape, full), (shape, low), ((2, width), full)],
        [pltpu.VMEM((shape[0], other_shape[0]), full)],
    )


def self_back_kernel(query, key, value, logsum, d_context, ids_column, ids_row, d_rows, allowed):
    self_allowed(ids_column, ids_row, allowed)
    count = query.shape[0]
    outs = [d_rows.at[n * count : (n + 1) * count] for n in range(3)]
    attend_heads_back(query, key, value, allowed, logsum, d_context, *outs)


def self_back(query, key, value, logsum, d_context, ids_column, ids_row):
    count, width = query.shape
    return whole_call(
        self_back_kernel,
        "self_back",
        [query, key, value, logsum, d_context, ids_column, ids_row],
        [((3 * count, width), jnp.bfloat16)],
        [pltpu.VMEM((count, count), jnp.float32)],
    )[0]


def inputs_back_kernel(d_rows, d_key, d_value, d_sum_one, w_query, w_key, w_value, w_key_two, w_value_two, tokens_grad, memory_grad):
    count = d_sum_one.shape[0]
    total = RESIDUAL_SCALE * d_sum_one[...]
    for n, weight in enumerate((w_query, w_key, w_value)):
        total += dot_rows(d_rows[n * count : (n + 1) * count, :], weight[0])
    tokens_grad[...] = total
    memory_grad[...] = dot_rows(d_key[0], w_key_two[0]) + dot_rows(d_value[0], w_value_two[0])


def inputs_back(d_rows, back, d_sum_one, first_full, second_full):
    count, width = d_sum_one.shape
    others = (back.shape[1] - 3 * count) // 2
    first_row = 3 * count // others
    block = (1, width, width)
    return whole_call(
        inputs_back_kernel,
        "inputs_back",
        [d_rows]
        + [(back, (1, others, width), (0, first_row + n, 0)) for n in (0, 1)]
        + [d_sum_one]
        + [(first_full, block, (n, 0, 0)) for n in range(3)]
        + [(second_full, block, (n, 0, 0)) for n in (1, 2)],
        [((count, width), jnp.float32), ((others, width), jnp.float32)],
    )


def turn(depth, rows, place, sources, turned, spots=range(4)):
    z, c, y, x = place[0], place[1], place[2], place[3]
    tokens = sources[0].shape[0]
    for k in range(depth):
        there = z ^ k
        columns = pl.ds(pl.multiple_of((there * 2 + c) * (4 * rows), 4 * rows), 4 * rows)
        for side, source in enumerate(sources):
            block = source[:, columns].T
            named = [block[n * rows : (n + 1) * rows] for n in range(4)]
            named = [jnp.where(x == 0, named[n], named[n ^ 1]) for n in range(4)]
            named = [jnp.where(y == 0, named[n], named[n ^ 2]) for n in range(4)]
            for at, spot in enumerate(spots):
                turned[at, k * rows : (k + 1) * rows, side * tokens : (side + 1) * tokens] = named[spot]


def spread(depth, rows, turned, rights, outs, spots=range(4)):
    tokens = rights[0].shape[0]
    half = depth // 2
    for at, spot in enumerate(spots):
        part = turned[at]
        total = jnp.dot(part[:, :tokens], rights[0][...], preferred_element_type=jnp.float32)
        total += jnp.dot(
            part[:, tokens : 2 * tokens], rights[1][...], preferred_element_type=jnp.float32
        )
        total = total.astype(jnp.bfloat16).reshape(depth, rows, -1)
        if spot < 3:
            outs[at][...] = total
        else:
            outs[at][...] = total[:half]
            outs[at + 1][...] = total[half:]


def tiled_kernel(depth, rows, spots, place, left, left_far, right, right_far, *refs):
    outs, turned = refs[:-1], refs[-1]

    @pl.when(pl.program_id(0) == 0)
    def _():
        turn(depth, rows, place, (left, left_far), turned, spots)

    spread(depth, rows, turned, (right, right_far), outs, spots)


def group_kernel(depth, rows, count, by_core, place, *refs):
    each = 3 if by_core else 4
    core = place[1]
    inputs, outs, turned = refs[: each * count], refs[each * count : each * count + 5], refs[-1]
    for m in range(count):
        left, left_far, *rights = inputs[each * m : each * m + each]
        if by_core:
            rights = (rights[0].at[core], rights[0].at[1 - core])
        turn(depth, rows, place, (left, left_far), turned)
        spread(depth, rows, turned, rights, [out.at[:, m] for out in outs])


def piece_counts(depth, spots=range(4)):
    counts = []
    for spot in spots:
        counts += [depth] if spot < 3 else [depth // 2, depth // 2]
    return counts


def tiled_terms(grid, place, left, left_far, right, right_far, tile, spots=range(4)):
    tokens, features = left.shape
    width = right.shape[1]
    rows = features // grid.count
    left_row = 4 if left_far.shape[0] != tokens else 0
    counts = piece_counts(grid.depth, spots)
    return pl.pallas_call(
        functools.partial(tiled_kernel, grid.depth, rows, spots),
        grid=(width // tile,),
        out_shape=[jax.ShapeDtypeStruct((n, rows, width), jnp.bfloat16) for n in counts],
        in_specs=[
            pl.BlockSpec(memory_space=pltpu.SMEM),
            pl.BlockSpec((tokens, features), lambda j: (0, 0)),
            pl.BlockSpec((tokens, features), lambda j: (left_row, 0)),
        ]
        + [pl.BlockSpec((tokens, tile), lambda j: (0, j))] * 2,
        out_specs=[pl.BlockSpec((n, rows, tile), lambda j: (0, 0, j)) for n in counts],
        scratch_shapes=[pltpu.VMEM((len(spots), grid.depth * rows, 2 * tokens), jnp.bfloat16)],
        compiler_params=pltpu.CompilerParams(vmem_limit_bytes=40 * 2**20),
        cost_estimate=pl.CostEstimate(flops=1, bytes_accessed=1, transcendentals=0),
        name="terms",
    )(place, left, left_far, right, right_far)


def group_terms(grid, place, held, held_far, right, right_far, pairs):
    by_core = right_far is None
    width = held.shape[1]
    rows = width // grid.count
    arrays, specs = [], []
    for tokens, left_row, right_row in pairs:
        arrays += [held, held_far, right]
        specs += [pl.BlockSpec((tokens, width), lambda i, row=left_row: (row, 0))] * 2
        if by_core:
            specs += [pl.BlockSpec((2, tokens, width), lambda i, row=right_row: (0, row, 0))]
        else:
            arrays += [right_far]
            specs += [pl.BlockSpec((tokens, width), lambda i, row=right_row: (row, 0))] * 2
    most = max(tokens for tokens, _, _ in pairs)
    shapes = [(n, len(pairs), rows, width) for n in piece_counts(grid.depth)]
    return pl.pallas_call(
        functools.partial(group_kernel, grid.depth, rows, len(pairs), by_core),
        grid=(1,),
        out_shape=[jax.ShapeDtypeStruct(shape, jnp.bfloat16) for shape in shapes],
        in_specs=[pl.BlockSpec(memory_space=pltpu.SMEM)] + specs,
        out_specs=[pl.BlockSpec(shape, lambda i: (0, 0, 0, 0)) for shape in shapes],
        scratch_shapes=[pltpu.VMEM((4, grid.depth * rows, 2 * most), jnp.bfloat16)],
        compiler_params=pltpu.CompilerParams(vmem_limit_bytes=48 * 2**20),
        cost_estimate=pl.CostEstimate(flops=1, bytes_accessed=1, transcendentals=0),
        name="terms",
    )(place, *arrays)


def corner_kernel(over_x, low, over_y, high, sent_x, sent_y):
    wide = jnp.float32
    sent_x[...] = (over_x[...].astype(wide) + low[...].astype(wide)).astype(jnp.bfloat16)
    sent_y[...] = (over_y[...].astype(wide) + high[...].astype(wide)).astype(jnp.bfloat16)


def corner_added(grid, pieces, low, high):
    zeros = (0,) * (low.ndim - 1)
    first = pl.BlockSpec(low.shape, lambda i: (0,) + zeros)
    second = pl.BlockSpec(low.shape, lambda i: (1,) + zeros)
    return pl.pallas_call(
        corner_kernel,
        grid=(1,),
        out_shape=[jax.ShapeDtypeStruct(pieces[n].shape, jnp.bfloat16) for n in (1, 2)],
        in_specs=[first, first, second, first],
        out_specs=[first, second],
        input_output_aliases={0: 0, 2: 1},
        compiler_params=pltpu.CompilerParams(vmem_limit_bytes=32 * 2**20),
        cost_estimate=pl.CostEstimate(flops=1, bytes_accessed=1, transcendentals=0),
        name="corner_added",
    )(pieces[1], low, pieces[2], high)


def plane_sum(own, over_x, over_y):
    wide = jnp.float32
    return (own.astype(wide) + over_x.astype(wide) + over_y.astype(wide)).astype(jnp.bfloat16)


def plane_sums(grid, pieces, over_x, over_y):
    half = grid.depth // 2
    return [
        plane_sum(pieces[0][part], over_x[part], over_y[part]) for part in (slice(0, half), slice(half, None))
    ]


def pair_sum(near, got):
    return (near[1].astype(jnp.float32) + got[1].astype(jnp.float32)).astype(jnp.bfloat16)


def total_of(*terms_of):
    return sum([term.astype(jnp.float32) for term in terms_of[1:]], terms_of[0].astype(jnp.float32))


def fetch(attention_rows, expand_rows, reduce_rows, norm_rows):
    gathered = (
        lax.all_gather(attention_rows, ("dp", "fsdp"), axis=1, tiled=True),
        lax.all_gather(expand_rows, ("dp", "fsdp"), axis=0, tiled=True),
        lax.all_gather(reduce_rows, ("dp", "fsdp"), axis=0, tiled=True),
        lax.all_gather(norm_rows, ("dp", "fsdp"), axis=1, tiled=True),
    )
    return gathered


def settle(attention_terms, expand_terms, reduce_terms, norm_terms):
    owned = (
        lax.psum_scatter(attention_terms, ("dp", "fsdp"), scatter_dimension=1, tiled=True),
        lax.psum_scatter(expand_terms, ("dp", "fsdp"), scatter_dimension=0, tiled=True),
        lax.psum_scatter(reduce_terms, ("dp", "fsdp"), scatter_dimension=0, tiled=True),
        lax.psum_scatter(norm_terms, ("dp", "fsdp"), scatter_dimension=1, tiled=True),
    )
    return owned


def matmul(left, right):
    return jnp.dot(left, right, preferred_element_type=jnp.float32)


def across(left, right):
    return jnp.einsum("ti,tj->ij", left, right, preferred_element_type=jnp.float32)


def against(left, right):
    return jnp.einsum("ti,ji->tj", left, right, preferred_element_type=jnp.float32)


def gelu_tanh(values):
    return jax.nn.gelu(values, approximate=True)


def normalize(summed, gain, shift):
    center = jnp.mean(summed, axis=-1, keepdims=True)
    centred = summed - center
    inverse = lax.rsqrt(jnp.mean(centred * centred, axis=-1, keepdims=True) + EPSILON)
    scaled = centred * inverse
    return (scaled * gain + shift, scaled, inverse)


def normalize_back(incoming, scaled, inverse, gain):
    spread = incoming * gain
    d_summed = inverse * (
        spread
        - jnp.mean(spread, axis=-1, keepdims=True)
        - scaled * jnp.mean(spread * scaled, axis=-1, keepdims=True)
    )
    return (d_summed, jnp.sum(incoming * scaled, axis=0), jnp.sum(incoming, axis=0))


def split_heads(matrix):
    return matrix.reshape(matrix.shape[0], HEADS, HEAD_DIM)


def scores_of(query_rows, key_rows, allowed):
    raw = jnp.einsum(
        "qhd,khd->hqk",
        split_heads(query_rows),
        split_heads(key_rows),
        preferred_element_type=jnp.float32,
    ) * HEAD_DIM ** (-0.5)
    return jnp.where(allowed[None], raw, NEGATIVE)


def attend_forward(query_rows, key_rows, value_rows, allowed):
    scores = scores_of(query_rows, key_rows, allowed)
    highest = jnp.max(scores, axis=-1, keepdims=True)
    weights = jnp.exp(scores - highest)
    totals = jnp.sum(weights, axis=-1, keepdims=True)
    chances = (weights / totals).astype(jnp.bfloat16)
    context = jnp.einsum(
        "hqk,khd->qhd", chances, split_heads(value_rows), preferred_element_type=jnp.float32
    )
    return (
        context.reshape(query_rows.shape[0], HEADS * HEAD_DIM).astype(jnp.bfloat16),
        highest + jnp.log(totals),
    )


def attend_back(query_rows, key_rows, value_rows, allowed, logsum, d_context):
    query_heads = split_heads(query_rows)
    key_heads = split_heads(key_rows)
    d_heads = split_heads(d_context)
    chances = jnp.exp(scores_of(query_rows, key_rows, allowed) - logsum)
    d_chances = jnp.einsum(
        "qhd,khd->hqk", d_heads, split_heads(value_rows), preferred_element_type=jnp.float32
    )
    d_value = jnp.einsum(
        "hqk,qhd->khd", chances.astype(jnp.bfloat16), d_heads, preferred_element_type=jnp.float32
    )
    centre = jnp.sum(d_chances * chances, axis=-1, keepdims=True)
    d_scores = (chances * (d_chances - centre)).astype(jnp.bfloat16)
    d_query = jnp.einsum(
        "hqk,khd->qhd", d_scores, key_heads, preferred_element_type=jnp.float32
    ) * HEAD_DIM ** (-0.5)
    d_key = jnp.einsum(
        "hqk,qhd->khd", d_scores, query_heads, preferred_element_type=jnp.float32
    ) * HEAD_DIM ** (-0.5)
    query_count = query_rows.shape[0]
    key_count = key_rows.shape[0]
    return (
        d_query.reshape(query_count, HEADS * HEAD_DIM).astype(jnp.bfloat16),
        d_key.reshape(key_count, HEADS * HEAD_DIM).astype(jnp.bfloat16),
        d_value.reshape(key_count, HEADS * HEAD_DIM).astype(jnp.bfloat16),
    )


def plain_device(
    tokens,
    memory,
    target_segments,
    source_segments,
    self_query,
    self_key,
    self_value,
    self_output,
    cross_query,
    cross_key,
    cross_value,
    cross_output,
    expand_weight,
    reduce_weight,
    self_gain,
    self_shift,
    cross_gain,
    cross_shift,
    final_gain,
    final_shift,
    output_grad,
):
    attention_rows = jnp.stack(
        [
            self_query,
            self_key,
            self_value,
            self_output,
            cross_query,
            cross_key,
            cross_value,
            cross_output,
        ]
    )
    norm_rows = jnp.stack([self_gain, self_shift, cross_gain, cross_shift, final_gain, final_shift])
    matrices, expand_full, reduce_full, norm_full = fetch(
        attention_rows, expand_weight, reduce_weight, norm_rows
    )
    gains = norm_full.astype(jnp.float32)
    target_ids = target_segments[0]
    source_ids = source_segments[0]
    positions = lax.iota(jnp.int32, tokens.shape[0])
    causal = (target_ids[:, None] == target_ids[None, :]) & (
        positions[None, :] <= positions[:, None]
    )
    crossing = target_ids[:, None] == source_ids[None, :]
    query_one = matmul(tokens, matrices[0]).astype(jnp.bfloat16)
    key_one = matmul(tokens, matrices[1]).astype(jnp.bfloat16)
    value_one = matmul(tokens, matrices[2]).astype(jnp.bfloat16)
    context_one, logsum_one = attend_forward(query_one, key_one, value_one, causal)
    branch_one = matmul(context_one, matrices[3])
    first, first_scaled, first_inverse = normalize(
        RESIDUAL_SCALE * tokens.astype(jnp.float32) + branch_one, gains[0], gains[1]
    )
    first_low = first.astype(jnp.bfloat16)
    query_two = matmul(first_low, matrices[4]).astype(jnp.bfloat16)
    key_two = matmul(memory, matrices[5]).astype(jnp.bfloat16)
    value_two = matmul(memory, matrices[6]).astype(jnp.bfloat16)
    context_two, logsum_two = attend_forward(query_two, key_two, value_two, crossing)
    branch_two = matmul(context_two, matrices[7])
    second, second_scaled, second_inverse = normalize(
        RESIDUAL_SCALE * first + branch_two, gains[2], gains[3]
    )
    second_low = second.astype(jnp.bfloat16)
    inner = matmul(second_low, expand_full)
    active = gelu_tanh(inner).astype(jnp.bfloat16)
    branch_three = matmul(active, reduce_full)
    final, final_scaled, final_inverse = normalize(
        RESIDUAL_SCALE * second + branch_three, gains[4], gains[5]
    )
    output = final.astype(jnp.bfloat16)
    matrices, expand_full, reduce_full, norm_full = fetch(
        attention_rows, expand_weight, reduce_weight, norm_rows
    )
    gains = norm_full.astype(jnp.float32)
    d_sum_three, final_gain_term, final_shift_term = normalize_back(
        output_grad.astype(jnp.float32), final_scaled, final_inverse, gains[4]
    )
    d_branch_three = d_sum_three.astype(jnp.bfloat16)
    reduce_term = across(active, d_branch_three)
    d_active = against(d_branch_three, reduce_full)
    d_inner = jax.vjp(gelu_tanh, inner)[1](d_active)[0].astype(jnp.bfloat16)
    expand_term = across(second_low, d_inner)
    d_second = RESIDUAL_SCALE * d_sum_three + against(d_inner, expand_full)
    d_sum_two, cross_gain_term, cross_shift_term = normalize_back(
        d_second, second_scaled, second_inverse, gains[2]
    )
    d_branch_two = d_sum_two.astype(jnp.bfloat16)
    cross_output_term = across(context_two, d_branch_two)
    d_context_two = against(d_branch_two, matrices[7]).astype(jnp.bfloat16)
    d_query_two, d_key_two, d_value_two = attend_back(
        query_two, key_two, value_two, crossing, logsum_two, d_context_two
    )
    cross_query_term = across(first_low, d_query_two)
    cross_key_term = across(memory, d_key_two)
    cross_value_term = across(memory, d_value_two)
    memory_grad = against(d_key_two, matrices[5]) + against(d_value_two, matrices[6])
    d_first = RESIDUAL_SCALE * d_sum_two + against(d_query_two, matrices[4])
    d_sum_one, self_gain_term, self_shift_term = normalize_back(
        d_first, first_scaled, first_inverse, gains[0]
    )
    d_branch_one = d_sum_one.astype(jnp.bfloat16)
    self_output_term = across(context_one, d_branch_one)
    d_context_one = against(d_branch_one, matrices[3]).astype(jnp.bfloat16)
    d_query_one, d_key_one, d_value_one = attend_back(
        query_one, key_one, value_one, causal, logsum_one, d_context_one
    )
    self_query_term = across(tokens, d_query_one)
    self_key_term = across(tokens, d_key_one)
    self_value_term = across(tokens, d_value_one)
    tokens_grad = (
        RESIDUAL_SCALE * d_sum_one
        + against(d_query_one, matrices[0])
        + against(d_key_one, matrices[1])
        + against(d_value_one, matrices[2])
    )
    attention_terms = jnp.stack(
        [
            self_query_term,
            self_key_term,
            self_value_term,
            self_output_term,
            cross_query_term,
            cross_key_term,
            cross_value_term,
            cross_output_term,
        ]
    )
    norm_terms = jnp.stack(
        [
            self_gain_term,
            self_shift_term,
            cross_gain_term,
            cross_shift_term,
            final_gain_term,
            final_shift_term,
        ]
    )
    attention_owned, expand_owned, reduce_owned, norm_owned = settle(
        attention_terms, expand_term, reduce_term, norm_terms
    )
    return (
        output,
        tokens_grad,
        memory_grad,
        attention_owned[0],
        attention_owned[1],
        attention_owned[2],
        attention_owned[3],
        attention_owned[4],
        attention_owned[5],
        attention_owned[6],
        attention_owned[7],
        expand_owned,
        reduce_owned,
        norm_owned[0],
        norm_owned[1],
        norm_owned[2],
        norm_owned[3],
        norm_owned[4],
        norm_owned[5],
    )


def per_device(
    grid,
    tokens,
    memory,
    target_segments,
    source_segments,
    self_query,
    self_key,
    self_value,
    self_output,
    cross_query,
    cross_key,
    cross_value,
    cross_output,
    expand_weight,
    reduce_weight,
    self_gain,
    self_shift,
    cross_gain,
    cross_shift,
    final_gain,
    final_shift,
    output_grad,
):
    if not grid.fast:
        return plain_device(
            tokens,
            memory,
            target_segments,
            source_segments,
            self_query,
            self_key,
            self_value,
            self_output,
            cross_query,
            cross_key,
            cross_value,
            cross_output,
            expand_weight,
            reduce_weight,
            self_gain,
            self_shift,
            cross_gain,
            cross_shift,
            final_gain,
            final_shift,
            output_grad,
        )
    place = grid.place()
    held_rows = self_gain.shape[0]
    norm_rows = jnp.stack([self_gain, self_shift, cross_gain, cross_shift, final_gain, final_shift])
    extra = jnp.zeros((16, held_rows * grid.count), jnp.bfloat16)
    extra = lax.dynamic_update_slice(extra, norm_rows, (0, grid.index() * held_rows))
    extra = extra.reshape(4, 32, 128)
    first_rows = jnp.concatenate([jnp.stack([self_query, self_key, self_value, self_output]), extra], axis=-1)
    second_rows = jnp.stack([cross_query, cross_key, cross_value, cross_output])
    target_column, target_row = target_segments.reshape(-1, 1), target_segments
    source_row = source_segments

    half = grid.depth // 2
    width = expand_weight.shape[1] // 4
    expand_rows = jnp.stack([expand_weight[:, n * width : (n + 1) * width] for n in range(4)])
    reduce_rows = reduce_weight.reshape(expand_rows.shape)

    first_z = [grid.move(first_rows, dz=k) for k in (2, 3, 1)]
    second_z = grid.move(second_rows, dz=1)
    first_own = jnp.stack([first_rows, first_z[2], first_z[0], first_z[1]])
    second_pair = jnp.stack([second_rows, second_z])
    first_own, second_pair, expand_rows, reduce_rows = after(
        (first_own, second_pair, expand_rows, reduce_rows)
    )
    first_x, first_y = grid.move(first_own, dx=1), grid.move(first_own, dy=1)
    second_z = grid.move(second_pair, dz=2)
    expand_z = grid.move(expand_rows, dz=1)
    reduce_z = grid.move(reduce_rows, dz=1)
    first_x, first_y, second_z, expand_z, reduce_z = after((first_x, first_y, second_z, expand_z, reduce_z))
    second_own = jnp.concatenate([second_pair, second_z])
    expand_pair = jnp.stack([expand_rows, expand_z])
    first_low, first_high, second_own, expand_pair = after(
        (first_x[:half], first_y[half:], second_own, expand_pair)
    )
    first_low, first_high = grid.move(first_low, dy=1), grid.move(first_high, dx=1)
    second_x, second_y = grid.move(second_own, dx=1), grid.move(second_own, dy=1)
    expand_z = grid.move(expand_pair, dz=2)
    first_low, first_high, second_x, second_y, expand_z = after(
        (first_low, first_high, second_x, second_y, expand_z)
    )
    reduce_pair = jnp.stack([reduce_rows, reduce_z])
    first_near = jnp.concatenate([first_own, first_x, first_y, first_low, first_high])
    sides = jnp.concatenate([second_own, second_x, second_y, expand_pair, expand_z])
    sent_y = jnp.concatenate([second_x[:half], expand_pair, expand_z])
    sent_x = jnp.concatenate([second_y[half:], expand_pair, expand_z])
    sent_x, sent_y, reduce_pair, first_near, sides = after((sent_x, sent_y, reduce_pair, first_near, sides))
    got_x, got_y = grid.move(sent_x, dx=1), grid.move(sent_y, dy=1)
    reduce_z = grid.move(reduce_pair, dz=2)
    first_far = grid.move(first_near, dc=1)
    sides_far = grid.move(sides, dc=1)
    first_out = self_forward(grid, place, tokens, target_column, target_row, (first_near, first_far))
    first_out, got_x, got_y, reduce_z, sides_far = after((first_out, got_x, got_y, reduce_z, sides_far))
    first_full, gains, query_one, key_one, value_one, context_one, logsum_one = first_out[:7]
    first, first_low, first_scaled, first_inverse = first_out[7:]
    reduce_own = jnp.concatenate([reduce_pair, reduce_z])
    sent_y = jnp.concatenate([got_x[half : 2 * half], reduce_pair, reduce_z])
    sent_x = jnp.concatenate([got_y[2 * half :], reduce_pair, reduce_z])
    sent_x, sent_y, got_x, got_y, reduce_own = after((sent_x, sent_y, got_x, got_y, reduce_own))
    last_x, last_y = grid.move(sent_x, dx=1), grid.move(sent_y, dy=1)
    got_x_far, got_y_far = grid.move(got_x, dc=1), grid.move(got_y, dc=1)
    reduce_own_far = grid.move(reduce_own, dc=1)
    second_out = cross_forward(
        grid, place, first, first_low, memory, gains, target_column, source_row,
        (sides, got_y, got_x, sides_far, got_y_far, got_x_far),
    )
    second_out, last_x, last_y, reduce_own_far = after((second_out, last_x, last_y, reduce_own_far))
    second_full, query_two, key_two, value_two, context_two, logsum_two = second_out[:6]
    second, second_low, second_scaled, second_inverse = second_out[6:]
    reduce_low, reduce_high, last_x, last_y = after(
        (last_x[half : 2 * half], last_y[2 * half :], last_x, last_y)
    )
    reduce_low, reduce_high = grid.move(reduce_low, dy=1), grid.move(reduce_high, dx=1)
    last_x_far, last_y_far = grid.move(last_x, dc=1), grid.move(last_y, dc=1)
    expand_full, active, slope = expand_forward(
        grid, place, second_low,
        (sides, got_x, got_y, last_y, last_x, sides_far, got_x_far, got_y_far, last_y_far, last_x_far),
    )
    held = jnp.concatenate([tokens, context_one, first_low, context_two, second_low, memory])
    held, active = after((held, active))
    held_far = grid.move(held, dc=1)
    active_far = grid.move(active, dc=1)
    reduce_low, reduce_high, active = after((reduce_low, reduce_high, active))
    reduce_corner, active = after((jnp.concatenate([reduce_low, reduce_high]), active))
    reduce_corner_far = grid.move(reduce_corner, dc=1)
    partial = reduce_first(
        grid, place, active, (reduce_own, last_x, last_y, reduce_own_far, last_x_far, last_y_far)
    )
    reduce_pieces = (
        reduce_own, last_x, last_y, reduce_corner, reduce_own_far, last_x_far, last_y_far, reduce_corner_far
    )
    reduce_corner = (reduce_corner, reduce_corner_far)
    output, d_sum_three, d_branch_three, final_norm_terms = reduce_finish(
        grid, place, active, partial, second, gains, output_grad, reduce_corner
    )
    d_branches = (d_branch_three, grid.move(d_branch_three, dc=1))
    reduce_low, reduce_high = after(
        tuple(tiled_terms(grid, place, active, active_far, *d_branches, 1024, (3,)))
    )
    reduce_terms = tiled_terms(
        grid, place, after(active, reduce_low), active_far, *d_branches, 512, (0, 1, 2)
    )
    d_inner = reduce_back(grid, place, after(d_branch_three, *reduce_terms), slope, reduce_pieces)
    reduce_low, reduce_high = grid.move(reduce_low, dy=1), grid.move(reduce_high, dx=1)
    reduce_low, reduce_high, d_inner = after((reduce_low, reduce_high, d_inner))
    reduce_sends = corner_added(grid, reduce_terms, reduce_low, reduce_high)
    reduce_sends, d_inner = after((reduce_sends, d_inner))
    reduce_x, reduce_y = grid.move(reduce_sends[0], dx=1), grid.move(reduce_sends[1], dy=1)
    d_inner_far = grid.move(d_inner, dc=1)
    d_sum_two, d_branch_two, d_context_two, cross_norm_terms = expand_back(
        d_inner, expand_full, d_sum_three, second_scaled, second_inverse, gains, second_full
    )
    expand_terms = tiled_terms(grid, place, second_low, held_far, after(d_inner, d_context_two), d_inner_far, 1024)
    expand_terms, d_context_two = after((expand_terms, d_context_two))
    expand_low, expand_high = grid.move(expand_terms[3], dy=1), grid.move(expand_terms[4], dx=1)
    back, d_sum_one, d_context_one, self_norm_terms = cross_back(
        query_two, key_two, value_two, logsum_two, d_context_two, target_column,
        source_row, d_branch_two, d_sum_two, first_scaled, first_inverse, gains, second_full, first_full,
    )
    norm_terms = jnp.concatenate([self_norm_terms, cross_norm_terms, final_norm_terms])
    expand_low, expand_high, reduce_x, reduce_y, back, norm_terms = after(
        (expand_low, expand_high, reduce_x, reduce_y, back, norm_terms)
    )
    expand_sends = corner_added(grid, expand_terms, expand_low, expand_high)
    expand_sends, back = after((expand_sends, back))
    expand_x, expand_y = grid.move(expand_sends[0], dx=1), grid.move(expand_sends[1], dy=1)
    reduce_near, reduce_pass = plane_sums(grid, reduce_terms, *after((reduce_x, reduce_y), expand_sends))
    reduce_near, reduce_pass, back = after((reduce_near, reduce_pass, back))
    reduce_got = grid.move(reduce_pass, dz=2)
    backs = grid.cores(back)
    pairs = [(256, 1, 2), (256, 2, 1), (128, 10, 6), (128, 10, 7), (256, 3, 0)]
    cross_terms = group_terms(grid, place, held, held_far, backs, None, pairs)
    cross_terms, d_context_one = after((cross_terms, d_context_one))
    cross_low, cross_high = grid.move(cross_terms[3], dy=1), grid.move(cross_terms[4], dx=1)
    back_one = self_back(
        query_one, key_one, value_one, logsum_one, d_context_one, target_column, target_row
    )
    cross_low, cross_high, back_one, reduce_got, expand_x, expand_y = after(
        (cross_low, cross_high, back_one, reduce_got, expand_x, expand_y)
    )
    cross_sends = corner_added(grid, cross_terms, cross_low, cross_high)
    reduce_leaving = pair_sum(reduce_near, reduce_got)
    cross_sends, back_one, reduce_leaving = after((cross_sends, back_one, reduce_leaving))
    cross_x, cross_y = grid.move(cross_sends[0], dx=1), grid.move(cross_sends[1], dy=1)
    back_one_far = grid.move(back_one, dc=1)
    reduce_last = grid.move(reduce_leaving, dz=1)
    expand_x, expand_y = after((expand_x, expand_y), cross_sends)
    expand_pass = after(plane_sum(expand_terms[0][half:], expand_x[half:], expand_y[half:]))
    expand_got = grid.move(expand_pass, dz=2)
    expand_x, expand_y = after((expand_x, expand_y), expand_pass, back_one_far)
    expand_near = after(plane_sum(expand_terms[0][:half], expand_x[:half], expand_y[:half]))
    back_one = after(back_one, expand_pass)
    self_terms = group_terms(
        grid, place, held, held_far, back_one, back_one_far, [(256, 0, n) for n in range(3)]
    )
    tokens_grad, memory_grad = inputs_back(
        after(back_one, *self_terms), back, d_sum_one, first_full, second_full
    )
    expand_got, reduce_last, self_low, self_high = after(
        (expand_got, reduce_last, self_terms[3], self_terms[4]), tokens_grad
    )
    expand_leaving = pair_sum(expand_near, expand_got)
    self_low, self_high, expand_leaving = after((self_low, self_high, expand_leaving))
    self_low, self_high = grid.move(self_low, dy=1), grid.move(self_high, dx=1)
    expand_last = grid.move(expand_leaving, dz=1)
    cross_x, cross_y = after((cross_x, cross_y), expand_leaving)
    cross_pass = after(plane_sum(cross_terms[0][half:], cross_x[half:], cross_y[half:]))
    cross_got = grid.move(cross_pass, dz=2)
    cross_x, cross_y = after((cross_x, cross_y), cross_pass)
    cross_near = after(plane_sum(cross_terms[0][:half], cross_x[:half], cross_y[:half]))
    self_low, self_high, expand_last = after((self_low, self_high, expand_last), cross_pass)
    self_sends = corner_added(grid, self_terms, self_low, self_high)
    self_sends, norm_terms = after((self_sends, norm_terms))
    self_x, self_y = grid.move(self_sends[0], dx=1), grid.move(self_sends[1], dy=1)
    norm_got = lax.all_to_all(norm_terms.reshape(6, grid.count, held_rows), grid.axes, 1, 0, tiled=True)
    cross_got, norm_got, self_x, self_y = after((cross_got, norm_got, self_x, self_y))
    self_column = [plane_sum(self_terms[0][k], self_x[k], self_y[k]) for k in range(grid.depth)]
    cross_leaving = pair_sum(cross_near, cross_got)
    self_column, cross_leaving = after((self_column, cross_leaving))
    self_others = [grid.move(self_column[k], dz=k) for k in (2, 3, 1)]
    cross_last = grid.move(cross_leaving, dz=1)
    reduce_term = total_of(reduce_near[0], reduce_got[0], reduce_last)
    expand_term = total_of(expand_near[0], expand_got[0], expand_last)
    cross_owned = total_of(cross_near[0], cross_got[0], cross_last)
    self_owned = total_of(self_column[0], *self_others)
    norm_owned = jnp.sum(norm_got.reshape(grid.count, 6, held_rows), axis=0)
    return (
        output,
        tokens_grad,
        memory_grad,
        *[self_owned[i] for i in range(3)],
        *[cross_owned[i] for i in range(5)],
        expand_term,
        reduce_term,
        *[norm_owned[i] for i in range(6)],
    )


def solution(mesh):
    grid = Grid(mesh)
    rows = P(grid.axes, None)
    parts = P(grid.axes)
    return jax.shard_map(
        functools.partial(per_device, grid),
        mesh=grid.mesh,
        in_specs=(
            rows,
            rows,
            rows,
            rows,
            rows,
            rows,
            rows,
            rows,
            rows,
            rows,
            rows,
            rows,
            rows,
            rows,
            parts,
            parts,
            parts,
            parts,
            parts,
            parts,
            rows,
        ),
        out_specs=(
            rows,
            rows,
            rows,
            rows,
            rows,
            rows,
            rows,
            rows,
            rows,
            rows,
            rows,
            rows,
            rows,
            parts,
            parts,
            parts,
            parts,
            parts,
            parts,
        ),
        check_vma=False,
    )
```
